32 devices in a mesh: dp: 4 (over y, x), fsdp: 8 (over z, core).
Axes of the slice: x: 2, y: 2, z: 4, core: 2. Of those that a mesh axis runs over, the one named last changes fastest.
Arguments:
- tokens: bfloat16 [5120, 2048], P(('dp', 'fsdp')), may hold values from -6 to 6
- cotangent: bfloat16 [5120, 2048], P(('dp', 'fsdp')), may hold values from -6 to 6
- lengths: int32 [4], P('dp'), may hold values from 320 to 1280, as said below
- norm_attn: bfloat16 [2048], P(('dp', 'fsdp')), may hold values from 0.5 to 1.5
- w_query: bfloat16 [2048, 2048], P(('dp', 'fsdp')), may hold values from -0.125 to 0.125
- w_key: bfloat16 [2048, 2048], P(('dp', 'fsdp')), may hold values from -0.125 to 0.125
- w_value: bfloat16 [2048, 2048], P(('dp', 'fsdp')), may hold values from -0.125 to 0.125
- w_output: bfloat16 [2048, 2048], P(('dp', 'fsdp')), may hold values from -2 to 2
- norm_mlp: bfloat16 [2048], P(('dp', 'fsdp')), may hold values from 0.5 to 1.5
- w_gate: bfloat16 [2048, 8192], P(('dp', 'fsdp')), may hold values from -0.125 to 0.125
- w_up: bfloat16 [2048, 8192], P(('dp', 'fsdp')), may hold values from -0.125 to 0.125
- w_down: bfloat16 [8192, 2048], P(('dp', 'fsdp')), may hold values from -0.0625 to 0.0625
Outputs:
- output: bfloat16 [5120, 2048], P(('dp', 'fsdp'))
- grad_tokens: bfloat16 [5120, 2048], P(('dp', 'fsdp'))
- grad_norm_attn: float32 [2048], P(('dp', 'fsdp'))
- grad_w_query: float32 [2048, 2048], P(('dp', 'fsdp'))
- grad_w_key: float32 [2048, 2048], P(('dp', 'fsdp'))
- grad_w_value: float32 [2048, 2048], P(('dp', 'fsdp'))
- grad_w_output: float32 [2048, 2048], P(('dp', 'fsdp'))
- grad_norm_mlp: float32 [2048], P(('dp', 'fsdp'))
- grad_w_gate: float32 [2048, 8192], P(('dp', 'fsdp'))
- grad_w_up: float32 [2048, 8192], P(('dp', 'fsdp'))
- grad_w_down: float32 [8192, 2048], P(('dp', 'fsdp'))
The draws below stay inside these ranges and needn't reach their ends.
Inputs may be any that keep to these rules, and one draw needn't show every extreme that they name: `lengths`: one sequence, drawn from the seed, has all 1280 positions live.
All inputs are finite; a program needn't handle non-finite values.
Results may differ from the reference program's by a relative error of at most 0.017.
Values may be sent and summed in bfloat16 or wider, within the bound.
A program may use at most 512 MiB of HBM per device.

```python
import math
import jax
import jax.numpy as jnp
from jax import lax

D = 2048
HEADS = 32
HEAD_DIM = 64
FF = 8192
SEQ = 1280
SEQS = 4
TOKENS = 5120


def draw_lengths(key, part):
    key = jax.random.fold_in(key, 7)
    length_key, choose_key = jax.random.split(key)
    drawn_lengths = jax.random.randint(length_key, (SEQS,), SEQ // 4, SEQ + 1)
    chosen = jax.random.randint(choose_key, (), 0, SEQS)
    return jnp.where(jnp.arange(SEQS) == chosen, SEQ, drawn_lengths).astype(jnp.int32)


def strengthened(values, rng, source, target, shards_of, factor):
    owner, partner = [(jnp.arange(values.shape[dim]) // (values.shape[dim] // shards_of)).reshape([-1 if axis == dim else 1 for axis in range(values.ndim)]) for dim in (source, target)]
    chosen = jax.random.permutation(rng, shards_of)[partner]
    strong = (owner == chosen) | (owner == (partner + shards_of // 2) % shards_of)
    return jnp.where(strong, factor * values, values)


def shard_levels(rng, dims, shards, low, largest):
    gain, own = 1.0, jax.random.fold_in(rng, 6)
    for axis_at, blocks in shards:
        draws = jnp.exp(jax.random.uniform(jax.random.fold_in(own, axis_at), (blocks,), jnp.float32, low / len(shards), largest / len(shards)))
        gain = gain * jnp.repeat(draws, dims[axis_at] // blocks).reshape([-1 if axis == axis_at else 1 for axis in range(len(dims))])
    return gain


def scatter_about(own_key, shape, spread, most, cuts=(), kind=jnp.bfloat16):
    values = jax.random.normal(own_key, shape, jnp.float32) * spread
    if len(cuts) > 0:
        values = shard_levels(own_key, shape, cuts, -0.22, 0.18) * values
    return jnp.clip(values, min=-most, max=most).astype(kind)


def bell_draw_with(stream_key, extent, deviation, reach, shards, heavy, kind=jnp.bfloat16):
    drawn = deviation * jax.random.normal(stream_key, extent, jnp.float32)
    if shards:
        drawn = drawn * shard_levels(stream_key, extent, shards, -0.22, 0.18)
    return jnp.clip(strengthened(drawn, jax.random.fold_in(stream_key, 3), *heavy), -reach, reach).astype(kind)


def setup_inputs(seed: int = 0) -> dict:
    arg_keys = jax.random.split(jax.random.key(seed), 13)
    tokens = bell_draw_with(arg_keys[0], (TOKENS, D), 1.0, 6.0, ((0, 32),), (0, 1, 32, 2.75))
    cotangent = scatter_about(arg_keys[1], (TOKENS, D), 1.0, 6.0, ((0, 32),))
    lengths = draw_lengths(jax.random.fold_in(arg_keys[12], 71), 0)
    norm_attn = jnp.clip(1.0 + 0.1 * jax.random.normal(arg_keys[3], (D,), jnp.float32), 0.5, 1.5).astype(jnp.bfloat16)
    w_query = scatter_about(arg_keys[4], (D, D), D ** -0.5, 0.125, ((0, 32),))
    w_key = scatter_about(arg_keys[5], (D, D), D ** -0.5, 0.125, ((0, 32),))
    w_value = scatter_about(arg_keys[6], (D, D), D ** -0.5, 0.125, ((0, 32),))
    w_output = scatter_about(arg_keys[7], (D, D), (max(D // 256, 8)) ** -0.5, 2.0, ((0, 32),))
    norm_mlp = jnp.clip(1.0 + 0.1 * jax.random.normal(arg_keys[8], (D,), jnp.float32), 0.5, 1.5).astype(jnp.bfloat16)
    w_gate = scatter_about(arg_keys[9], (D, FF), D ** -0.5, 0.125, ((0, 32),))
    w_up = scatter_about(arg_keys[10], (D, FF), D ** -0.5, 0.125, ((0, 32),))
    w_down = scatter_about(arg_keys[11], (FF, D), FF ** -0.5, 0.0625, ((0, 32),))
    return {"tokens": tokens, "cotangent": cotangent, "lengths": lengths, "norm_attn": norm_attn, "w_query": w_query, "w_key": w_key, "w_value": w_value, "w_output": w_output, "norm_mlp": norm_mlp, "w_gate": w_gate, "w_up": w_up, "w_down": w_down}


EPSILON = 1e-05
THETA = 130000.0

@jax.custom_vjp
def low(v):
    return lax.optimization_barrier(v.astype(jnp.bfloat16)).astype(jnp.float32)

@jax.custom_vjp
def low_back(v):
    return v

def low_keep(v):
    return (low(v), None)

def low_pass(kept, grad):
    return (grad,)

def back_keep(v):
    return (v, None)

def back_low(kept, grad):
    return (low(grad),)
low.defvjp(low_keep, low_pass)
low_back.defvjp(back_keep, back_low)

def matmul(left, right):
    return jnp.dot(left, right, precision=lax.Precision.HIGHEST, preferred_element_type=jnp.float32)

def rotary(values, positions):
    half = HEAD_DIM // 2
    inverse = THETA ** (-jnp.arange(half, dtype=jnp.float32) * 2.0 / HEAD_DIM)
    angles = positions[:, None] * inverse[None, :]
    cosine = jnp.cos(angles)[:, None, :]
    sine = jnp.sin(angles)[:, None, :]
    shaped = values.reshape(values.shape[0], HEADS, HEAD_DIM)
    first_half = shaped[..., :half]
    second_half = shaped[..., half:]
    turned = jnp.concatenate([first_half * cosine - second_half * sine, second_half * cosine + first_half * sine], -1)
    return turned.reshape(values.shape)

def split_heads(values, block):
    return values.reshape(values.shape[0], HEADS // block, block, HEAD_DIM).transpose(1, 2, 0, 3)

def join_heads(values):
    groups, block, count, width = values.shape
    return values.transpose(2, 0, 1, 3).reshape(count, groups * block * width)

def attend(queries, keys, values, length):
    block = math.gcd(4, HEADS)
    places = jnp.arange(queries.shape[0], dtype=jnp.int32)
    allowed = (places[None, :] <= places[:, None]) & (places[None, :] < length)

    def head_block(parts):
        query_part, key_part, value_part = parts
        scores = low_back(jnp.einsum('hqd,hkd->hqk', query_part, key_part, precision=lax.Precision.HIGHEST) * 0.125)
        scores = jnp.where(allowed[None], scores, -1000000000.0)
        row_max = lax.optimization_barrier(jnp.max(scores, -1, keepdims=True))
        log_total = row_max + jnp.log(lax.optimization_barrier(jnp.sum(jnp.exp(scores - row_max), -1, keepdims=True)))
        weights = low(jnp.exp(scores - log_total))
        return jnp.einsum('hqk,hkd->hqd', weights, value_part, precision=lax.Precision.HIGHEST)
    mapped = lax.map(jax.checkpoint(head_block), (split_heads(queries, block), split_heads(keys, block), split_heads(values, block)))
    return join_heads(mapped)

def layer(tokens_f, params, length):
    norm_attn, w_query, w_key, w_value, w_output, norm_mlp, w_gate, w_up, w_down = params
    positions = jnp.arange(SEQ).astype(jnp.float32)
    scale_one = lax.rsqrt(lax.optimization_barrier(jnp.mean(tokens_f * tokens_f, -1, keepdims=True)) + EPSILON)
    normed = low(tokens_f * scale_one * norm_attn)
    queries = low(rotary(low_back(matmul(normed, w_query)), positions))
    keys = low(rotary(low_back(matmul(normed, w_key)), positions))
    values = low(low_back(matmul(normed, w_value)))
    attended = low(low_back(attend(queries, keys, values, length)))
    hidden = tokens_f + low_back(matmul(attended, w_output))
    scale_two = lax.rsqrt(lax.optimization_barrier(jnp.mean(hidden * hidden, -1, keepdims=True)) + EPSILON)
    normed_two = low(hidden * scale_two * norm_mlp)
    gate = low_back(matmul(normed_two, w_gate))
    up_part = low_back(matmul(normed_two, w_up))
    mixed = low(jax.nn.silu(gate) * up_part)
    return hidden + low_back(matmul(mixed, w_down))

def reference(tokens, cotangent, lengths, norm_attn, w_query, w_key, w_value, w_output, norm_mlp, w_gate, w_up, w_down):
    params = tuple((p.astype(jnp.float32) for p in (norm_attn, w_query, w_key, w_value, w_output, norm_mlp, w_gate, w_up, w_down)))
    inputs = tokens.astype(jnp.float32).reshape(SEQS, SEQ, D)
    grads_in = cotangent.astype(jnp.float32).reshape(SEQS, SEQ, D)

    def one_sequence(totals, packed):
        sequence, grad_seq, length = packed
        live = (jnp.arange(SEQ, dtype=jnp.int32) < length).astype(jnp.float32)[:, None]

        def apply_layer(inner, *weights):
            return layer(inner, weights, length)
        result, pull = jax.vjp(apply_layer, sequence, *params)
        grads = pull(grad_seq * live)
        totals = tuple((total + grad for total, grad in zip(totals, grads[1:])))
        return (totals, (result.astype(jnp.bfloat16), grads[0].astype(jnp.bfloat16)))
    zeros = tuple((jnp.zeros(p.shape, jnp.float32) for p in params))
    totals, (outputs, grad_seqs) = lax.scan(one_sequence, zeros, (inputs, grads_in, lengths))
    return (outputs.reshape(TOKENS, D), grad_seqs.reshape(TOKENS, D), totals[0], totals[1], totals[2], totals[3], totals[4], totals[5], totals[6], totals[7], totals[8])
```

```python
import jax
import jax.numpy as jnp
from jax import lax
from jax.sharding import PartitionSpec as P

HEADS = 32
HEAD_DIM = 64


EPSILON = 1e-05
THETA = 130000.0
BF16 = jnp.bfloat16
F32 = jnp.float32


def rotary_tables(count):
    half = HEAD_DIM // 2
    inverse = THETA ** (-jnp.arange(half, dtype=F32) * 2.0 / HEAD_DIM)
    angles = jnp.arange(count, dtype=jnp.int32).astype(F32)[:, None] * inverse[None, :]
    return jnp.cos(angles)[:, None, :], jnp.sin(angles)[:, None, :]


def rotary(values, tables, sign):
    cosine, sine = tables
    sine = sine * sign
    half = HEAD_DIM // 2
    shaped = values.reshape(values.shape[0], -1, HEAD_DIM)
    first, second = shaped[..., :half], shaped[..., half:]
    turned = jnp.concatenate(
        [first * cosine - second * sine, second * cosine + first * sine], -1
    )
    return turned.reshape(values.shape)


def dot(left, right):
    return jnp.dot(left, right, preferred_element_type=F32)


def rows_inner(left, right):
    return lax.dot_general(left, right, (((0,), (0,)), ((), ())), preferred_element_type=F32)


def cols_inner(left, right):
    return lax.dot_general(left, right, (((1,), (1,)), ((), ())), preferred_element_type=F32)


def inverse_rms(values):
    return lax.rsqrt(jnp.mean(values * values, -1, keepdims=True) + EPSILON)


def norm_back(grad_scaled, scaled, scale):
    return scale * (grad_scaled - scaled * jnp.mean(grad_scaled * scaled, -1, keepdims=True))


def by_heads(values):
    return values.reshape(values.shape[0], -1, HEAD_DIM).transpose(1, 0, 2)


def by_rows(values):
    return values.transpose(1, 0, 2).reshape(values.shape[1], -1)


def attend(queries, keys, values, allowed):
    scores = (
        jnp.einsum("hqd,hkd->hqk", by_heads(queries), by_heads(keys), preferred_element_type=F32)
        * 0.125
    )
    scores = jnp.where(allowed[None], scores, -1000000000.0)
    row_max = jnp.max(scores, -1, keepdims=True)
    log_total = row_max + jnp.log(jnp.sum(jnp.exp(scores - row_max), -1, keepdims=True))
    weights = jnp.exp(scores - log_total).astype(BF16)
    result = jnp.einsum("hqk,hkd->hqd", weights, by_heads(values), preferred_element_type=F32)
    return by_rows(result), log_total


def attend_back(queries, keys, values, grad, log_total, allowed):
    queries, keys, values, grad = (by_heads(v) for v in (queries, keys, values, grad))
    scores = jnp.einsum("hqd,hkd->hqk", queries, keys, preferred_element_type=F32) * 0.125
    scores = jnp.where(allowed[None], scores, -1000000000.0)
    weights = jnp.exp(scores - log_total)
    grad_weights = jnp.einsum("hqd,hkd->hqk", grad, values, preferred_element_type=F32)
    grad_scores = (
        weights * (grad_weights - jnp.sum(weights * grad_weights, -1, keepdims=True))
    ).astype(BF16)
    grad_q = 0.125 * jnp.einsum("hqk,hkd->hqd", grad_scores, keys, preferred_element_type=F32)
    grad_k = 0.125 * jnp.einsum("hqk,hqd->hkd", grad_scores, queries, preferred_element_type=F32)
    grad_v = jnp.einsum("hqk,hqd->hkd", weights.astype(BF16), grad, preferred_element_type=F32)
    return by_rows(grad_q), by_rows(grad_k), by_rows(grad_v)


def build(groups, ranks):
    def gather_rows(value):
        return lax.all_gather(value, "fsdp", axis=0, tiled=True)

    def scatter_rows(value):
        return lax.psum_scatter(
            value.astype(BF16), "fsdp", scatter_dimension=0, tiled=True
        ).astype(F32)

    def exchange(value):
        return lax.all_to_all(value, "fsdp", 0, 0, tiled=True)

    def body(
        tokens, cotangent, lengths, norm_attn, w_query, w_key, w_value, w_output, norm_mlp, w_gate, w_up, w_down
    ):
        rows, width = tokens.shape
        depth = w_query.shape[0]
        count = rows * ranks
        rank_heads = HEADS // ranks
        hidden_part = w_down.shape[0]
        out_rows = w_output.shape[0]
        split = max(1, HEAD_DIM // out_rows)
        rank = lax.axis_index("fsdp")

        def heads_out(weight):
            shaped = weight.reshape(depth, split, rank_heads, ranks // split, HEAD_DIM)
            return shaped.transpose(3, 1, 0, 2, 4).reshape(ranks, depth, rank_heads * HEAD_DIM)

        def heads_in(pieces):
            shaped = pieces.reshape(ranks // split, split, depth, rank_heads, HEAD_DIM)
            return shaped.transpose(2, 1, 3, 0, 4).reshape(depth, HEADS * HEAD_DIM)

        def units_out(weight):
            shaped = weight.reshape(depth, groups, ranks, hidden_part)
            return shaped.transpose(2, 0, 1, 3).reshape(ranks, depth, groups * hidden_part)

        def units_in(pieces):
            shaped = pieces.reshape(ranks, depth, groups, hidden_part)
            return shaped.transpose(1, 2, 0, 3).reshape(depth, groups * ranks * hidden_part)

        span = [[base * split + i for i in range(split)] for base in range(ranks // split)]

        def gather_output(weight):
            if split > 1:
                weight = lax.all_gather(weight, "fsdp", axis=0, tiled=True, axis_index_groups=span)
            whole = lax.all_gather(weight, "dp", axis=0, tiled=True)
            if split > 1:
                whole = whole.reshape(split, -1, width)[lax.rem(rank, split)]
            return whole

        def scatter_output(grad):
            grad = grad.astype(BF16)
            if split > 1:
                place = lax.rem(rank, split)
                grad = jnp.where(
                    (jnp.arange(split) == place)[:, None, None], grad[None], jnp.zeros((), BF16)
                ).reshape(-1, width)
            grad = lax.psum_scatter(grad, "dp", scatter_dimension=0, tiled=True)
            if split > 1:
                grad = lax.psum_scatter(
                    grad, "fsdp", scatter_dimension=0, tiled=True, axis_index_groups=span
                )
            return grad.astype(F32)

        head_cols = rank_heads * HEAD_DIM
        unit_cols = groups * hidden_part
        qkv_out = jnp.concatenate([heads_out(w) for w in (w_query, w_key, w_value)], -1)
        gate_up_out = jnp.concatenate([units_out(w) for w in (w_gate, w_up)], -1)
        x_all = gather_rows(tokens)
        qkv = lax.all_gather(exchange(qkv_out), "dp", axis=0, tiled=True).reshape(width, -1)
        gains = lax.all_gather(jnp.stack([norm_attn, norm_mlp], -1), ("dp", "fsdp"), axis=0, tiled=True)
        gain_one, gain_two = gains[:, 0].astype(F32), gains[:, 1].astype(F32)
        out_w = gather_output(w_output)
        gate_up = lax.all_gather(exchange(gate_up_out), "dp", axis=0, tiled=True).reshape(width, -1)
        down_w = lax.all_gather(w_down, "dp", axis=0, tiled=True)

        tokens_f = tokens.astype(F32)
        x_f = x_all.astype(F32)
        normed_one = (x_f * inverse_rms(x_f) * gain_one).astype(BF16)
        qkv_lin = dot(normed_one, qkv)
        tables = rotary_tables(count)
        queries = rotary(qkv_lin[:, :head_cols], tables, 1.0).astype(BF16)
        keys = rotary(qkv_lin[:, head_cols : 2 * head_cols], tables, 1.0).astype(BF16)
        values = qkv_lin[:, 2 * head_cols :].astype(BF16)
        places = jnp.arange(count, dtype=jnp.int32)
        allowed = (places[None, :] <= places[:, None]) & (places[None, :] < lengths[0])
        attended, log_total = attend(queries, keys, values, allowed)
        attended = attended.astype(BF16)
        hidden = tokens_f + scatter_rows(dot(attended, out_w))
        scale_two = inverse_rms(hidden)
        scaled_two = hidden * scale_two
        normed_two = gather_rows((scaled_two * gain_two).astype(BF16))
        gate_up_lin = dot(normed_two, gate_up)
        gate, up = gate_up_lin[:, :unit_cols], gate_up_lin[:, unit_cols:]
        sigmoid = 1.0 / (1.0 + jnp.exp(-gate))
        silu = gate * sigmoid
        mixed = (silu * up).astype(BF16)
        output = (hidden + scatter_rows(dot(mixed, down_w))).astype(BF16)

        live = places[:, None] < lengths[0]
        grad_out_all = jnp.where(live, gather_rows(cotangent), jnp.zeros((), BF16))
        own_places = rank * rows + jnp.arange(rows, dtype=jnp.int32)
        grad_out = cotangent.astype(F32) * (own_places < lengths[0]).astype(F32)[:, None]
        grad_mixed = cols_inner(grad_out_all, down_w)
        grad_w_down = lax.psum_scatter(
            rows_inner(mixed, grad_out_all).astype(BF16), "dp", scatter_dimension=0, tiled=True
        ).astype(F32)
        grad_gate = grad_mixed * up * (sigmoid * (1.0 + gate * (1.0 - sigmoid)))
        grad_up = grad_mixed * silu
        grad_gate_up = jnp.concatenate([grad_gate.astype(BF16), grad_up.astype(BF16)], -1)
        grad_normed_two = scatter_rows(cols_inner(grad_gate_up, gate_up))
        sum_two = jnp.sum(grad_normed_two * scaled_two, 0)
        grad_hidden = grad_out + norm_back(grad_normed_two * gain_two, scaled_two, scale_two)
        grad_hidden_all = gather_rows(grad_hidden.astype(BF16))
        grad_gate_up_w = exchange(
            lax.psum_scatter(
                rows_inner(normed_two, grad_gate_up).astype(BF16), "dp", scatter_dimension=0, tiled=True
            ).reshape(ranks, depth, 2 * unit_cols)
        )
        grad_w_gate = units_in(grad_gate_up_w[..., :unit_cols]).astype(F32)
        grad_w_up = units_in(grad_gate_up_w[..., unit_cols:]).astype(F32)
        grad_w_output = scatter_output(rows_inner(attended, grad_hidden_all))
        grad_attended = cols_inner(grad_hidden_all, out_w).astype(BF16)
        grad_q, grad_k, grad_v = attend_back(queries, keys, values, grad_attended, log_total, allowed)
        grad_qkv = jnp.concatenate(
            [
                rotary(grad_q, tables, -1.0).astype(BF16),
                rotary(grad_k, tables, -1.0).astype(BF16),
                grad_v.astype(BF16),
            ],
            -1,
        )
        grad_normed_one = scatter_rows(cols_inner(grad_qkv, qkv))
        scale_one = inverse_rms(tokens_f)
        scaled_one = tokens_f * scale_one
        sum_one = jnp.sum(grad_normed_one * scaled_one, 0)
        grad_tokens = (
            grad_hidden + norm_back(grad_normed_one * gain_one, scaled_one, scale_one)
        ).astype(BF16)
        grad_qkv_w = exchange(
            lax.psum_scatter(
                rows_inner(normed_one, grad_qkv).astype(BF16), "dp", scatter_dimension=0, tiled=True
            ).reshape(ranks, depth, 3 * head_cols)
        )
        grad_w_query, grad_w_key, grad_w_value = (
            heads_in(grad_qkv_w[..., i * head_cols : (i + 1) * head_cols]).astype(F32) for i in range(3)
        )
        sums = lax.psum_scatter(
            jnp.stack([sum_one, sum_two], -1), ("dp", "fsdp"), scatter_dimension=0, tiled=True
        )
        return (
            output,
            grad_tokens,
            sums[:, 0],
            grad_w_query,
            grad_w_key,
            grad_w_value,
            grad_w_output,
            sums[:, 1],
            grad_w_gate,
            grad_w_up,
            grad_w_down,
        )

    return body


def solution(mesh):
    both = P(("dp", "fsdp"))
    rows = P(("dp", "fsdp"), None)
    return jax.shard_map(
        build(mesh.shape["dp"], mesh.shape["fsdp"]),
        mesh=mesh,
        in_specs=(rows, rows, P("dp"), both, rows, rows, rows, rows, both, rows, rows, rows),
        out_specs=(rows, rows, both, rows, rows, rows, rows, both, rows, rows, rows),
        check_vma=False,
    )
```

```python
import functools

import jax
import jax.numpy as jnp
from jax import lax
from jax.experimental import pallas as pl
from jax.experimental.pallas import tpu as pltpu
from jax.sharding import PartitionSpec as P

HEADS = 32
HEAD_DIM = 64


EPSILON = 1e-05
THETA = 130000.0
BF16 = jnp.bfloat16
F32 = jnp.float32


def dot(left, right):
    return jnp.dot(left, right, preferred_element_type=F32)


def rows_inner(left, right):
    return lax.dot_general(left, right, (((0,), (0,)), ((), ())), preferred_element_type=F32)


def cols_inner(left, right):
    return lax.dot_general(left, right, (((1,), (1,)), ((), ())), preferred_element_type=F32)


def inverse_rms(values):
    return lax.rsqrt(jnp.mean(values * values, -1, keepdims=True) + EPSILON)


def norm_back(grad_scaled, scaled, scale):
    return scale * (grad_scaled - scaled * jnp.mean(grad_scaled * scaled, -1, keepdims=True))


BLOCK = 256
SCALE = 0.125


def turn_halves(values, cosine, sine):
    width = values.shape[1]
    half = HEAD_DIM // 2
    lane = lax.broadcasted_iota(jnp.int32, values.shape, 1)
    ahead = pltpu.roll(values, width - half, 1)
    behind = pltpu.roll(values, half, 1)
    return values * cosine + jnp.where(lane % HEAD_DIM < half, ahead, behind) * sine


def wide_tables(count, width):
    half = HEAD_DIM // 2
    inverse = THETA ** (-jnp.arange(half, dtype=F32) * 2.0 / HEAD_DIM)
    angles = jnp.arange(count, dtype=jnp.int32).astype(F32)[:, None] * inverse[None, :]
    cosine, sine = jnp.cos(angles), jnp.sin(angles)
    repeats = width // HEAD_DIM
    return (
        jnp.tile(jnp.concatenate([cosine, cosine], -1), (1, repeats)),
        jnp.tile(jnp.concatenate([-sine, sine], -1), (1, repeats)),
    )


def head_rows(values, head):
    row = lax.broadcasted_iota(jnp.int32, values.shape, 0)
    return jnp.where((row >= head * HEAD_DIM) & (row < (head + 1) * HEAD_DIM), values, 0.0)


def future(shape):
    return lax.broadcasted_iota(jnp.int32, shape, 0) > lax.broadcasted_iota(jnp.int32, shape, 1)


def attend_block(i, rank_heads, queries, keys, values_t, bias, attended, log_totals):
    queries_t = queries.T
    masked = [(head_rows(queries_t, h) * SCALE).astype(BF16) for h in range(rank_heads)]

    def chunk(j, carry, last):
        part = pl.ds(pl.multiple_of(j * BLOCK, BLOCK), BLOCK)
        key_part, bias_part = keys[part, :], bias[part, :]
        after = []
        for h in range(rank_heads):
            top, total, out = carry[h]
            scores = dot(key_part, masked[h]) + bias_part
            if last:
                scores = jnp.where(future(scores.shape), -1000000000.0, scores)
            new_top = jnp.maximum(top, jnp.max(scores, 0, keepdims=True))
            keep = jnp.exp(top - new_top)
            weights = jnp.exp(scores - new_top)
            total = total * keep + jnp.sum(weights, 0, keepdims=True)
            out = out * keep + dot(
                values_t[j, h * HEAD_DIM : (h + 1) * HEAD_DIM, :], weights.astype(BF16)
            )
            after.append((new_top, total, out))
        return tuple(after)

    carry = tuple(
        (
            jnp.full((1, BLOCK), -3.0e38, F32),
            jnp.zeros((1, BLOCK), F32),
            jnp.zeros((HEAD_DIM, BLOCK), F32),
        )
        for _ in range(rank_heads)
    )
    carry = lax.fori_loop(0, i, lambda j, c: chunk(j, c, False), carry)
    carry = chunk(i, carry, True)
    outs = []
    for h, (top, total, out) in enumerate(carry):
        log_totals[i, h : h + 1, :] = top + jnp.log(total)
        outs.append(out * (1.0 / total))
    attended[pl.ds(pl.multiple_of(i * BLOCK, BLOCK), BLOCK), :] = (
        jnp.concatenate(outs, 0).T.astype(BF16)
    )


def project_block(i, x, gain, qkv, cosine, sine, normed, queries, keys, values, values_t):
    cols = queries.shape[1]
    start = i * BLOCK

    def rows_of(part):
        rows = x[part, :].astype(F32)
        normed[part, :] = (rows * inverse_rms(rows) * gain[...]).astype(BF16)

    pl.loop(0, BLOCK // 16)(
        lambda t: rows_of(pl.ds(pl.multiple_of(start + t * 16, 16), 16))
    )
    block = pl.ds(pl.multiple_of(start, BLOCK), BLOCK)
    rows = normed[block, :]
    cos, sin = cosine[block, :], sine[block, :]
    rounded = turn_halves(dot(rows, qkv[:, :cols]), cos, sin).astype(BF16)
    queries[block, :] = rounded
    keys[block, :] = turn_halves(dot(rows, qkv[:, cols : 2 * cols]), cos, sin).astype(BF16)
    value = dot(rows, qkv[:, 2 * cols :])
    values[block, :] = value.astype(BF16)
    values_t[i] = value.T.astype(BF16)
    return rounded.astype(F32)


def matmul_block(i, left, right, out, step=512):
    block = pl.ds(pl.multiple_of(i * BLOCK, BLOCK), BLOCK)
    rows = left[block, :]

    @pl.loop(0, right.shape[1] // step)
    def _(c):
        part = pl.ds(pl.multiple_of(c * step, step), step)
        out[block, part] = dot(rows, right[:, part]).astype(out.dtype)


def lanes_of(values, head):
    lane = lax.broadcasted_iota(jnp.int32, values.shape, 1)
    return jnp.where((lane >= head * HEAD_DIM) & (lane < (head + 1) * HEAD_DIM), values, 0.0)


def attend_back_block(
    i, rank_heads, queries, keys, keys_t, values, attended, grad, bias, log_totals, grad_keys, grad_values
):
    block = pl.ds(pl.multiple_of(i * BLOCK, BLOCK), BLOCK)
    query = queries[block, :].astype(F32) * SCALE
    query_t, grad_t = query.T, grad.T
    product = attended[block, :].astype(F32).T * grad_t
    masked_q = [head_rows(query_t, h).astype(BF16) for h in range(rank_heads)]
    masked_g = [head_rows(grad_t, h).astype(BF16) for h in range(rank_heads)]
    stacked_q = jnp.concatenate([lanes_of(query, h).astype(BF16) for h in range(rank_heads)], 0)
    stacked_g = jnp.concatenate([lanes_of(grad, h).astype(BF16) for h in range(rank_heads)], 0)
    deltas = [
        jnp.sum(product[h * HEAD_DIM : (h + 1) * HEAD_DIM], 0, keepdims=True)
        for h in range(rank_heads)
    ]
    totals = [log_totals[i, h : h + 1, :] for h in range(rank_heads)]

    def chunk(j, carry, last):
        part = pl.ds(pl.multiple_of(j * BLOCK, BLOCK), BLOCK)
        key_part, value_part, bias_part = keys[part, :], values[part, :], bias[part, :]
        after, weights_all, grads_all = [], [], []
        for h in range(rank_heads):
            scores = dot(key_part, masked_q[h]) + bias_part
            if last:
                scores = jnp.where(future(scores.shape), -1000000000.0, scores)
            weights = jnp.exp(scores - totals[h])
            grad_scores = weights * (dot(value_part, masked_g[h]) - deltas[h])
            weights_all.append(weights.astype(BF16))
            grads_all.append(grad_scores.astype(BF16))
            after.append(
                carry[h] + dot(keys_t[j, h * HEAD_DIM : (h + 1) * HEAD_DIM, :], grads_all[-1])
            )
        grad_values[part, :] += dot(jnp.concatenate(weights_all, 1), stacked_g)
        grad_keys[part, :] += dot(jnp.concatenate(grads_all, 1), stacked_q)
        return tuple(after)

    carry = tuple(jnp.zeros((HEAD_DIM, BLOCK), F32) for _ in range(rank_heads))
    carry = lax.fori_loop(0, i, lambda j, c: chunk(j, c, False), carry)
    carry = chunk(i, carry, True)
    return jnp.concatenate(carry, 0).T * SCALE


def attend_back_rows(
    i, rank_heads, grad_hidden, out_w, queries, keys, keys_t, values, attended, bias, log_totals,
    cosine, sine, grad_keys, grad_values, grad_qkv,
):
    block = pl.ds(pl.multiple_of(i * BLOCK, BLOCK), BLOCK)
    cols = queries.shape[1]
    grad = cols_inner(grad_hidden[block, :], out_w[...]).astype(BF16).astype(F32)
    grad_q = attend_back_block(
        i, rank_heads, queries, keys, keys_t, values, attended, grad, bias, log_totals, grad_keys, grad_values
    )
    grad_qkv[block, :cols] = turn_halves(grad_q, cosine[block, :], -sine[block, :]).astype(BF16)


def finish_back_rows(i, qkv, cosine, sine, grad_keys, grad_values, grad_qkv, parts):
    block = pl.ds(pl.multiple_of(i * BLOCK, BLOCK), BLOCK)
    cols = grad_keys.shape[1]
    grad_qkv[block, cols : 2 * cols] = turn_halves(
        grad_keys[block, :], cosine[block, :], -sine[block, :]
    ).astype(BF16)
    grad_qkv[block, 2 * cols :] = grad_values[block, :].astype(BF16)
    rows = grad_qkv[block, :]
    step = 512

    @pl.loop(0, qkv.shape[0] // step)
    def _(c):
        part = pl.ds(pl.multiple_of(c * step, step), step)
        parts[block, part] = cols_inner(rows, qkv[part, :]).astype(BF16)

MESH = pl.DeviceIdType.MESH


def when(cond, action):
    if cond is None:
        action()
    else:
        pl.when(cond)(action)


class Links:
    def __init__(self, groups, ranks, sends, recvs):
        self.groups, self.ranks, self.chips = groups, ranks, ranks // 2
        self.bits = groups.bit_length() - 1
        self.sends, self.recvs = sends, recvs
        self.used_sends = self.used_recvs = 0
        self.d, self.f = lax.axis_index("dp"), lax.axis_index("fsdp")
        self.z, self.c = lax.div(self.f, 2), lax.rem(self.f, 2)
        self.sibling = (self.d, self.z * 2 + 1 - self.c)
        self.pending = []

    def bit(self, b):
        return lax.rem(lax.div(self.d, 1 << b), 2)

    def partner(self, b):
        return (self.d + (1 - 2 * self.bit(b)) * (1 << b), self.f)

    def beside(self, way):
        return (self.d, self.f + 2 * way)

    def barrier(self):
        gate = pltpu.get_barrier_semaphore()
        for k in range(1, self.ranks):
            other = lax.rem(self.f + k, self.ranks)
            pl.semaphore_signal(gate, inc=1, device_id=(self.d, other), device_id_type=MESH)
        for k in range(1, self.groups):
            other = lax.rem(self.d + k, self.groups)
            pl.semaphore_signal(gate, inc=1, device_id=(other, self.f), device_id_type=MESH)
        pl.semaphore_wait(gate, self.ranks + self.groups - 2)

    def take(self, sends, recvs):
        first = (self.used_sends, self.used_recvs)
        self.used_sends += sends
        self.used_recvs += recvs
        return first

    def copy(self, source, target, send, recv, device):
        return pltpu.make_async_remote_copy(
            src_ref=source,
            dst_ref=target,
            send_sem=self.sends.at[send],
            recv_sem=self.recvs.at[recv],
            device_id=device,
            device_id_type=MESH,
        )

    def send(self, cond, source, target, send, recv, device, later=True):
        when(cond, lambda: self.copy(source, target, send, recv, device).start())
        gone = lambda: when(
            cond, lambda: self.copy(source, target, send, recv, device).wait_send()
        )
        if later:
            self.pending.append(gone)
        return gone

    def arrived(self, cond, target, recv):
        when(cond, lambda: self.copy(target, target, 0, recv, self.sibling).wait_recv())

    def move(self, source, target):
        send, _ = self.take(1, 0)
        make = lambda: pltpu.make_async_copy(source, target, self.sends.at[send])
        make().start()
        return lambda: make().wait()

    def finish(self):
        for wait in self.pending:
            wait()
        self.pending = []


class LineGather:
    def __init__(self, links, view):
        self.links, self.view = links, view
        chips = links.chips
        self.sends, self.recvs = links.take(3 * chips, 3 * chips)

    def start(self, source):
        k, chips = self.links, self.links.chips
        target = self.view(k.f)
        for side, way in enumerate((1, -1)):
            valid = (k.z + way >= 0) & (k.z + way < chips)
            k.send(
                valid, source, target, self.sends + side * chips, self.recvs + side * chips + 1, k.beside(way)
            )
        k.send(
            None, source, target, self.sends + 2 * chips + k.z, self.recvs + 2 * chips + k.z, k.sibling
        )

    def step(self, reach):
        k, chips = self.links, self.links.chips
        for side, way in enumerate((1, -1)):
            origin = k.z - way * reach
            here = (origin >= 0) & (origin < chips)
            block = self.view(origin * 2 + k.c)
            k.arrived(here, block, self.recvs + side * chips + reach)
            if reach + 1 < chips:
                onward = here & (k.z + way >= 0) & (k.z + way < chips)
                k.send(
                    onward,
                    block,
                    block,
                    self.sends + side * chips + reach,
                    self.recvs + side * chips + reach + 1,
                    k.beside(way),
                )
            k.send(
                here,
                block,
                block,
                self.sends + 2 * chips + origin,
                self.recvs + 2 * chips + origin,
                k.sibling,
            )

    def finish(self):
        k, chips = self.links, self.links.chips
        for chip in range(chips):
            k.arrived(None, self.view(chip * 2 + 1 - k.c), self.recvs + 2 * chips + chip)


def add_rows(target, *sources, step=16):
    rows = target.shape[0]

    @pl.loop(0, rows // step)
    def _(i):
        part = pl.ds(pl.multiple_of(i * step, step), step)
        total = sources[0][part].astype(F32)
        for source in sources[1:]:
            total = total + source[part].astype(F32)
        target[part] = total.astype(target.dtype)


class LineScatter:
    def __init__(self, links, parts, mine, held, landed):
        self.links, self.parts, self.mine = links, parts, mine
        self.held, self.landed = held, landed
        chips = links.chips
        self.sends, self.recvs = links.take(2 * chips, 3 * chips)
        self.gone = [lambda: None] * 2

    def start(self):
        k, chips = self.links, self.links.chips
        for chip in range(chips):
            k.send(
                None,
                self.parts(chip * 2 + 1 - k.c),
                self.held(chip),
                self.sends + chip,
                self.recvs + chip,
                k.sibling,
            )
        self.own = [k.move(self.parts(chip * 2 + k.c), self.mine(chip)) for chip in range(chips)]

    def pair(self):
        k = self.links
        for chip in range(k.chips):
            self.own[chip]()
            k.arrived(None, self.held(chip), self.recvs + chip)
            add_rows(self.held(chip), self.held(chip), self.mine(chip))

    def step(self, i):
        k, chips = self.links, self.links.chips
        for side, way in enumerate((1, -1)):
            chip = k.z + way * (chips - 1 - i)
            before = (chip >= 0) & (chip < chips)
            inner = before & (k.z > 0 if way > 0 else k.z < chips - 1)
            mine = self.recvs + (1 + side) * chips + chip

            def add():
                k.arrived(None, self.landed(side, chip), mine)
                add_rows(self.held(chip), self.held(chip), self.landed(side, chip))

            pl.when(inner)(add)
            self.gone[side]()
            self.gone[side] = k.send(
                before,
                self.held(chip),
                self.landed(side, chip),
                self.sends + chips + chip,
                mine,
                k.beside(way),
                later=False,
            )

    def last(self):
        k, chips = self.links, self.links.chips
        for side, inner in enumerate((k.z > 0, k.z < chips - 1)):

            def add():
                k.arrived(None, self.landed(side, k.z), self.recvs + (1 + side) * chips + k.z)
                add_rows(self.held(k.z), self.held(k.z), self.landed(side, k.z))

            pl.when(inner)(add)
        for gone in self.gone:
            gone()


class Exchange:
    def __init__(self, links):
        self.links = links
        self.sends, self.recvs = links.take(links.ranks, links.ranks)

    def start(self, source, target):
        k = self.links
        self.own = k.move(source(k.f), target(k.f))
        for i in range(1, k.ranks):
            other = lax.rem(k.f + i, k.ranks)
            k.send(
                None, source(other), target(k.f), self.sends + other, self.recvs + k.f, (k.d, other)
            )

    def finish(self, target, own=True):
        k = self.links
        if own:
            self.own()
        for i in range(1, k.ranks):
            other = lax.rem(k.f + i, k.ranks)
            k.arrived(None, target(other), self.recvs + other)

    def start_piece(self, rank, source, target):
        k = self.links
        k.send(
            k.f != rank, source, target(k.f), self.sends + rank, self.recvs + k.f, (k.d, rank)
        )
        here = lambda: pltpu.make_async_copy(source, target(k.f), k.sends.at[self.sends + rank])
        pl.when(k.f == rank)(lambda: here().start())
        k.pending.append(lambda: pl.when(k.f == rank)(lambda: here().wait()))


def spread_bits(base, bits):
    places = [base]
    for b, own in bits:
        places = places + [place + (1 - 2 * own) * (1 << b) for place in places]
    return places


class GroupGather:
    def __init__(self, links, view):
        self.links, self.view = links, view
        count = links.groups - 1
        self.sends, self.recvs = links.take(2 * count, 2 * count)

    def order(self, half):
        bits = list(range(self.links.bits))
        return bits if half == 0 else bits[::-1]

    def base(self, half, stage):
        return half * (self.links.groups - 1) + (1 << stage) - 1

    def start(self, half, stage, source=None):
        k = self.links
        order = self.order(half)
        blocks = spread_bits(k.d, [(b, k.bit(b)) for b in order[:stage]])
        for i, block in enumerate(blocks):
            at = self.base(half, stage) + i
            target = self.view(block, half)
            k.send(
                None,
                target if source is None else source(half),
                target,
                self.sends + at,
                self.recvs + at,
                k.partner(order[stage]),
            )

    def wait(self, half, stage):
        k = self.links
        order = self.order(half)
        far = k.partner(order[stage])[0]
        blocks = spread_bits(far, [(b, k.bit(b)) for b in order[:stage]])
        for i, block in enumerate(blocks):
            k.arrived(None, self.view(block, half), self.recvs + self.base(half, stage) + i)


class GroupScatter:
    def __init__(self, links, view, landed, high):
        self.links, self.view, self.landed = links, view, landed
        bits = list(range(links.bits))
        self.order = bits[::-1] if high else bits
        count = links.groups - 1
        self.sends, self.recvs = links.take(count, count)

    def base(self, stage):
        return sum(self.links.groups >> (s + 1) for s in range(stage))

    def sources(self, stage, flip):
        k = self.links
        b = self.order[stage]
        value = 1 - k.bit(b) if flip else k.bit(b)
        if stage > 0:
            count = k.groups >> (stage + 1)
            return [self.landed(self.base(stage - 1) + value + 2 * i) for i in range(count)]
        places = [value * (1 << b)]
        for b in self.order[1:]:
            places = places + [place + (1 << b) for place in places]
        return [self.view(place) for place in places]

    def start(self, stage):
        k = self.links
        for i, source in enumerate(self.sources(stage, True)):
            at = self.base(stage) + i
            k.send(
                None,
                source,
                self.landed(at),
                self.sends + at,
                self.recvs + at,
                k.partner(self.order[stage]),
            )

    def wait(self, stage, target=None):
        k = self.links
        for i, source in enumerate(self.sources(stage, False)):
            at = self.base(stage) + i
            k.arrived(None, self.landed(at), self.recvs + at)
            add_rows(self.landed(at) if target is None else target, source, self.landed(at))
        return self.landed(self.base(stage))


def row_loop(rows, action, step=16, first=0):
    @pl.loop(0, rows // step)
    def _(i):
        action(pl.ds(pl.multiple_of(first + i * step, step), step))


def halved(ref, count):
    return lambda group, half: ref.at[group, pl.ds(half * count, count)]


def first_kernel(
    groups, ranks, tokens, qkv_out, gains, out_w, down_w,
    x_all, qkv, gains_all, out_all, down_all, sends, recvs,
):
    k = Links(groups, ranks, sends, recvs)
    x_line = LineGather(k, lambda rank: x_all.at[rank])
    gains_ex, qkv_ex = Exchange(k), Exchange(k)
    out_half, down_half = out_w.shape[0] // 2, down_w.shape[0] // 2
    early = [
        (GroupGather(k, halved(out_all, out_half)), lambda h: out_w.at[pl.ds(h * out_half, out_half)]),
        (GroupGather(k, halved(down_all, down_half)), lambda h: down_w.at[pl.ds(h * down_half, down_half)]),
    ]
    late = [GroupGather(k, halved(qkv, ranks // 2)), GroupGather(k, halved(gains_all, ranks // 2))]
    k.barrier()
    gains_in = lambda rank: gains_all.at[k.d, rank]
    qkv_in = lambda rank: qkv.at[k.d, rank]
    gains_ex.start(lambda rank: gains, gains_in)
    qkv_ex.start(lambda rank: qkv_out.at[rank], qkv_in)
    for gather, source in early:
        for half in range(2):
            gather.start(half, 0, source)
    own = [
        k.move(tokens, x_all.at[k.f]),
        k.move(out_w, out_all.at[k.d]),
        k.move(down_w, down_all.at[k.d]),
    ]
    x_line.start(tokens)
    gains_ex.finish(gains_in)
    qkv_ex.finish(qkv_in)
    for gather in late:
        for half in range(2):
            gather.start(half, 0)
    for wait in own:
        wait()
    early = [gather for gather, _ in early]
    x_line.step(1)
    for gather in early:
        for half in range(2):
            gather.wait(half, 0)
            gather.start(half, 1)
    for reach in range(2, k.chips):
        x_line.step(reach)
        if reach == 2:
            for gather in late:
                for half in range(2):
                    gather.wait(half, 0)
                    gather.start(half, 1)
    for stage in range(1, k.bits):
        for gather in late + early:
            for half in range(2):
                gather.wait(half, stage)
                if stage + 1 < k.bits:
                    gather.start(half, stage + 1)
    x_line.finish()
    k.finish()


def spaced(events, blocks):
    count = len(events)
    return [events[b * count // blocks : (b + 1) * count // blocks] for b in range(blocks)]


def attend_kernel(
    groups, ranks, rank_heads, x_all, cotangent, gate_up_out, qkv, gain, out_w, cosine, sine, bias,
    parts, normed, queries, keys, values, attended, log_totals, cotangent_all, gate_up,
    values_t, sends, recvs,
):
    k = Links(groups, ranks, sends, recvs)
    depth = gate_up_out.shape[1]
    pieces = depth // 16
    exchanges = [Exchange(k) for _ in range(pieces)]
    gathers = [
        GroupGather(
            k,
            lambda group, half, q=q: gate_up.at[
                group, pl.ds(half * (ranks // 2), ranks // 2), pl.ds(q * 16, 16)
            ],
        )
        for q in range(pieces)
    ]
    line = LineGather(k, lambda rank: cotangent_all.at[rank])
    k.barrier()
    own = k.move(cotangent, cotangent_all.at[k.f])

    def send_out(q):
        part = pl.ds(q * 16, 16)
        exchanges[q].start(
            lambda rank: gate_up_out.at[rank, part], lambda rank: gate_up.at[k.d, rank, part]
        )

    def came_in(q):
        exchanges[q].finish(lambda rank: gate_up.at[k.d, rank, pl.ds(q * 16, 16)])
        for half in range(2):
            gathers[q].start(half, 0)

    def onward(q, stage):
        for half in range(2):
            gathers[q].wait(half, stage)
            if stage + 1 < k.bits:
                gathers[q].start(half, stage + 1)

    events = []
    for q in range(pieces):
        events.append([lambda q=q: came_in(q)])
        if q + 2 < pieces:
            events[-1].append(lambda q=q: send_out(q + 2))
        if q > 0:
            events[-1].append(lambda q=q: onward(q - 1, 0))
        if q == pieces - 2 or pieces == 1:
            events[-1].append(lambda: line.start(cotangent))
    events.append([lambda: line.step(1), lambda: onward(pieces - 1, 0)])
    for q in range(min(2, pieces)):
        send_out(q)
    blocks = values_t.shape[0]
    plan = spaced(events, blocks)
    for i in range(blocks):
        query = project_block(
            i, x_all, gain, qkv, cosine, sine, normed, queries, keys, values, values_t
        )
        attend_block(i, rank_heads, query, keys, values_t, bias, attended, log_totals)
        matmul_block(i, attended, out_w, parts)
        for event in plan[i]:
            for action in event:
                action()
    for reach in range(2, k.chips):
        line.step(reach)
    for stage in range(1, k.bits):
        for q in range(pieces):
            onward(q, stage)
    own()
    line.finish()
    k.finish()


def sub_lines(k, subs, rows, parts, mine, held, landed, gathered):
    scatters, gathers = [], []
    for sub in range(subs):
        part = pl.ds(sub * rows, rows)
        scatters.append(
            LineScatter(
                k,
                lambda rank, part=part: parts.at[rank, part],
                lambda chip, part=part: mine.at[chip, part],
                lambda chip, part=part: held.at[chip, part],
                lambda side, chip, part=part: landed.at[side, chip, part],
            )
        )
        gathers.append(LineGather(k, lambda rank, part=part: gathered.at[rank, part]))
    return scatters, gathers


def hidden_kernel(groups, ranks, subs, parts, tokens, gain, hidden, normed_all, mine, held, landed, normed, sends, recvs):
    k = Links(groups, ranks, sends, recvs)
    rows = tokens.shape[0] // subs
    scatters, gathers = sub_lines(k, subs, rows, parts, mine, held, landed, normed_all)
    k.barrier()
    for scatter in scatters:
        scatter.start()
    own = []
    for turn in range(subs + 1):
        if turn < subs:
            scatters[turn].pair()
        for i in range(k.chips - 1):
            if turn < subs:
                scatters[turn].step(i)
            if turn > 0:
                gathers[turn - 1].step(i + 1)
        if turn < subs:
            scatters[turn].last()

            def rows_of(part):
                total = tokens[part].astype(F32) + held[k.z, part].astype(F32)
                hidden[part] = total
                scaled = total * inverse_rms(total)
                normed[part] = (scaled * gain[...]).astype(BF16)

            row_loop(rows, rows_of, first=turn * rows)
            piece = pl.ds(turn * rows, rows)
            gathers[turn].start(normed.at[piece])
            own.append(k.move(normed.at[piece], normed_all.at[k.f, piece]))
    for gather in gathers:
        gather.finish()
    for wait in own:
        wait()
    k.finish()


def middle_kernel(
    groups, ranks, subs, parts, hidden, grad_out, gain, grad_gate_up,
    grad_all, grad_hidden, sums, gate_up_sum,
    mine, held, landed, rounded, gate_up_landed, sends, recvs,
):
    k = Links(groups, ranks, sends, recvs)
    rows = hidden.shape[0] // subs
    scatters, gathers = sub_lines(k, subs, rows, parts, mine, held, landed, grad_all)
    gate_up_sums = [
        GroupScatter(
            k,
            lambda group, n=n: grad_gate_up.at[group, n],
            lambda i, n=n: gate_up_landed.at[n, i],
            n % 2 == 1,
        )
        for n in range(ranks)
    ]
    k.barrier()
    for scatter in scatters:
        scatter.start()
    for sums_of in gate_up_sums:
        sums_of.start(0)
    sums[...] = jnp.zeros_like(sums)

    def rows_of(part):
        total = hidden[part]
        scale = inverse_rms(total)
        scaled = total * scale
        grad = held[k.z, part].astype(F32)
        sums[...] += jnp.sum(grad * scaled, 0, keepdims=True)
        grad_total = grad_out[part].astype(F32) + norm_back(grad * gain[...], scaled, scale)
        grad_hidden[part] = grad_total
        rounded[part] = grad_total.astype(BF16)

    own = []
    for turn in range(subs + 1):
        if turn < subs:
            scatters[turn].pair()
        for i in range(k.chips - 1):
            if turn < subs:
                scatters[turn].step(i)
            if turn > 0:
                gathers[turn - 1].step(i + 1)
        if turn < subs:
            scatters[turn].last()
            row_loop(rows, rows_of, first=turn * rows)
            piece = pl.ds(turn * rows, rows)
            gathers[turn].start(rounded.at[piece])
            own.append(k.move(rounded.at[piece], grad_all.at[k.f, piece]))
        if turn == subs - 1:
            for sums_of in gate_up_sums:
                sums_of.wait(0)
                sums_of.start(1)
    for stage in range(1, k.bits):
        for n, sums_of in enumerate(gate_up_sums):
            if stage + 1 < k.bits:
                sums_of.wait(stage)
                sums_of.start(stage + 1)
            else:
                sums_of.wait(stage, gate_up_sum.at[n])
    for gather in gathers:
        gather.finish()
    for wait in own:
        wait()
    k.finish()


def attend_back_kernel(
    groups, ranks, rank_heads, grad_hidden, out_w, queries, keys, values, attended, bias, log_totals,
    cosine, sine, qkv, normed, gate_up_sum, grad_down,
    parts, grad_qkv_w, grad_out_w, gate_up_grad, down_grad,
    grad_qkv, keys_t, grad_keys, grad_values, down_landed, sends, recvs,
):
    k = Links(groups, ranks, sends, recvs)
    pieces = down_landed.shape[0]
    down_rows = down_grad.shape[0] // pieces
    down_sums = [
        GroupScatter(
            k,
            lambda group, n=n: grad_down.at[group, pl.ds(n * down_rows, down_rows)],
            lambda i, n=n: down_landed.at[n, i],
            n % 2 == 1,
        )
        for n in range(pieces)
    ]
    exchange = Exchange(k)
    gate_up_in = lambda rank: gate_up_grad.at[rank]
    k.barrier()
    exchange.start(lambda rank: gate_up_sum.at[rank], gate_up_in)
    for sums_of in down_sums:
        sums_of.start(0)
    blocks = keys_t.shape[0]
    grad_keys[...] = jnp.zeros_like(grad_keys)
    grad_values[...] = jnp.zeros_like(grad_values)

    @pl.loop(0, blocks)
    def _(i):
        block = pl.ds(pl.multiple_of(i * BLOCK, BLOCK), BLOCK)
        keys_t[i] = keys[block, :].astype(F32).T.astype(BF16)

    @pl.loop(0, blocks)
    def _(i):
        attend_back_rows(
            i, rank_heads, grad_hidden, out_w, queries, keys, keys_t, values, attended, bias, log_totals,
            cosine, sine, grad_keys, grad_values, grad_qkv,
        )

    for stage in range(k.bits - 1):
        for sums_of in down_sums:
            sums_of.wait(stage)
            sums_of.start(stage + 1)

    @pl.loop(0, blocks)
    def _(i):
        finish_back_rows(i, qkv, cosine, sine, grad_keys, grad_values, grad_qkv, parts)

    @pl.loop(0, normed.shape[1] // BLOCK)
    def _(t):
        part = pl.ds(pl.multiple_of(t * BLOCK, BLOCK), BLOCK)
        grad_qkv_w[part, :] = rows_inner(normed[:, part], grad_qkv[...]).astype(BF16)
        grad_out_w[:, part] = rows_inner(attended[...], grad_hidden[:, part]).astype(BF16)

    for n, sums_of in enumerate(down_sums):
        sums_of.wait(k.bits - 1, down_grad.at[pl.ds(n * down_rows, down_rows)])
    exchange.finish(gate_up_in)
    k.finish()


def last_kernel(
    groups, ranks, slice_width, parts, tokens, grad_hidden, gain, sums_two, grad_qkv, grad_out_w,
    grad_tokens, qkv_grad, out_grad, gain_grads,
    mine, held, landed, sums, qkv_landed, out_landed, tiles, tiles_landed, tiles_sum, group_tiles, sends, recvs,
):
    k = Links(groups, ranks, sends, recvs)
    rows = tokens.shape[0]
    scatter = LineScatter(
        k, lambda rank: parts.at[rank], lambda chip: mine.at[chip], lambda chip: held.at[chip], lambda side, chip: landed.at[side, chip]
    )
    qkv_sums = [
        GroupScatter(
            k,
            lambda group, n=n: grad_qkv.at[group, n],
            lambda i, n=n: qkv_landed.at[n, i],
            n % 2 == 1,
        )
        for n in range(ranks)
    ]
    pieces = out_landed.shape[0]
    piece_rows = out_grad.shape[0] // pieces
    out_sums = [
        GroupScatter(
            k,
            lambda group, n=n: grad_out_w.at[group, pl.ds(n * piece_rows, piece_rows)],
            lambda i, n=n: out_landed.at[n, i],
            n % 2 == 1,
        )
        for n in range(pieces)
    ]
    exchange, tile_exchange = Exchange(k), Exchange(k)
    tile_sends, tile_recvs = k.take(groups, groups)
    qkv_in = lambda rank: qkv_grad.at[rank]
    k.barrier()
    scatter.start()
    for sums_of in qkv_sums:
        sums_of.start(0)
    for sums_of in out_sums:
        sums_of.start(0)
    scatter.pair()
    for i in range(k.chips - 1):
        scatter.step(i)
        if i == 0:
            for sums_of in qkv_sums:
                sums_of.wait(0)
                sums_of.start(1)
    for stage in range(1, k.bits - 1):
        for sums_of in qkv_sums:
            sums_of.wait(stage)
            sums_of.start(stage + 1)
    for n, sums_of in enumerate(qkv_sums):
        exchange.start_piece(n, sums_of.wait(k.bits - 1), qkv_in)
    scatter.last()
    sums[...] = jnp.zeros_like(sums)

    def rows_of(part):
        total = tokens[part].astype(F32)
        scale = inverse_rms(total)
        scaled = total * scale
        grad = held[k.z, part].astype(F32)
        sums[...] += jnp.sum(grad * scaled, 0, keepdims=True)
        grad_tokens[part] = (
            grad_hidden[part] + norm_back(grad * gain[...], scaled, scale)
        ).astype(BF16)

    row_loop(rows, rows_of)
    tiles[...] = jnp.zeros_like(tiles)
    for rank in range(ranks):
        for group in range(groups):
            at = (group * ranks + rank) * slice_width // 128 * 128
            tiles[rank, group, 0:1] = sums[:, at : at + 128]
            tiles[rank, group, 1:2] = sums_two[:, at : at + 128]
    tile_in = lambda rank: tiles_landed.at[rank]
    tile_exchange.start(lambda rank: tiles.at[rank], tile_in)
    for stage in range(k.bits - 1):
        for sums_of in out_sums:
            sums_of.wait(stage)
            sums_of.start(stage + 1)
    for n, sums_of in enumerate(out_sums):
        sums_of.wait(k.bits - 1, out_grad.at[pl.ds(n * piece_rows, piece_rows)])
    tile_exchange.finish(tile_in)
    total = tiles_landed[0]
    for rank in range(1, ranks):
        total = total + tiles_landed[rank]
    tiles_sum[...] = total
    for i in range(1, groups):
        other = lax.rem(k.d + i, groups)
        k.send(
            None,
            tiles_sum.at[other],
            group_tiles.at[k.d],
            tile_sends + other,
            tile_recvs + k.d,
            (other, k.f),
        )
    group_tiles[k.d] = tiles_sum[k.d]
    for i in range(1, groups):
        other = lax.rem(k.d + i, groups)
        k.arrived(None, group_tiles.at[other], tile_recvs + other)
    total = group_tiles[0]
    for group in range(1, groups):
        total = total + group_tiles[group]
    gain_grads[...] = total
    exchange.finish(qkv_in, own=False)
    k.finish()


VMEM = pl.BlockSpec(memory_space=pltpu.VMEM)
ANY = pl.BlockSpec(memory_space=pl.ANY)


def call(kernel, identity, ins, outs, scratch, semaphores, args):
    return pl.pallas_call(
        kernel,
        out_shape=[jax.ShapeDtypeStruct(shape, kind) for shape, kind, _ in outs],
        in_specs=ins,
        out_specs=[place for _, _, place in outs],
        scratch_shapes=[pltpu.VMEM(shape, kind) for shape, kind in scratch]
        + [pltpu.SemaphoreType.DMA((semaphores,))] * 2,
        compiler_params=pltpu.CompilerParams(
            collective_id=identity, has_side_effects=True, vmem_limit_bytes=60 * 1024 * 1024
        ),
    )(*args)


def build(groups, ranks):
    def body(
        tokens, cotangent, lengths, norm_attn, w_query, w_key, w_value, w_output, norm_mlp, w_gate, w_up, w_down
    ):
        rows, width = tokens.shape
        depth = w_query.shape[0]
        count = rows * ranks
        rank_heads = HEADS // ranks
        hidden_part = w_down.shape[0]
        out_rows = w_output.shape[0]
        split = max(1, HEAD_DIM // out_rows)
        rank = lax.axis_index("fsdp")

        def heads_out(weight):
            shaped = weight.reshape(depth, split, rank_heads, ranks // split, HEAD_DIM)
            return shaped.transpose(3, 1, 0, 2, 4).reshape(ranks, depth, rank_heads * HEAD_DIM)

        def heads_in(pieces):
            shaped = pieces.reshape(ranks // split, split, depth, rank_heads, HEAD_DIM)
            return shaped.transpose(2, 1, 3, 0, 4).reshape(depth, HEADS * HEAD_DIM)

        def units_out(weight):
            shaped = weight.reshape(depth, groups, ranks, hidden_part)
            return shaped.transpose(2, 0, 1, 3).reshape(ranks, depth, groups * hidden_part)

        def units_in(pieces):
            shaped = pieces.reshape(ranks, depth, groups, hidden_part)
            return shaped.transpose(1, 2, 0, 3).reshape(depth, groups * ranks * hidden_part)

        span = [[base * split + i for i in range(split)] for base in range(ranks // split)]

        def widen(weight):
            if split > 1:
                weight = lax.all_gather(weight, "fsdp", axis=0, tiled=True, axis_index_groups=span)
            return weight

        def narrow(whole):
            if split > 1:
                whole = whole.reshape(split, -1, width)[lax.rem(rank, split)]
            return whole

        def place_output(grad):
            if split > 1:
                place = lax.rem(rank, split)
                grad = jnp.where(
                    (jnp.arange(split) == place)[:, None, None], grad[None], jnp.zeros((), BF16)
                )
            return grad.reshape(groups, -1, width)

        head_cols = rank_heads * HEAD_DIM
        unit_cols = groups * hidden_part
        chips = ranks // 2
        slice_width = norm_attn.shape[0]
        qkv_out = jnp.concatenate([heads_out(w) for w in (w_query, w_key, w_value)], -1)
        gate_up_out = jnp.concatenate([units_out(w) for w in (w_gate, w_up)], -1)
        gains = jnp.pad(
            jnp.stack([norm_attn, norm_mlp]), ((0, 14), (0, 128 - slice_width))
        )
        out_own = widen(w_output)
        x_all, qkv, gains_all, out_w, down_w = call(
            functools.partial(first_kernel, groups, ranks),
            1,
            [VMEM] * 5,
            [
                ((ranks, rows, width), BF16, ANY),
                ((groups,) + qkv_out.shape, BF16, ANY),
                ((groups, ranks, 16, 128), BF16, ANY),
                ((groups,) + out_own.shape, BF16, ANY),
                ((groups,) + w_down.shape, BF16, ANY),
            ],
            [],
            160,
            (tokens, qkv_out, gains, out_own, w_down),
        )
        qkv = qkv.reshape(width, -1)
        gain_one, gain_two = (
            gains_all[:, :, i, :slice_width].astype(F32).reshape(1, width) for i in range(2)
        )
        out_w = narrow(out_w.reshape(-1, width))
        down_w = down_w.reshape(-1, width)

        places = jnp.arange(count, dtype=jnp.int32)
        bias = jnp.where(places < lengths[0], 0.0, -1000000000.0).astype(F32)[:, None]
        cosine, sine = wide_tables(count, head_cols)
        blocks = count // BLOCK
        heads_shape = ((count, head_cols), BF16, VMEM)
        parts, normed_one, queries, keys, values, attended, log_totals, cotangent_all, gate_up = call(
            functools.partial(attend_kernel, groups, ranks, rank_heads),
            5,
            [VMEM] * 9,
            [((count, width), BF16, VMEM)] * 2
            + [heads_shape] * 4
            + [
                ((blocks, rank_heads, BLOCK), F32, VMEM),
                ((ranks, rows, width), BF16, ANY),
                ((groups,) + gate_up_out.shape, BF16, ANY),
            ],
            [((blocks, head_cols, BLOCK), BF16)],
            192,
            (
                x_all.reshape(count, width),
                cotangent,
                gate_up_out,
                qkv,
                gain_one,
                out_w,
                cosine,
                sine,
                bias,
            ),
        )
        gate_up = gate_up.reshape(width, -1)
        line_scratch = [((chips, rows, width), BF16)] * 2 + [((2, chips, rows, width), BF16)]
        hidden, normed_two = call(
            functools.partial(hidden_kernel, groups, ranks, 2),
            2,
            [ANY] + [VMEM] * 2,
            [((rows, width), F32, VMEM), ((ranks, rows, width), BF16, ANY)],
            line_scratch + [((rows, width), BF16)],
            160,
            (parts.reshape(ranks, rows, width), tokens, gain_two),
        )
        normed_two = normed_two.reshape(count, width)
        gate_up_lin = dot(normed_two, gate_up)
        gate, up = gate_up_lin[:, :unit_cols], gate_up_lin[:, unit_cols:]
        sigmoid = 1.0 / (1.0 + jnp.exp(-gate))
        silu = gate * sigmoid
        mixed = (silu * up).astype(BF16)
        down_sum = lax.psum_scatter(
            dot(mixed, down_w).astype(BF16), "fsdp", scatter_dimension=0, tiled=True
        )
        output = (hidden + down_sum.astype(F32)).astype(BF16)

        live = places[:, None] < lengths[0]
        grad_out_all = jnp.where(
            live, cotangent_all.reshape(count, width), jnp.zeros((), BF16)
        )
        own_places = rank * rows + jnp.arange(rows, dtype=jnp.int32)
        grad_out = jnp.where(own_places[:, None] < lengths[0], cotangent, jnp.zeros((), BF16))
        grad_mixed = cols_inner(grad_out_all, down_w)
        grad_down = rows_inner(mixed, grad_out_all).astype(BF16).reshape(groups, hidden_part, width)
        grad_gate = grad_mixed * up * (sigmoid * (1.0 + gate * (1.0 - sigmoid)))
        grad_up = grad_mixed * silu
        grad_gate_up = jnp.concatenate([grad_gate.astype(BF16), grad_up.astype(BF16)], -1)
        parts = cols_inner(grad_gate_up, gate_up).astype(BF16).reshape(ranks, rows, width)
        grad_gate_up_w = rows_inner(normed_two, grad_gate_up).astype(BF16)
        grad_hidden_all, grad_hidden, sums_two, gate_up_sum = call(
            functools.partial(middle_kernel, groups, ranks, 2),
            3,
            [ANY] + [VMEM] * 4,
            [
                ((ranks, rows, width), BF16, ANY),
                ((rows, width), F32, VMEM),
                ((1, width), F32, VMEM),
                ((ranks, depth, 2 * unit_cols), BF16, VMEM),
            ],
            line_scratch
            + [
                ((rows, width), BF16),
                ((ranks, groups - 1, depth, 2 * unit_cols), BF16),
            ],
            160,
            (
                parts,
                hidden,
                grad_out,
                gain_two,
                grad_gate_up_w.reshape(groups, ranks, depth, 2 * unit_cols),
            ),
        )
        pieces = 4
        parts, grad_qkv_w, grad_out_w, grad_gate_up_w, grad_w_down = call(
            functools.partial(attend_back_kernel, groups, ranks, rank_heads),
            6,
            [VMEM] * 14,
            [
                ((count, width), BF16, VMEM),
                ((width, 3 * head_cols), BF16, VMEM),
                ((head_cols, width), BF16, VMEM),
                ((ranks, depth, 2 * unit_cols), BF16, ANY),
                ((hidden_part, width), F32, VMEM),
            ],
            [
                ((count, 3 * head_cols), BF16),
                ((blocks, head_cols, BLOCK), BF16),
                ((count, head_cols), F32),
                ((count, head_cols), F32),
                ((pieces, groups - 1, hidden_part // pieces, width), BF16),
            ],
            160,
            (
                grad_hidden_all.reshape(count, width),
                out_w,
                queries,
                keys,
                values,
                attended,
                bias,
                log_totals,
                cosine,
                sine,
                qkv,
                normed_one,
                gate_up_sum,
                grad_down,
            ),
        )
        grad_out_w = place_output(grad_out_w)
        grad_w_gate = units_in(grad_gate_up_w[..., :unit_cols]).astype(F32)
        grad_w_up = units_in(grad_gate_up_w[..., unit_cols:]).astype(F32)
        parts = parts.reshape(ranks, rows, width)
        pieces = 2
        out_rows = grad_out_w.shape[1]
        tile = (8, 128)
        grad_tokens, grad_qkv_w, grad_w_output, sums = call(
            functools.partial(last_kernel, groups, ranks, slice_width),
            4,
            [ANY] + [VMEM] * 6,
            [
                ((rows, width), BF16, VMEM),
                ((ranks, depth, 3 * head_cols), BF16, ANY),
                ((out_rows, width), F32, VMEM),
                (tile, F32, VMEM),
            ],
            line_scratch
            + [
                ((1, width), F32),
                ((ranks, groups - 1, depth, 3 * head_cols), BF16),
                ((pieces, groups - 1, out_rows // pieces, width), BF16),
                ((ranks, groups) + tile, F32),
                ((ranks, groups) + tile, F32),
                ((groups,) + tile, F32),
                ((groups,) + tile, F32),
            ],
            160,
            (
                parts,
                tokens,
                grad_hidden,
                gain_one,
                sums_two,
                grad_qkv_w.reshape(groups, ranks, depth, 3 * head_cols),
                grad_out_w,
            ),
        )
        if split > 1:
            grad_w_output = lax.psum_scatter(
                grad_w_output, "fsdp", scatter_dimension=0, tiled=True, axis_index_groups=span
            )
        grad_w_query, grad_w_key, grad_w_value = (
            heads_in(grad_qkv_w[..., i * head_cols : (i + 1) * head_cols]).astype(F32) for i in range(3)
        )
        place = (lax.axis_index("dp") * ranks + rank) * slice_width % 128
        sums = lax.dynamic_slice_in_dim(sums, place, slice_width, 1)
        return (
            output,
            grad_tokens,
            sums[0],
            grad_w_query,
            grad_w_key,
            grad_w_value,
            grad_w_output,
            sums[1],
            grad_w_gate,
            grad_w_up,
            grad_w_down,
        )

    return body


def solution(mesh):
    both = P(("dp", "fsdp"))
    rows = P(("dp", "fsdp"), None)
    return jax.shard_map(
        build(mesh.shape["dp"], mesh.shape["fsdp"]),
        mesh=mesh,
        in_specs=(rows, rows, P("dp"), both, rows, rows, rows, rows, both, rows, rows, rows),
        out_specs=(rows, rows, both, rows, rows, rows, rows, both, rows, rows, rows),
        check_vma=False,
    )
```

```python
import functools

import jax
import jax.numpy as jnp
import numpy as np
from jax import lax
from jax.experimental import pallas as pl
from jax.experimental.pallas import tpu as pltpu
from jax.sharding import PartitionSpec as P

HEADS = 32
HEAD_DIM = 64


EPSILON = 1e-05
THETA = 130000.0
BF16 = jnp.bfloat16
F32 = jnp.float32


def dot(left, right):
    return jnp.dot(left, right, preferred_element_type=F32)


def rows_inner(left, right):
    return lax.dot_general(left, right, (((0,), (0,)), ((), ())), preferred_element_type=F32)


def cols_inner(left, right):
    return lax.dot_general(left, right, (((1,), (1,)), ((), ())), preferred_element_type=F32)


def inverse_rms(values):
    return lax.rsqrt(jnp.mean(values * values, -1, keepdims=True) + EPSILON)


def norm_back(grad_scaled, scaled, scale):
    return scale * (grad_scaled - scaled * jnp.mean(grad_scaled * scaled, -1, keepdims=True))


BLOCK = 256
SCALE = 0.125


def turn_halves(values, cosine, sine):
    width = values.shape[1]
    half = HEAD_DIM // 2
    lane = lax.broadcasted_iota(jnp.int32, values.shape, 1)
    ahead = pltpu.roll(values, width - half, 1)
    behind = pltpu.roll(values, half, 1)
    return values * cosine + jnp.where(lane % HEAD_DIM < half, ahead, behind) * sine


def wide_tables(count):
    half = HEAD_DIM // 2
    inverse = np.float32(THETA) ** (-np.arange(half, dtype=np.float32) * np.float32(2.0) / HEAD_DIM)
    angles = np.arange(count, dtype=np.float32)[:, None] * inverse.astype(np.float32)[None, :]
    cosine, sine = np.cos(angles).astype(np.float32), np.sin(angles).astype(np.float32)
    return np.concatenate([cosine] * 4, -1), np.concatenate([-sine, sine] * 2, -1)


def table_rows(table, block, width):
    return jnp.concatenate([table[block, :]] * (width // 128), 1)


def key_bias(j, length):
    place = j * BLOCK + lax.broadcasted_iota(jnp.int32, (BLOCK, 1), 0)
    return jnp.where(place < length, 0.0, -1000000000.0)


def head_rows(values, head):
    row = lax.broadcasted_iota(jnp.int32, values.shape, 0)
    return jnp.where((row >= head * HEAD_DIM) & (row < (head + 1) * HEAD_DIM), values, 0.0)


def future(shape):
    return lax.broadcasted_iota(jnp.int32, shape, 0) > lax.broadcasted_iota(jnp.int32, shape, 1)


def attend_block(i, rank_heads, queries, keys, values_t, length, attended, log_totals):
    queries_t = queries.T
    masked = [(head_rows(queries_t, h) * SCALE).astype(BF16) for h in range(rank_heads)]

    def chunk(j, carry, last):
        part = pl.ds(pl.multiple_of(j * BLOCK, BLOCK), BLOCK)
        key_part, bias_part = keys[part, :], key_bias(j, length)
        after = []
        for h in range(rank_heads):
            top, total, out = carry[h]
            scores = dot(key_part, masked[h]) + bias_part
            if last:
                scores = jnp.where(future(scores.shape), -1000000000.0, scores)
            new_top = jnp.maximum(top, jnp.max(scores, 0, keepdims=True))
            keep = jnp.exp(top - new_top)
            weights = jnp.exp(scores - new_top)
            total = total * keep + jnp.sum(weights, 0, keepdims=True)
            out = out * keep + dot(
                values_t[j, h * HEAD_DIM : (h + 1) * HEAD_DIM, :], weights.astype(BF16)
            )
            after.append((new_top, total, out))
        return tuple(after)

    carry = tuple(
        (
            jnp.full((1, BLOCK), -3.0e38, F32),
            jnp.zeros((1, BLOCK), F32),
            jnp.zeros((HEAD_DIM, BLOCK), F32),
        )
        for _ in range(rank_heads)
    )
    carry = lax.fori_loop(0, i, lambda j, c: chunk(j, c, False), carry)
    carry = chunk(i, carry, True)
    outs = []
    for h, (top, total, out) in enumerate(carry):
        log_totals[i, h : h + 1, :] = top + jnp.log(total)
        outs.append(out * (1.0 / total))
    attended[pl.ds(pl.multiple_of(i * BLOCK, BLOCK), BLOCK), :] = (
        jnp.concatenate(outs, 0).T.astype(BF16)
    )


def project_block(i, x, gain, qkv, cosine, sine, normed, queries, keys, values, values_t):
    cols = queries.shape[1]
    start = i * BLOCK

    def rows_of(part):
        rows = x[part, :].astype(F32)
        normed[part, :] = (rows * inverse_rms(rows) * gain[0:1, :]).astype(BF16)

    pl.loop(0, BLOCK // 16)(
        lambda t: rows_of(pl.ds(pl.multiple_of(start + t * 16, 16), 16))
    )
    block = pl.ds(pl.multiple_of(start, BLOCK), BLOCK)
    rows = normed[block, :]

    def weight(n):
        return qkv[:, :, :, n * cols : (n + 1) * cols].reshape(x.shape[1], cols)

    cos, sin = table_rows(cosine, block, cols), table_rows(sine, block, cols)
    rounded = turn_halves(dot(rows, weight(0)), cos, sin).astype(BF16)
    queries[block, :] = rounded
    keys[block, :] = turn_halves(dot(rows, weight(1)), cos, sin).astype(BF16)
    value = dot(rows, weight(2))
    values[block, :] = value.astype(BF16)
    values_t[i] = value.T.astype(BF16)
    return rounded.astype(F32)


def lanes_of(values, head):
    lane = lax.broadcasted_iota(jnp.int32, values.shape, 1)
    return jnp.where((lane >= head * HEAD_DIM) & (lane < (head + 1) * HEAD_DIM), values, 0.0)


def attend_back_block(
    i, rank_heads, queries, keys, keys_t, values, attended, grad, length, log_totals, grad_keys, grad_values
):
    block = pl.ds(pl.multiple_of(i * BLOCK, BLOCK), BLOCK)
    query = queries[block, :].astype(F32) * SCALE
    query_t, grad_t = query.T, grad.T
    product = attended[block, :].astype(F32).T * grad_t
    masked_q = [head_rows(query_t, h).astype(BF16) for h in range(rank_heads)]
    masked_g = [head_rows(grad_t, h).astype(BF16) for h in range(rank_heads)]
    stacked_q = jnp.concatenate([lanes_of(query, h).astype(BF16) for h in range(rank_heads)], 0)
    stacked_g = jnp.concatenate([lanes_of(grad, h).astype(BF16) for h in range(rank_heads)], 0)
    deltas = [
        jnp.sum(product[h * HEAD_DIM : (h + 1) * HEAD_DIM], 0, keepdims=True)
        for h in range(rank_heads)
    ]
    totals = [log_totals[i, h : h + 1, :] for h in range(rank_heads)]

    def chunk(j, carry, last):
        part = pl.ds(pl.multiple_of(j * BLOCK, BLOCK), BLOCK)
        key_part, value_part, bias_part = keys[part, :], values[part, :], key_bias(j, length)
        after, weights_all, grads_all = [], [], []
        for h in range(rank_heads):
            scores = dot(key_part, masked_q[h]) + bias_part
            if last:
                scores = jnp.where(future(scores.shape), -1000000000.0, scores)
            weights = jnp.exp(scores - totals[h])
            grad_scores = weights * (dot(value_part, masked_g[h]) - deltas[h])
            weights_all.append(weights.astype(BF16))
            grads_all.append(grad_scores.astype(BF16))
            after.append(
                carry[h] + dot(keys_t[j, h * HEAD_DIM : (h + 1) * HEAD_DIM, :], grads_all[-1])
            )
        grad_values[part, :] += dot(jnp.concatenate(weights_all, 1), stacked_g)
        grad_keys[part, :] += dot(jnp.concatenate(grads_all, 1), stacked_q)
        return tuple(after)

    carry = tuple(jnp.zeros((HEAD_DIM, BLOCK), F32) for _ in range(rank_heads))
    carry = lax.fori_loop(0, i, lambda j, c: chunk(j, c, False), carry)
    carry = chunk(i, carry, True)
    return jnp.concatenate(carry, 0).T * SCALE


def attend_back_rows(
    i, rank_heads, grad_hidden, out_w, queries, keys, keys_t, values, attended, length, log_totals,
    cosine, sine, grad_keys, grad_values, grad_qkv,
):
    block = pl.ds(pl.multiple_of(i * BLOCK, BLOCK), BLOCK)
    cols = queries.shape[1]
    grad = cols_inner(grad_hidden[block, :], out_w[...]).astype(BF16).astype(F32)
    grad_q = attend_back_block(
        i, rank_heads, queries, keys, keys_t, values, attended, grad, length, log_totals, grad_keys, grad_values
    )
    grad_qkv[block, :cols] = turn_halves(
        grad_q, table_rows(cosine, block, cols), -table_rows(sine, block, cols)
    ).astype(BF16)


def finish_back_rows(i, qkv, cosine, sine, grad_keys, grad_values, grad_qkv, parts):
    block = pl.ds(pl.multiple_of(i * BLOCK, BLOCK), BLOCK)
    cols = grad_keys.shape[1]
    grad_qkv[block, cols : 2 * cols] = turn_halves(
        grad_keys[block, :], table_rows(cosine, block, cols), -table_rows(sine, block, cols)
    ).astype(BF16)
    grad_qkv[block, 2 * cols :] = grad_values[block, :].astype(BF16)
    rows = grad_qkv[block, :]
    step = 512

    @pl.loop(0, qkv.shape[0] // step)
    def _(c):
        part = pl.ds(pl.multiple_of(c * step, step), step)
        parts[block, part] = cols_inner(rows, qkv[part, :]).astype(BF16)

MESH = pl.DeviceIdType.MESH


def when(cond, action):
    if cond is None:
        action()
    else:
        pl.when(cond)(action)


class Links:
    def __init__(self, groups, ranks, sends, recvs):
        self.groups, self.ranks, self.chips = groups, ranks, ranks // 2
        self.bits = groups.bit_length() - 1
        self.sends, self.recvs = sends, recvs
        self.used_sends = self.used_recvs = 0
        self.d, self.f = lax.axis_index("dp"), lax.axis_index("fsdp")
        self.z, self.c = lax.div(self.f, 2), lax.rem(self.f, 2)
        self.sibling = (self.d, self.z * 2 + 1 - self.c)
        self.pending = []

    def bit(self, b):
        return lax.rem(lax.div(self.d, 1 << b), 2)

    def partner(self, b):
        return (self.d + (1 - 2 * self.bit(b)) * (1 << b), self.f)

    def beside(self, way):
        return (self.d, self.f + 2 * way)

    def barrier(self):
        gate = pltpu.get_barrier_semaphore()
        for k in range(1, self.ranks):
            other = lax.rem(self.f + k, self.ranks)
            pl.semaphore_signal(gate, inc=1, device_id=(self.d, other), device_id_type=MESH)
        for k in range(1, self.groups):
            other = lax.rem(self.d + k, self.groups)
            pl.semaphore_signal(gate, inc=1, device_id=(other, self.f), device_id_type=MESH)
        pl.semaphore_wait(gate, self.ranks + self.groups - 2)

    def take(self, sends, recvs):
        first = (self.used_sends, self.used_recvs)
        self.used_sends += sends
        self.used_recvs += recvs
        return first

    def copy(self, source, target, send, recv, device):
        return pltpu.make_async_remote_copy(
            src_ref=source,
            dst_ref=target,
            send_sem=self.sends.at[send],
            recv_sem=self.recvs.at[recv],
            device_id=device,
            device_id_type=MESH,
        )

    def send(self, cond, source, target, send, recv, device, later=True):
        when(cond, lambda: self.copy(source, target, send, recv, device).start())
        gone = lambda: when(
            cond, lambda: self.copy(source, target, send, recv, device).wait_send()
        )
        if later:
            self.pending.append(gone)
        return gone

    def arrived(self, cond, target, recv):
        when(cond, lambda: self.copy(target, target, 0, recv, self.sibling).wait_recv())

    def move(self, source, target):
        send, _ = self.take(1, 0)
        make = lambda: pltpu.make_async_copy(source, target, self.sends.at[send])
        make().start()
        return lambda: make().wait()

    def finish(self):
        for wait in self.pending:
            wait()
        self.pending = []


class LineGather:
    def __init__(self, links, view):
        self.links, self.view = links, view
        chips = links.chips
        self.sends, self.recvs = links.take(3 * chips, 3 * chips)

    def start(self, source):
        k, chips = self.links, self.links.chips
        target = self.view(k.f)
        for side, way in enumerate((1, -1)):
            valid = (k.z + way >= 0) & (k.z + way < chips)
            k.send(
                valid, source, target, self.sends + side * chips, self.recvs + side * chips + 1, k.beside(way)
            )
        k.send(
            None, source, target, self.sends + 2 * chips + k.z, self.recvs + 2 * chips + k.z, k.sibling
        )

    def step(self, reach):
        k, chips = self.links, self.links.chips
        for side, way in enumerate((1, -1)):
            origin = k.z - way * reach
            here = (origin >= 0) & (origin < chips)
            block = self.view(origin * 2 + k.c)
            k.arrived(here, block, self.recvs + side * chips + reach)
            if reach + 1 < chips:
                onward = here & (k.z + way >= 0) & (k.z + way < chips)
                k.send(
                    onward,
                    block,
                    block,
                    self.sends + side * chips + reach,
                    self.recvs + side * chips + reach + 1,
                    k.beside(way),
                )
            k.send(
                here,
                block,
                block,
                self.sends + 2 * chips + origin,
                self.recvs + 2 * chips + origin,
                k.sibling,
            )

    def over(self, chip):
        k = self.links
        k.arrived(None, self.view(chip * 2 + 1 - k.c), self.recvs + 2 * k.chips + chip)

    def finish(self):
        k, chips = self.links, self.links.chips
        for chip in range(chips):
            k.arrived(None, self.view(chip * 2 + 1 - k.c), self.recvs + 2 * chips + chip)


def add_rows(target, *sources, step=16):
    rows = target.shape[0]

    @pl.loop(0, rows // step)
    def _(i):
        part = pl.ds(pl.multiple_of(i * step, step), step)
        total = sources[0][part].astype(F32)
        for source in sources[1:]:
            total = total + source[part].astype(F32)
        target[part] = total.astype(target.dtype)


class LineScatter:
    def __init__(self, links, parts, mine, held, landed):
        self.links, self.parts, self.mine = links, parts, mine
        self.held, self.landed = held, landed
        chips = links.chips
        self.sends, self.recvs = links.take(2 * chips, 3 * chips)
        self.gone = [lambda: None] * 2

    def start(self):
        k, chips = self.links, self.links.chips
        for chip in range(chips):
            k.send(
                None,
                self.parts(chip * 2 + 1 - k.c),
                self.held(chip),
                self.sends + chip,
                self.recvs + chip,
                k.sibling,
            )
        self.own = [k.move(self.parts(chip * 2 + k.c), self.mine(chip)) for chip in range(chips)]

    def pair(self):
        k = self.links
        for chip in range(k.chips):
            self.own[chip]()
            k.arrived(None, self.held(chip), self.recvs + chip)
            add_rows(self.held(chip), self.held(chip), self.mine(chip))

    def step(self, i):
        k, chips = self.links, self.links.chips
        for side, way in enumerate((1, -1)):
            chip = k.z + way * (chips - 1 - i)
            before = (chip >= 0) & (chip < chips)
            inner = before & (k.z > 0 if way > 0 else k.z < chips - 1)
            mine = self.recvs + (1 + side) * chips + chip

            def add():
                k.arrived(None, self.landed(side, chip), mine)
                add_rows(self.held(chip), self.held(chip), self.landed(side, chip))

            pl.when(inner)(add)
            self.gone[side]()
            self.gone[side] = k.send(
                before,
                self.held(chip),
                self.landed(side, chip),
                self.sends + chips + chip,
                mine,
                k.beside(way),
                later=False,
            )

    def last(self):
        k, chips = self.links, self.links.chips
        for side, inner in enumerate((k.z > 0, k.z < chips - 1)):

            def add():
                k.arrived(None, self.landed(side, k.z), self.recvs + (1 + side) * chips + k.z)
                add_rows(self.held(k.z), self.held(k.z), self.landed(side, k.z))

            pl.when(inner)(add)
        for gone in self.gone:
            gone()


class Exchange:
    def __init__(self, links):
        self.links = links
        self.sends, self.recvs = links.take(links.ranks, links.ranks)

    def start(self, source, target):
        k = self.links
        self.own = k.move(source(k.f), target(k.f))
        for i in range(1, k.ranks):
            other = lax.rem(k.f + i, k.ranks)
            k.send(
                None, source(other), target(k.f), self.sends + other, self.recvs + k.f, (k.d, other)
            )

    def finish(self, target, own=True):
        k = self.links
        if own:
            self.own()
        for i in range(1, k.ranks):
            other = lax.rem(k.f + i, k.ranks)
            k.arrived(None, target(other), self.recvs + other)

    def start_piece(self, rank, source, target):
        k = self.links
        k.send(
            k.f != rank, source, target(k.f), self.sends + rank, self.recvs + k.f, (k.d, rank)
        )
        here = lambda: pltpu.make_async_copy(source, target(k.f), k.sends.at[self.sends + rank])
        pl.when(k.f == rank)(lambda: here().start())
        k.pending.append(lambda: pl.when(k.f == rank)(lambda: here().wait()))


class GroupGather:
    def __init__(self, links, view, high):
        self.links, self.view, self.high = links, view, high
        count = links.groups - 1
        self.sends, self.recvs = links.take(count, count)

    def flip(self, stage):
        k = self.links
        low, up = 1 << stage, 1 << (k.bits - 1 - stage)
        size = low + self.high * (up - low)
        return (1 - 2 * lax.rem(lax.div(k.d, size), 2)) * size

    def places(self, stage):
        places = [self.links.d]
        for past in range(stage):
            places = places + [place + self.flip(past) for place in places]
        return places

    def start(self, stage, source=None):
        k = self.links
        for i, place in enumerate(self.places(stage)):
            at = (1 << stage) - 1 + i
            target = self.view(place)
            k.send(
                None,
                target if source is None else source,
                target,
                self.sends + at,
                self.recvs + at,
                (k.d + self.flip(stage), k.f),
            )

    def arrivals(self, stage):
        return [place + self.flip(stage) for place in self.places(stage)]

    def wait(self, stage):
        for i, place in enumerate(self.arrivals(stage)):
            self.links.arrived(None, self.view(place), self.recvs + (1 << stage) - 1 + i)


class GroupScatter:
    def __init__(self, links, view, landed, high):
        self.links, self.view, self.landed = links, view, landed
        bits = list(range(links.bits))
        self.order = bits[::-1] if high else bits
        count = links.groups - 1
        self.sends, self.recvs = links.take(count, count)

    def base(self, stage):
        return sum(self.links.groups >> (s + 1) for s in range(stage))

    def sources(self, stage, flip):
        k = self.links
        b = self.order[stage]
        value = 1 - k.bit(b) if flip else k.bit(b)
        if stage > 0:
            count = k.groups >> (stage + 1)
            return [self.landed(self.base(stage - 1) + value + 2 * i) for i in range(count)]
        places = [value * (1 << b)]
        for b in self.order[1:]:
            places = places + [place + (1 << b) for place in places]
        return [self.view(place) for place in places]

    def start(self, stage):
        k = self.links
        for i, source in enumerate(self.sources(stage, True)):
            at = self.base(stage) + i
            k.send(
                None,
                source,
                self.landed(at),
                self.sends + at,
                self.recvs + at,
                k.partner(self.order[stage]),
            )

    def wait(self, stage, target=None):
        k = self.links
        for i, source in enumerate(self.sources(stage, False)):
            at = self.base(stage) + i
            k.arrived(None, self.landed(at), self.recvs + at)
            add_rows(self.landed(at) if target is None else target, source, self.landed(at))
        return self.landed(self.base(stage))


def row_loop(rows, action, step=16, first=0):
    @pl.loop(0, rows // step)
    def _(i):
        action(pl.ds(pl.multiple_of(first + i * step, step), step))


def spaced(events, blocks):
    count = len(events)
    return [events[b * count // blocks : (b + 1) * count // blocks] for b in range(blocks)]


def attend_kernel(
    groups, ranks, rank_heads, slice_width,
    lengths, tokens, qkv_out, gains, out_w, down_w, gate_up_out, cosine, sine,
    x_all, qkv, gain_rows, normed, queries, keys, values, attended, log_totals,
    attended_all, gate_up, out_all, down_all,
    gains_all, values_t, sends, recvs,
):
    k = Links(groups, ranks, sends, recvs)
    length = lengths[0]
    cols, rows = queries.shape[1], tokens.shape[0]
    depth, half = gate_up_out.shape[1], ranks // 2
    pieces = depth // 16
    blocks = values_t.shape[0]
    split = max(1, HEAD_DIM // out_w.shape[0])
    down_half = down_w.shape[0] // 2

    def unit(group, rank):
        return (
            (lax.div(rank, split) * split + lax.div(group, rank_heads)) * rank_heads
            + lax.rem(group, rank_heads)
        ) * split + lax.rem(rank, split)

    def out_block(group, rank):
        return out_all.at[unit(group, rank)]

    def attended_block(i, rank):
        return attended_all.at[
            pl.ds(i * BLOCK, BLOCK), pl.ds(pl.multiple_of(rank * cols, cols), cols)
        ]

    x_line = LineGather(k, lambda rank: x_all.at[pl.ds(pl.multiple_of(rank * rows, 16), rows)])
    out_line = LineGather(k, lambda rank: out_block(k.d, rank))
    lines = [LineGather(k, lambda rank, i=i: attended_block(i, rank)) for i in range(blocks)]
    gains_ex, qkv_ex = Exchange(k), Exchange(k)
    exchanges = [Exchange(k) for _ in range(pieces)]
    downs = [
        GroupGather(k, lambda group, h=h: down_all.at[group, pl.ds(h * down_half, down_half)], h)
        for h in range(2)
    ]
    late = [
        GroupGather(k, lambda group, h=h, ref=ref: ref.at[group, pl.ds(h * half, half)], h)
        for ref in (qkv, gains_all)
        for h in range(2)
    ]
    out_gathers = [
        GroupGather(k, lambda group, r=r: out_block(group, k.c * half + r), k.c) for r in range(half)
    ]
    gathers = [
        [
            GroupGather(
                k,
                lambda group, h=h, q=q: gate_up.at[group, pl.ds(h * half, half), pl.ds(q * 16, 16)],
                h,
            )
            for h in range(2)
        ]
        for q in range(pieces)
    ]
    over_sends, over_recvs = k.take(half * groups, half * groups)

    def onward(several, stage):
        for gather in several:
            gather.wait(stage)
            if stage + 1 < k.bits:
                gather.start(stage + 1)

    def out_onward(stage):
        for r, gather in enumerate(out_gathers):
            gather.wait(stage)
            if stage + 1 < k.bits:
                gather.start(stage + 1)
            for group in gather.arrivals(stage):
                block = out_block(group, k.c * half + r)
                at = r * groups + group
                k.send(None, block, block, over_sends + at, over_recvs + at, k.sibling)

    def send_out(q):
        part = pl.ds(q * 16, 16)
        exchanges[q].start(
            lambda rank: gate_up_out.at[rank, part], lambda rank: gate_up.at[k.d, rank, part]
        )

    def came_in(q):
        exchanges[q].finish(lambda rank: gate_up.at[k.d, rank, pl.ds(q * 16, 16)])
        for gather in gathers[q]:
            gather.start(0)
        if q + 2 < pieces:
            send_out(q + 2)

    gains_in = lambda rank: gains_all.at[k.d, rank]
    qkv_in = lambda rank: qkv.at[k.d, rank]
    k.barrier()
    gains_ex.start(lambda rank: gains, gains_in)
    qkv_ex.start(lambda rank: qkv_out.at[rank], qkv_in)
    for h, gather in enumerate(downs):
        gather.start(0, down_w.at[pl.ds(h * down_half, down_half)])
    own_down = k.move(down_w, down_all.at[k.d])
    gains_ex.finish(gains_in)
    qkv_ex.finish(qkv_in)
    out_line.start(out_w)
    x_line.start(tokens)
    own = [
        k.move(out_w, out_block(k.d, k.f)),
        k.move(tokens, x_all.at[pl.ds(pl.multiple_of(k.f * rows, 16), rows)]),
    ]
    for gather in late:
        gather.start(0)
    own_down()
    onward(downs, 0)
    for wait in own:
        wait()
    out_line.step(1)
    x_line.step(1)
    onward(late, 0)
    for reach in range(2, k.chips):
        out_line.step(reach)
    out_line.finish()
    for gather in out_gathers:
        gather.start(0)
    for q in range(min(2, pieces)):
        x_line.step(2 + q)
        send_out(q)
    for reach in range(2 + min(2, pieces), k.chips):
        x_line.step(reach)
    for stage in range(1, k.bits):
        onward(late, stage)
    out_onward(0)
    for stage in range(1, k.bits):
        onward(downs, stage)
    x_line.finish()
    members = 128 // slice_width
    for at in range(groups * ranks // members):
        group, first = at * members // ranks, at * members % ranks
        tile = gains_all[group, first].astype(F32)
        for other in range(1, members):
            tile = tile + gains_all[group, first + other].astype(F32)
        gain_rows[:, at * 128 : (at + 1) * 128] = tile[:8]

    events = []
    for q in range(pieces):
        events.append(lambda q=q: came_in(q))
        if q > 0:
            events.append(lambda q=q: onward(gathers[q - 1], 0))
    events.append(lambda: onward(gathers[pieces - 1], 0))
    if k.bits == 2:
        events.append(lambda: out_onward(1))
    plan = spaced(events, 2 * blocks)
    own = []
    for i in range(blocks):
        query = project_block(
            i, x_all, gain_rows, qkv, cosine, sine, normed, queries, keys, values, values_t
        )
        for event in plan[2 * i]:
            event()
        attend_block(i, rank_heads, query, keys, values_t, length, attended, log_totals)
        mine = attended.at[pl.ds(i * BLOCK, BLOCK)]
        lines[i].start(mine)
        own.append(k.move(mine, attended_block(i, k.f)))
        for reach in range(1, k.chips):
            if i - reach >= 0:
                lines[i - reach].step(reach)
        for event in plan[2 * i + 1]:
            event()
    for i in range(blocks, blocks + k.chips - 1):
        for reach in range(1, k.chips):
            if 0 <= i - reach < blocks:
                lines[i - reach].step(reach)
    for stage in range(1, k.bits):
        if k.bits > 2:
            out_onward(stage)
        for several in gathers:
            onward(several, stage)
    for r in range(half):
        for i in range(1, groups):
            group = lax.rem(k.d + i, groups)
            block = out_block(group, (1 - k.c) * half + r)
            k.arrived(None, block, over_recvs + r * groups + group)
    for wait in own:
        wait()
    for line in lines:
        line.finish()
    k.finish()


def feed_forward_kernel(
    groups, ranks, attended_all, x_all, grad_out, out_w, gate_up, down_w, gain,
    grad_out_all, hidden, normed, mixed, grad_gate_up, down_parts, parts,
    attended_in, x_in, grad_in, hidden_b, normed_b, mixed_b, grad_b, down_b, parts_b, local, sends, recvs,
):
    k = Links(groups, ranks, sends, recvs)
    chips, rows = k.chips, hidden_b.shape[0]
    width, units = out_w.shape[0], down_w.shape[0]
    line = LineGather(k, lambda rank: grad_out_all.at[rank])
    k.barrier()

    def chip(t):
        up = lax.rem(k.z + t, chips)
        down = lax.rem(k.z + chips - t, chips)
        return jnp.where(k.z < chips // 2, up, down)

    def span(t):
        return pl.ds(pl.multiple_of(chip(t) * rows, rows), rows)

    def loads(t):
        return [
            pltpu.make_async_copy(ref.at[span(t)], buffer.at[t % 2], local.at[2 * n + t % 2])
            for n, (ref, buffer) in enumerate(((attended_all, attended_in), (x_all, x_in)))
        ]

    results = ((hidden_b, hidden), (normed_b, normed), (mixed_b, mixed), (grad_b, grad_gate_up), (down_b, down_parts), (parts_b, parts))

    def store(t, n):
        buffer, ref = results[n]
        return pltpu.make_async_copy(buffer, ref.at[span(t)], local.at[4 + n])

    for load in loads(0):
        load.start()
    line.start(grad_out)
    own = k.move(grad_out, grad_out_all.at[k.f])
    own()
    step = 512
    for t in range(chips):
        if t + 1 < chips:
            for load in loads(t + 1):
                load.start()
        for load in loads(t):
            load.wait()
        if t > 0:
            store(t - 1, 0).wait()

        @pl.loop(0, width // step)
        def _(c):
            part = pl.ds(pl.multiple_of(c * step, step), step)
            hidden_b[:, part] = x_in[t % 2, :, part].astype(F32) + dot(
                attended_in[t % 2], out_w[:, part]
            )

        store(t, 0).start()
        if t > 0:
            store(t - 1, 1).wait()
            line.step(t)

        def normalise(part):
            total = hidden_b[part, :]
            normed_b[part, :] = (total * inverse_rms(total) * gain[...]).astype(BF16)

        row_loop(rows, normalise)
        store(t, 1).start()
        line.over(chip(t))
        place = chip(t) * 2
        fetch = [
            pltpu.make_async_copy(
                grad_out_all.at[place + c], grad_in.at[pl.ds(c * (rows // 2), rows // 2)], local.at[10 + c]
            )
            for c in range(2)
        ]
        for copy in fetch:
            copy.start()
        for copy in fetch:
            copy.wait()
        if t > 0:
            store(t - 1, 2).wait()
            store(t - 1, 3).wait()

        @pl.loop(0, units // BLOCK)
        def _(u):
            part = pl.ds(pl.multiple_of(u * BLOCK, BLOCK), BLOCK)
            far = pl.ds(pl.multiple_of(units + u * BLOCK, BLOCK), BLOCK)
            gate = dot(normed_b[...], gate_up[:, part])
            up = dot(normed_b[...], gate_up[:, far])
            grad_mixed = cols_inner(grad_in[...], down_w[part, :])
            sigmoid = 1.0 / (1.0 + jnp.exp(-gate))
            silu = gate * sigmoid
            mixed_b[:, part] = (silu * up).astype(BF16)
            grad_b[:, part] = (
                grad_mixed * up * (sigmoid * (1.0 + gate * (1.0 - sigmoid)))
            ).astype(BF16)
            grad_b[:, far] = (grad_mixed * silu).astype(BF16)

        store(t, 2).start()
        store(t, 3).start()
        if t > 0:
            store(t - 1, 4).wait()
            store(t - 1, 5).wait()

        @pl.loop(0, width // step)
        def _(c):
            part = pl.ds(pl.multiple_of(c * step, step), step)
            down_b[:, part] = dot(mixed_b[...], down_w[:, part]).astype(BF16)
            parts_b[:, part] = cols_inner(grad_b[...], gate_up[part, :]).astype(BF16)

        store(t, 4).start()
        store(t, 5).start()
    for n in range(len(results)):
        store(chips - 1, n).wait()
    k.finish()


def middle_kernel(
    groups, ranks, parts, down_parts, hidden_all, grad_out, gain, normed, grad_gate_up,
    grad_all, grad_hidden, output, sums, gate_up_sum,
    mine, held, landed, down_held, down_landed, rounded, hidden, tile, grad_w, gate_up_landed, local, sends, recvs,
):
    k = Links(groups, ranks, sends, recvs)
    rows = hidden.shape[0]
    depth = grad_w.shape[2]
    scatter = LineScatter(
        k,
        lambda rank: parts.at[rank],
        lambda chip: mine.at[chip],
        lambda chip: held.at[chip],
        lambda side, chip: landed.at[side, chip],
    )
    down_scatter = LineScatter(
        k,
        lambda rank: down_parts.at[rank],
        lambda chip: mine.at[chip],
        lambda chip: down_held.at[chip],
        lambda side, chip: down_landed.at[side, chip],
    )
    gather = LineGather(k, lambda rank: grad_all.at[rank])
    gate_up_sums = [
        GroupScatter(
            k,
            lambda group, n=n: grad_w.at[group, n],
            lambda i, n=n: gate_up_landed.at[n, i],
            n % 2 == 1,
        )
        for n in range(ranks)
    ]
    per_group = ranks * depth // BLOCK
    tiles = [(q, g) for q in range(per_group) for g in range(groups)]
    per_tile = BLOCK // depth

    def load(i):
        q, g = tiles[i]
        return pltpu.make_async_copy(
            normed.at[:, pl.ds((g * per_group + q) * BLOCK, BLOCK)], tile.at[i % 2], local.at[i % 2]
        )

    own_hidden = pltpu.make_async_copy(
        hidden_all.at[pl.ds(pl.multiple_of(k.f * rows, rows), rows)], hidden, local.at[2]
    )
    load(0).start()
    own_hidden.start()
    k.barrier()
    scatter.start()

    def weight_tile(i):
        q, g = tiles[i]
        if i + 1 < len(tiles):
            load(i + 1).start()
        load(i).wait()
        flipped = tile[i % 2].astype(F32).T.astype(BF16)
        step = 512

        @pl.loop(0, grad_gate_up.shape[1] // step)
        def _(c):
            part = pl.ds(pl.multiple_of(c * step, step), step)
            total = dot(flipped, grad_gate_up[:, part]).astype(BF16)
            for n in range(per_tile):
                grad_w[g, q * per_tile + n, :, part] = total[n * depth : (n + 1) * depth]

        if g == groups - 1:
            for n in range(per_tile):
                gate_up_sums[q * per_tile + n].start(0)

    weight_tile(0)
    scatter.pair()
    scatter.step(0)
    spots = spaced(list(range(1, len(tiles))), k.chips - 1)
    for i in range(k.chips - 1):
        for place in spots[i]:
            weight_tile(place)
        if i > 0:
            scatter.step(i)
    scatter.last()
    sums[...] = jnp.zeros_like(sums)
    own_hidden.wait()

    def rows_of(part):
        total = hidden[part]
        scale = inverse_rms(total)
        scaled = total * scale
        grad = held[k.z, part].astype(F32)
        sums[...] += jnp.sum(grad * scaled, 0, keepdims=True)
        grad_total = grad_out[part].astype(F32) + norm_back(grad * gain[...], scaled, scale)
        grad_hidden[part] = grad_total
        rounded[part] = grad_total.astype(BF16)

    row_loop(rows, rows_of)
    gather.start(rounded)
    down_scatter.start()
    own = k.move(rounded, grad_all.at[k.f])
    down_scatter.pair()
    for i in range(k.chips - 1):
        down_scatter.step(i)
        gather.step(i + 1)
        if i == 0:
            for sums_of in gate_up_sums:
                sums_of.wait(0)
                sums_of.start(1)
    down_scatter.last()

    def out_rows(part):
        output[part] = (hidden[part] + down_held[k.z, part].astype(F32)).astype(BF16)

    row_loop(rows, out_rows)
    for stage in range(1, k.bits):
        for n, sums_of in enumerate(gate_up_sums):
            if stage + 1 < k.bits:
                sums_of.wait(stage)
                sums_of.start(stage + 1)
            else:
                sums_of.wait(stage, gate_up_sum.at[n])
    gather.finish()
    own()
    k.finish()


def attend_back_kernel(
    groups, ranks, rank_heads, lengths, out_all, grad_hidden, queries, keys, values, attended, log_totals,
    cosine, sine, qkv, normed, gate_up_sum, grad_down,
    parts, grad_qkv_w, grad_out_w, gate_up_grad, down_grad,
    out_w, grad_qkv, keys_t, grad_keys, grad_values, down_landed, sends, recvs,
):
    k = Links(groups, ranks, sends, recvs)
    pieces = down_landed.shape[0]
    down_rows = down_grad.shape[0] // pieces
    down_sums = [
        GroupScatter(
            k,
            lambda group, n=n: grad_down.at[group, pl.ds(n * down_rows, down_rows)],
            lambda i, n=n: down_landed.at[n, i],
            n % 2 == 1,
        )
        for n in range(pieces)
    ]
    exchange = Exchange(k)
    gate_up_in = lambda rank: gate_up_grad.at[rank]
    length = lengths[0]
    cols = queries.shape[1]
    fetch = k.move(out_all.at[pl.ds(pl.multiple_of(k.f * cols, cols), cols)], out_w)
    k.barrier()
    exchange.start(lambda rank: gate_up_sum.at[rank], gate_up_in)
    for sums_of in down_sums:
        sums_of.start(0)
    blocks = keys_t.shape[0]
    grad_keys[...] = jnp.zeros_like(grad_keys)
    grad_values[...] = jnp.zeros_like(grad_values)

    fetch()

    @pl.loop(0, blocks)
    def _(i):
        block = pl.ds(pl.multiple_of(i * BLOCK, BLOCK), BLOCK)
        keys_t[i] = keys[block, :].astype(F32).T.astype(BF16)

    @pl.loop(0, blocks)
    def _(i):
        attend_back_rows(
            i, rank_heads, grad_hidden, out_w, queries, keys, keys_t, values, attended, length, log_totals,
            cosine, sine, grad_keys, grad_values, grad_qkv,
        )

    for stage in range(k.bits - 1):
        for sums_of in down_sums:
            sums_of.wait(stage)
            sums_of.start(stage + 1)

    @pl.loop(0, blocks)
    def _(i):
        finish_back_rows(i, qkv, cosine, sine, grad_keys, grad_values, grad_qkv, parts)

    @pl.loop(0, normed.shape[1] // BLOCK)
    def _(t):
        part = pl.ds(pl.multiple_of(t * BLOCK, BLOCK), BLOCK)
        grad_qkv_w[part, :] = rows_inner(normed[:, part], grad_qkv[...]).astype(BF16)
        grad_out_w[:, part] = rows_inner(attended[...], grad_hidden[:, part]).astype(BF16)

    for n, sums_of in enumerate(down_sums):
        sums_of.wait(k.bits - 1, down_grad.at[pl.ds(n * down_rows, down_rows)])
    exchange.finish(gate_up_in)
    k.finish()


def last_kernel(
    groups, ranks, slice_width, parts, tokens, grad_hidden, gain, sums_two, grad_qkv, grad_out_w,
    grad_tokens, qkv_grad, out_grad, gain_grads,
    mine, held, landed, sums, qkv_landed, out_landed, tiles, tiles_landed, tiles_sum, group_tiles, sends, recvs,
):
    k = Links(groups, ranks, sends, recvs)
    rows = tokens.shape[0]
    scatter = LineScatter(
        k, lambda rank: parts.at[rank], lambda chip: mine.at[chip], lambda chip: held.at[chip], lambda side, chip: landed.at[side, chip]
    )
    qkv_sums = [
        GroupScatter(
            k,
            lambda group, n=n: grad_qkv.at[group, n],
            lambda i, n=n: qkv_landed.at[n, i],
            n % 2 == 1,
        )
        for n in range(ranks)
    ]
    pieces = out_landed.shape[0]
    piece_rows = out_grad.shape[0] // pieces
    out_sums = [
        GroupScatter(
            k,
            lambda group, n=n: grad_out_w.at[group, pl.ds(n * piece_rows, piece_rows)],
            lambda i, n=n: out_landed.at[n, i],
            n % 2 == 1,
        )
        for n in range(pieces)
    ]
    exchange, tile_exchange = Exchange(k), Exchange(k)
    tile_sends, tile_recvs = k.take(groups, groups)
    qkv_in = lambda rank: qkv_grad.at[rank]
    k.barrier()
    scatter.start()
    for sums_of in qkv_sums:
        sums_of.start(0)
    for sums_of in out_sums:
        sums_of.start(0)
    scatter.pair()
    for i in range(k.chips - 1):
        scatter.step(i)
        if i == 0:
            for sums_of in qkv_sums:
                sums_of.wait(0)
                sums_of.start(1)
    for stage in range(1, k.bits - 1):
        for sums_of in qkv_sums:
            sums_of.wait(stage)
            sums_of.start(stage + 1)
    for n, sums_of in enumerate(qkv_sums):
        exchange.start_piece(n, sums_of.wait(k.bits - 1), qkv_in)
    scatter.last()
    sums[...] = jnp.zeros_like(sums)

    def rows_of(part):
        total = tokens[part].astype(F32)
        scale = inverse_rms(total)
        scaled = total * scale
        grad = held[k.z, part].astype(F32)
        sums[...] += jnp.sum(grad * scaled, 0, keepdims=True)
        grad_tokens[part] = (
            grad_hidden[part] + norm_back(grad * gain[...], scaled, scale)
        ).astype(BF16)

    row_loop(rows, rows_of)
    tiles[...] = jnp.zeros_like(tiles)
    for rank in range(ranks):
        for group in range(groups):
            at = (group * ranks + rank) * slice_width // 128 * 128
            tiles[rank, group, 0:1] = sums[:, at : at + 128]
            tiles[rank, group, 1:2] = sums_two[:, at : at + 128]
    tile_in = lambda rank: tiles_landed.at[rank]
    tile_exchange.start(lambda rank: tiles.at[rank], tile_in)
    for stage in range(k.bits - 1):
        for sums_of in out_sums:
            sums_of.wait(stage)
            sums_of.start(stage + 1)
    for n, sums_of in enumerate(out_sums):
        sums_of.wait(k.bits - 1, out_grad.at[pl.ds(n * piece_rows, piece_rows)])
    tile_exchange.finish(tile_in)
    total = tiles_landed[0]
    for rank in range(1, ranks):
        total = total + tiles_landed[rank]
    tiles_sum[...] = total
    for i in range(1, groups):
        other = lax.rem(k.d + i, groups)
        k.send(
            None,
            tiles_sum.at[other],
            group_tiles.at[k.d],
            tile_sends + other,
            tile_recvs + k.d,
            (other, k.f),
        )
    group_tiles[k.d] = tiles_sum[k.d]
    for i in range(1, groups):
        other = lax.rem(k.d + i, groups)
        k.arrived(None, group_tiles.at[other], tile_recvs + other)
    total = group_tiles[0]
    for group in range(1, groups):
        total = total + group_tiles[group]
    gain_grads[...] = total
    exchange.finish(qkv_in, own=False)
    k.finish()


VMEM = pl.BlockSpec(memory_space=pltpu.VMEM)
ANY = pl.BlockSpec(memory_space=pl.ANY)
SMEM = pl.BlockSpec(memory_space=pltpu.SMEM)


def call(kernel, identity, ins, outs, scratch, semaphores, args, local=0):
    return pl.pallas_call(
        kernel,
        out_shape=[jax.ShapeDtypeStruct(shape, kind) for shape, kind, _ in outs],
        in_specs=ins,
        out_specs=[place for _, _, place in outs],
        scratch_shapes=[pltpu.VMEM(shape, kind) for shape, kind in scratch]
        + [pltpu.SemaphoreType.DMA((local,))] * (local > 0)
        + [pltpu.SemaphoreType.DMA((semaphores,))] * 2,
        compiler_params=pltpu.CompilerParams(
            collective_id=identity, has_side_effects=True, vmem_limit_bytes=60 * 1024 * 1024
        ),
    )(*args)


def build(groups, ranks):
    def body(
        tokens, cotangent, lengths, norm_attn, w_query, w_key, w_value, w_output, norm_mlp, w_gate, w_up, w_down
    ):
        rows, width = tokens.shape
        depth = w_query.shape[0]
        count = rows * ranks
        rank_heads = HEADS // ranks
        hidden_part = w_down.shape[0]
        out_rows = w_output.shape[0]
        split = max(1, HEAD_DIM // out_rows)
        rank = lax.axis_index("fsdp")

        def heads_out(weight):
            shaped = weight.reshape(depth, split, rank_heads, ranks // split, HEAD_DIM)
            return shaped.transpose(3, 1, 0, 2, 4).reshape(ranks, depth, rank_heads * HEAD_DIM)

        def heads_in(pieces):
            shaped = pieces.reshape(ranks // split, split, depth, rank_heads, HEAD_DIM)
            return shaped.transpose(2, 1, 3, 0, 4).reshape(depth, HEADS * HEAD_DIM)

        def units_out(weight):
            shaped = weight.reshape(depth, groups, ranks, hidden_part)
            return shaped.transpose(2, 0, 1, 3).reshape(ranks, depth, groups * hidden_part)

        def units_in(pieces):
            shaped = pieces.reshape(ranks, depth, groups, hidden_part)
            return shaped.transpose(1, 2, 0, 3).reshape(depth, groups * ranks * hidden_part)

        span = [[base * split + i for i in range(split)] for base in range(ranks // split)]

        def place_output(grad):
            if split > 1:
                place = lax.rem(rank, split)
                grad = jnp.where(
                    (jnp.arange(split) == place)[:, None, None], grad[None], jnp.zeros((), BF16)
                )
            return grad.reshape(groups, -1, width)

        head_cols = rank_heads * HEAD_DIM
        unit_cols = groups * hidden_part
        chips = ranks // 2
        slice_width = norm_attn.shape[0]
        qkv_out = jnp.concatenate([heads_out(w) for w in (w_query, w_key, w_value)], -1)
        gate_up_out = jnp.concatenate([units_out(w) for w in (w_gate, w_up)], -1)
        place = (lax.axis_index("dp") * ranks + rank) * slice_width % 128
        gains = lax.dynamic_update_slice(
            jnp.zeros((16, 128), BF16), jnp.stack([norm_attn, norm_mlp]), (0, place)
        )
        cosine, sine = (jnp.asarray(table) for table in wide_tables(count))
        blocks = count // BLOCK
        heads_shape = ((count, head_cols), BF16, VMEM)
        (
            x_all, qkv, gain_rows, normed_one, queries, keys, values, attended, log_totals,
            attended_all, gate_up, out_all, down_w,
        ) = call(
            functools.partial(attend_kernel, groups, ranks, rank_heads, slice_width),
            5,
            [SMEM] + [VMEM] * 8,
            [
                ((count, width), BF16, VMEM),
                ((groups,) + qkv_out.shape, BF16, VMEM),
                ((8, width), F32, VMEM),
                ((count, width), BF16, VMEM),
            ]
            + [heads_shape] * 4
            + [
                ((blocks, rank_heads, BLOCK), F32, VMEM),
                ((count, width), BF16, ANY),
                ((groups,) + gate_up_out.shape, BF16, ANY),
                ((groups * ranks, out_rows, width), BF16, ANY),
                ((groups,) + w_down.shape, BF16, ANY),
            ],
            [
                ((groups, ranks, 16, 128), BF16),
                ((blocks, head_cols, BLOCK), BF16),
            ],
            448,
            (lengths, tokens, qkv_out, gains, w_output, w_down, gate_up_out, cosine, sine),
        )
        qkv = qkv.reshape(width, -1)
        gain_one, gain_two = gain_rows[0:1], gain_rows[1:2]
        gate_up = gate_up.reshape(width, -1)
        out_all = out_all.reshape(width, width)
        down_w = down_w.reshape(-1, width)
        own_places = rank * rows + jnp.arange(rows, dtype=jnp.int32)
        grad_out = jnp.where(own_places[:, None] < lengths[0], cotangent, jnp.zeros((), BF16))
        pair = 2 * rows
        grad_out_all, hidden, normed_two, mixed, grad_gate_up, down_parts, parts = call(
            functools.partial(feed_forward_kernel, groups, ranks),
            2,
            [ANY] * 2 + [VMEM] * 5,
            [
                ((ranks, rows, width), BF16, ANY),
                ((count, width), F32, ANY),
                ((count, width), BF16, ANY),
                ((count, unit_cols), BF16, ANY),
                ((count, 2 * unit_cols), BF16, ANY),
                ((count, width), BF16, ANY),
                ((count, width), BF16, ANY),
            ],
            [
                ((2, pair, width), BF16),
                ((2, pair, width), BF16),
                ((pair, width), BF16),
                ((pair, width), F32),
                ((pair, width), BF16),
                ((pair, unit_cols), BF16),
                ((pair, 2 * unit_cols), BF16),
                ((pair, width), BF16),
                ((pair, width), BF16),
            ],
            64,
            (attended_all, x_all, grad_out, out_all, gate_up, down_w, gain_two),
            local=12,
        )
        grad_down = rows_inner(mixed, grad_out_all.reshape(count, width)).astype(BF16)
        line_scratch = [((chips, rows, width), BF16), ((2, chips, rows, width), BF16)]
        grad_hidden_all, grad_hidden, output, sums_two, gate_up_sum = call(
            functools.partial(middle_kernel, groups, ranks),
            3,
            [ANY] * 3 + [VMEM] * 2 + [ANY, VMEM],
            [
                ((ranks, rows, width), BF16, ANY),
                ((rows, width), F32, VMEM),
                ((rows, width), BF16, VMEM),
                ((1, width), F32, VMEM),
                ((ranks, depth, 2 * unit_cols), BF16, VMEM),
            ],
            [((chips, rows, width), BF16)]
            + line_scratch * 2
            + [
                ((rows, width), BF16),
                ((rows, width), F32),
                ((2, count, BLOCK), BF16),
                ((groups, ranks, depth, 2 * unit_cols), BF16),
                ((ranks, groups - 1, depth, 2 * unit_cols), BF16),
            ],
            160,
            (
                parts.reshape(ranks, rows, width),
                down_parts.reshape(ranks, rows, width),
                hidden,
                grad_out,
                gain_two,
                normed_two,
                grad_gate_up,
            ),
            local=3,
        )
        pieces = 4
        parts, grad_qkv_w, grad_out_w, grad_gate_up_w, grad_w_down = call(
            functools.partial(attend_back_kernel, groups, ranks, rank_heads),
            6,
            [SMEM, ANY] + [VMEM] * 12,
            [
                ((count, width), BF16, VMEM),
                ((width, 3 * head_cols), BF16, VMEM),
                ((head_cols, width), BF16, VMEM),
                ((ranks, depth, 2 * unit_cols), BF16, ANY),
                ((hidden_part, width), F32, VMEM),
            ],
            [
                ((head_cols, width), BF16),
                ((count, 3 * head_cols), BF16),
                ((blocks, head_cols, BLOCK), BF16),
                ((count, head_cols), F32),
                ((count, head_cols), F32),
                ((pieces, groups - 1, hidden_part // pieces, width), BF16),
            ],
            160,
            (
                lengths,
                out_all,
                grad_hidden_all.reshape(count, width),
                queries,
                keys,
                values,
                attended,
                log_totals,
                cosine,
                sine,
                qkv,
                normed_one,
                gate_up_sum,
                grad_down.reshape(groups, hidden_part, width),
            ),
        )
        grad_out_w = place_output(grad_out_w)
        grad_w_gate = units_in(grad_gate_up_w[..., :unit_cols]).astype(F32)
        grad_w_up = units_in(grad_gate_up_w[..., unit_cols:]).astype(F32)
        parts = parts.reshape(ranks, rows, width)
        pieces = 2
        out_rows = grad_out_w.shape[1]
        tile = (8, 128)
        grad_tokens, grad_qkv_w, grad_w_output, sums = call(
            functools.partial(last_kernel, groups, ranks, slice_width),
            4,
            [ANY] + [VMEM] * 6,
            [
                ((rows, width), BF16, VMEM),
                ((ranks, depth, 3 * head_cols), BF16, ANY),
                ((out_rows, width), F32, VMEM),
                (tile, F32, VMEM),
            ],
            [((chips, rows, width), BF16)]
            + line_scratch
            + [
                ((1, width), F32),
                ((ranks, groups - 1, depth, 3 * head_cols), BF16),
                ((pieces, groups - 1, out_rows // pieces, width), BF16),
                ((ranks, groups) + tile, F32),
                ((ranks, groups) + tile, F32),
                ((groups,) + tile, F32),
                ((groups,) + tile, F32),
            ],
            160,
            (
                parts,
                tokens,
                grad_hidden,
                gain_one,
                sums_two,
                grad_qkv_w.reshape(groups, ranks, depth, 3 * head_cols),
                grad_out_w,
            ),
        )
        if split > 1:
            grad_w_output = lax.psum_scatter(
                grad_w_output, "fsdp", scatter_dimension=0, tiled=True, axis_index_groups=span
            )
        grad_w_query, grad_w_key, grad_w_value = (
            heads_in(grad_qkv_w[..., i * head_cols : (i + 1) * head_cols]).astype(F32) for i in range(3)
        )
        place = (lax.axis_index("dp") * ranks + rank) * slice_width % 128
        sums = lax.dynamic_slice_in_dim(sums, place, slice_width, 1)
        return (
            output,
            grad_tokens,
            sums[0],
            grad_w_query,
            grad_w_key,
            grad_w_value,
            grad_w_output,
            sums[1],
            grad_w_gate,
            grad_w_up,
            grad_w_down,
        )

    return body


def solution(mesh):
    both = P(("dp", "fsdp"))
    rows = P(("dp", "fsdp"), None)
    return jax.shard_map(
        build(mesh.shape["dp"], mesh.shape["fsdp"]),
        mesh=mesh,
        in_specs=(rows, rows, P("dp"), both, rows, rows, rows, rows, both, rows, rows, rows),
        out_specs=(rows, rows, both, rows, rows, rows, rows, both, rows, rows, rows),
        check_vma=False,
    )
```

```python
import functools

import jax
import jax.numpy as jnp
import numpy as np
from jax import lax
from jax.experimental import pallas as pl
from jax.experimental.pallas import tpu as pltpu
from jax.sharding import PartitionSpec as P

HEADS = 32
HEAD_DIM = 64


EPSILON = 1e-05
THETA = 130000.0
BF16 = jnp.bfloat16
F32 = jnp.float32


def dot(left, right):
    return jnp.dot(left, right, preferred_element_type=F32)


def rows_inner(left, right):
    return lax.dot_general(left, right, (((0,), (0,)), ((), ())), preferred_element_type=F32)


def cols_inner(left, right):
    return lax.dot_general(left, right, (((1,), (1,)), ((), ())), preferred_element_type=F32)


def inverse_rms(values):
    return lax.rsqrt(jnp.mean(values * values, -1, keepdims=True) + EPSILON)


def norm_back(grad_scaled, scaled, scale):
    return scale * (grad_scaled - scaled * jnp.mean(grad_scaled * scaled, -1, keepdims=True))


BLOCK = 256
SCALE = 0.125


def turn_halves(values, cosine, sine):
    width = values.shape[1]
    half = HEAD_DIM // 2
    lane = lax.broadcasted_iota(jnp.int32, values.shape, 1)
    ahead = pltpu.roll(values, width - half, 1)
    behind = pltpu.roll(values, half, 1)
    return values * cosine + jnp.where(lane % HEAD_DIM < half, ahead, behind) * sine


def wide_tables(count):
    half = HEAD_DIM // 2
    inverse = np.float32(THETA) ** (-np.arange(half, dtype=np.float32) * np.float32(2.0) / HEAD_DIM)
    angles = np.arange(count, dtype=np.float32)[:, None] * inverse.astype(np.float32)[None, :]
    cosine, sine = np.cos(angles).astype(np.float32), np.sin(angles).astype(np.float32)
    return np.concatenate([cosine] * 4, -1), np.concatenate([-sine, sine] * 2, -1)


def table_rows(table, block, width):
    return jnp.concatenate([table[block, :]] * (width // 128), 1)


def key_bias(j, length):
    place = j * BLOCK + lax.broadcasted_iota(jnp.int32, (BLOCK, 1), 0)
    return jnp.where(place < length, 0.0, -1000000000.0)


def head_rows(values, head):
    row = lax.broadcasted_iota(jnp.int32, values.shape, 0)
    return jnp.where((row >= head * HEAD_DIM) & (row < (head + 1) * HEAD_DIM), values, 0.0)


def future(shape):
    return lax.broadcasted_iota(jnp.int32, shape, 0) > lax.broadcasted_iota(jnp.int32, shape, 1)


def attend_block(i, rank_heads, queries, keys, values_t, length, attended, log_totals):
    queries_t = queries.T
    masked = [(head_rows(queries_t, h) * SCALE).astype(BF16) for h in range(rank_heads)]

    def chunk(j, carry, last):
        part = pl.ds(pl.multiple_of(j * BLOCK, BLOCK), BLOCK)
        key_part, bias_part = keys[part, :], key_bias(j, length)
        after = []
        for h in range(rank_heads):
            top, total, out = carry[h]
            scores = dot(key_part, masked[h]) + bias_part
            if last:
                scores = jnp.where(future(scores.shape), -1000000000.0, scores)
            new_top = jnp.maximum(top, jnp.max(scores, 0, keepdims=True))
            keep = jnp.exp(top - new_top)
            weights = jnp.exp(scores - new_top)
            total = total * keep + jnp.sum(weights, 0, keepdims=True)
            out = out * keep + dot(
                values_t[j, h * HEAD_DIM : (h + 1) * HEAD_DIM, :], weights.astype(BF16)
            )
            after.append((new_top, total, out))
        return tuple(after)

    carry = tuple(
        (
            jnp.full((1, BLOCK), -3.0e38, F32),
            jnp.zeros((1, BLOCK), F32),
            jnp.zeros((HEAD_DIM, BLOCK), F32),
        )
        for _ in range(rank_heads)
    )
    carry = lax.fori_loop(0, i, lambda j, c: chunk(j, c, False), carry)
    carry = chunk(i, carry, True)
    outs = []
    for h, (top, total, out) in enumerate(carry):
        log_totals[i, h : h + 1, :] = top + jnp.log(total)
        outs.append(out * (1.0 / total))
    attended[pl.ds(pl.multiple_of(i * BLOCK, BLOCK), BLOCK), :] = (
        jnp.concatenate(outs, 0).T.astype(BF16)
    )


def project_block(i, x, gain, qkv, cosine, sine, normed, queries, keys, values, values_t):
    cols = queries.shape[1]
    start = i * BLOCK

    def rows_of(part):
        rows = x[part, :].astype(F32)
        normed[part, :] = (rows * inverse_rms(rows) * gain[0:1, :]).astype(BF16)

    pl.loop(0, BLOCK // 16)(
        lambda t: rows_of(pl.ds(pl.multiple_of(start + t * 16, 16), 16))
    )
    block = pl.ds(pl.multiple_of(start, BLOCK), BLOCK)
    rows = normed[block, :]

    def weight(n):
        return qkv[:, :, :, n * cols : (n + 1) * cols].reshape(x.shape[1], cols)

    cos, sin = table_rows(cosine, block, cols), table_rows(sine, block, cols)
    rounded = turn_halves(dot(rows, weight(0)), cos, sin).astype(BF16)
    queries[block, :] = rounded
    keys[block, :] = turn_halves(dot(rows, weight(1)), cos, sin).astype(BF16)
    value = dot(rows, weight(2))
    values[block, :] = value.astype(BF16)
    values_t[i] = value.T.astype(BF16)
    return rounded.astype(F32)


def lanes_of(values, head):
    lane = lax.broadcasted_iota(jnp.int32, values.shape, 1)
    return jnp.where((lane >= head * HEAD_DIM) & (lane < (head + 1) * HEAD_DIM), values, 0.0)


def attend_back_block(
    i, rank_heads, queries, keys, keys_t, values, attended, grad, length, log_totals, grad_keys, grad_values
):
    block = pl.ds(pl.multiple_of(i * BLOCK, BLOCK), BLOCK)
    query = queries[block, :].astype(F32) * SCALE
    query_t, grad_t = query.T, grad.T
    product = attended[block, :].astype(F32).T * grad_t
    masked_q = [head_rows(query_t, h).astype(BF16) for h in range(rank_heads)]
    masked_g = [head_rows(grad_t, h).astype(BF16) for h in range(rank_heads)]
    stacked_q = jnp.concatenate([lanes_of(query, h).astype(BF16) for h in range(rank_heads)], 0)
    stacked_g = jnp.concatenate([lanes_of(grad, h).astype(BF16) for h in range(rank_heads)], 0)
    deltas = [
        jnp.sum(product[h * HEAD_DIM : (h + 1) * HEAD_DIM], 0, keepdims=True)
        for h in range(rank_heads)
    ]
    totals = [log_totals[i, h : h + 1, :] for h in range(rank_heads)]

    def chunk(j, carry, last):
        part = pl.ds(pl.multiple_of(j * BLOCK, BLOCK), BLOCK)
        key_part, value_part, bias_part = keys[part, :], values[part, :], key_bias(j, length)
        after, weights_all, grads_all = [], [], []
        for h in range(rank_heads):
            scores = dot(key_part, masked_q[h]) + bias_part
            if last:
                scores = jnp.where(future(scores.shape), -1000000000.0, scores)
            weights = jnp.exp(scores - totals[h])
            grad_scores = weights * (dot(value_part, masked_g[h]) - deltas[h])
            weights_all.append(weights.astype(BF16))
            grads_all.append(grad_scores.astype(BF16))
            after.append(
                carry[h] + dot(keys_t[j, h * HEAD_DIM : (h + 1) * HEAD_DIM, :], grads_all[-1])
            )
        grad_values[part, :] += dot(jnp.concatenate(weights_all, 1), stacked_g)
        grad_keys[part, :] += dot(jnp.concatenate(grads_all, 1), stacked_q)
        return tuple(after)

    carry = tuple(jnp.zeros((HEAD_DIM, BLOCK), F32) for _ in range(rank_heads))
    carry = lax.fori_loop(0, i, lambda j, c: chunk(j, c, False), carry)
    carry = chunk(i, carry, True)
    return jnp.concatenate(carry, 0).T * SCALE


def attend_back_rows(
    i, rank_heads, grad_hidden, out_w, queries, keys, keys_t, values, attended, length, log_totals,
    cosine, sine, grad_keys, grad_values, grad_qkv,
):
    block = pl.ds(pl.multiple_of(i * BLOCK, BLOCK), BLOCK)
    cols = queries.shape[1]
    grad = cols_inner(grad_hidden[block, :], out_w[...]).astype(BF16).astype(F32)
    grad_q = attend_back_block(
        i, rank_heads, queries, keys, keys_t, values, attended, grad, length, log_totals, grad_keys, grad_values
    )
    grad_qkv[block, :cols] = turn_halves(
        grad_q, table_rows(cosine, block, cols), -table_rows(sine, block, cols)
    ).astype(BF16)


def finish_back_rows(i, cosine, sine, grad_keys, grad_values, grad_qkv):
    block = pl.ds(pl.multiple_of(i * BLOCK, BLOCK), BLOCK)
    cols = grad_keys.shape[1]
    grad_qkv[block, cols : 2 * cols] = turn_halves(
        grad_keys[block, :], table_rows(cosine, block, cols), -table_rows(sine, block, cols)
    ).astype(BF16)
    grad_qkv[block, 2 * cols :] = grad_values[block, :].astype(BF16)


MESH = pl.DeviceIdType.MESH


def when(cond, action):
    if cond is None:
        action()
    else:
        pl.when(cond)(action)


class Links:
    def __init__(self, groups, ranks, sends, recvs):
        self.groups, self.ranks, self.chips = groups, ranks, ranks // 2
        self.bits = groups.bit_length() - 1
        self.sends, self.recvs = sends, recvs
        self.used_sends = self.used_recvs = 0
        self.d, self.f = lax.axis_index("dp"), lax.axis_index("fsdp")
        self.z, self.c = lax.div(self.f, 2), lax.rem(self.f, 2)
        self.sibling = (self.d, self.z * 2 + 1 - self.c)
        self.pending = []

    def bit(self, b):
        return lax.rem(lax.div(self.d, 1 << b), 2)

    def partner(self, b):
        return (self.d + (1 - 2 * self.bit(b)) * (1 << b), self.f)

    def beside(self, way):
        return (self.d, self.f + 2 * way)

    def barrier(self):
        gate = pltpu.get_barrier_semaphore()
        for k in range(1, self.ranks):
            other = lax.rem(self.f + k, self.ranks)
            pl.semaphore_signal(gate, inc=1, device_id=(self.d, other), device_id_type=MESH)
        for k in range(1, self.groups):
            other = lax.rem(self.d + k, self.groups)
            pl.semaphore_signal(gate, inc=1, device_id=(other, self.f), device_id_type=MESH)
        pl.semaphore_wait(gate, self.ranks + self.groups - 2)

    def take(self, sends, recvs):
        first = (self.used_sends, self.used_recvs)
        self.used_sends += sends
        self.used_recvs += recvs
        return first

    def copy(self, source, target, send, recv, device):
        return pltpu.make_async_remote_copy(
            src_ref=source,
            dst_ref=target,
            send_sem=self.sends.at[send],
            recv_sem=self.recvs.at[recv],
            device_id=device,
            device_id_type=MESH,
        )

    def send(self, cond, source, target, send, recv, device, later=True):
        when(cond, lambda: self.copy(source, target, send, recv, device).start())
        gone = lambda: when(
            cond, lambda: self.copy(source, target, send, recv, device).wait_send()
        )
        if later:
            self.pending.append(gone)
        return gone

    def arrived(self, cond, target, recv):
        when(cond, lambda: self.copy(target, target, 0, recv, self.sibling).wait_recv())

    def move(self, source, target):
        send, _ = self.take(1, 0)
        make = lambda: pltpu.make_async_copy(source, target, self.sends.at[send])
        make().start()
        return lambda: make().wait()

    def finish(self):
        for wait in self.pending:
            wait()
        self.pending = []


class LineGather:
    def __init__(self, links, view):
        self.links, self.view = links, view
        chips = links.chips
        self.sends, self.recvs = links.take(3 * chips, 3 * chips)

    def start(self, source):
        k, chips = self.links, self.links.chips
        target = self.view(k.f)
        for side, way in enumerate((1, -1)):
            valid = (k.z + way >= 0) & (k.z + way < chips)
            k.send(
                valid, source, target, self.sends + side * chips, self.recvs + side * chips + 1, k.beside(way)
            )
        k.send(
            None, source, target, self.sends + 2 * chips + k.z, self.recvs + 2 * chips + k.z, k.sibling
        )

    def step(self, reach):
        k, chips = self.links, self.links.chips
        for side, way in enumerate((1, -1)):
            origin = k.z - way * reach
            here = (origin >= 0) & (origin < chips)
            block = self.view(origin * 2 + k.c)
            k.arrived(here, block, self.recvs + side * chips + reach)
            if reach + 1 < chips:
                onward = here & (k.z + way >= 0) & (k.z + way < chips)
                k.send(
                    onward,
                    block,
                    block,
                    self.sends + side * chips + reach,
                    self.recvs + side * chips + reach + 1,
                    k.beside(way),
                )
            k.send(
                here,
                block,
                block,
                self.sends + 2 * chips + origin,
                self.recvs + 2 * chips + origin,
                k.sibling,
            )

    def over(self, chip):
        k = self.links
        k.arrived(None, self.view(chip * 2 + 1 - k.c), self.recvs + 2 * k.chips + chip)

    def finish(self):
        k, chips = self.links, self.links.chips
        for chip in range(chips):
            k.arrived(None, self.view(chip * 2 + 1 - k.c), self.recvs + 2 * chips + chip)


def add_rows(target, *sources, step=16):
    rows = target.shape[0]

    @pl.loop(0, rows // step)
    def _(i):
        part = pl.ds(pl.multiple_of(i * step, step), step)
        total = sources[0][part].astype(F32)
        for source in sources[1:]:
            total = total + source[part].astype(F32)
        target[part] = total.astype(target.dtype)


class LineScatter:
    def __init__(self, links, mine, held, landed):
        self.links, self.mine, self.held, self.landed = links, mine, held, landed
        chips = links.chips
        self.sends, self.recvs = links.take(2 * chips, 3 * chips)
        self.gone = [lambda: None] * 2
        self.own = {}

    def give(self, chip, other, later=True):
        k = self.links
        return k.send(
            None, other, self.held(chip), self.sends + chip, self.recvs + chip, k.sibling, later=later
        )

    def start(self, parts):
        k = self.links
        for chip in range(k.chips):
            self.give(chip, parts(chip * 2 + 1 - k.c))
            self.own[chip] = k.move(parts(chip * 2 + k.c), self.mine(chip))

    def pair(self, chip, mine=None):
        k = self.links
        k.arrived(None, self.held(chip), self.recvs + chip)
        add_rows(self.held(chip), self.held(chip), self.mine(chip) if mine is None else mine)

    def pairs(self):
        for chip in range(self.links.chips):
            self.own[chip]()
            self.pair(chip)

    def place(self, side, chip, at):
        return self.landed(chip if side == 0 else jnp.where(chip == at, self.links.chips, chip))

    def onward(self, side, way, chip, before):
        k, chips = self.links, self.links.chips
        inner = before & (k.z > 0 if way > 0 else k.z < chips - 1)
        arrival = self.recvs + (1 + side) * chips + chip

        def add():
            k.arrived(None, self.place(side, chip, k.z), arrival)
            add_rows(self.held(chip), self.held(chip), self.place(side, chip, k.z))

        pl.when(inner)(add)
        return k.send(
            before,
            self.held(chip),
            self.place(side, chip, k.z + way),
            self.sends + chips + chip,
            arrival,
            k.beside(way),
        )

    def step(self, i):
        k, chips = self.links, self.links.chips
        for side, way in enumerate((1, -1)):
            chip = k.z + way * (chips - 1 - i)
            self.onward(side, way, chip, (chip >= 0) & (chip < chips))

    def toward(self, chip):
        k = self.links
        for side, way in enumerate((1, -1)):
            self.onward(side, way, chip, chip > k.z if way > 0 else chip < k.z)

    def last(self):
        k, chips = self.links, self.links.chips
        for side, inner in enumerate((k.z > 0, k.z < chips - 1)):

            def add():
                block = self.place(side, k.z, k.z)
                k.arrived(None, block, self.recvs + (1 + side) * chips + k.z)
                add_rows(self.held(k.z), self.held(k.z), block)

            pl.when(inner)(add)


class Exchange:
    def __init__(self, links):
        self.links = links
        self.sends, self.recvs = links.take(links.ranks, links.ranks)

    def start(self, source, target):
        k = self.links
        self.own = k.move(source(k.f), target(k.f))
        for i in range(1, k.ranks):
            other = lax.rem(k.f + i, k.ranks)
            k.send(
                None, source(other), target(k.f), self.sends + other, self.recvs + k.f, (k.d, other)
            )

    def finish(self, target, own=True):
        k = self.links
        if own:
            self.own()
        for i in range(1, k.ranks):
            other = lax.rem(k.f + i, k.ranks)
            k.arrived(None, target(other), self.recvs + other)

    def start_piece(self, rank, source, target):
        k = self.links
        k.send(
            k.f != rank, source, target(k.f), self.sends + rank, self.recvs + k.f, (k.d, rank)
        )
        here = lambda: pltpu.make_async_copy(source, target(k.f), k.sends.at[self.sends + rank])
        pl.when(k.f == rank)(lambda: here().start())
        k.pending.append(lambda: pl.when(k.f == rank)(lambda: here().wait()))


class GroupGather:
    def __init__(self, links, view, high):
        self.links, self.view, self.high = links, view, high
        count = links.groups - 1
        self.sends, self.recvs = links.take(count, count)

    def flip(self, stage):
        k = self.links
        low, up = 1 << stage, 1 << (k.bits - 1 - stage)
        size = low + self.high * (up - low)
        return (1 - 2 * lax.rem(lax.div(k.d, size), 2)) * size

    def places(self, stage):
        places = [self.links.d]
        for past in range(stage):
            places = places + [place + self.flip(past) for place in places]
        return places

    def start(self, stage, source=None):
        k = self.links
        for i, place in enumerate(self.places(stage)):
            at = (1 << stage) - 1 + i
            target = self.view(place)
            k.send(
                None,
                target if source is None else source,
                target,
                self.sends + at,
                self.recvs + at,
                (k.d + self.flip(stage), k.f),
            )

    def arrivals(self, stage):
        return [place + self.flip(stage) for place in self.places(stage)]

    def wait(self, stage):
        for i, place in enumerate(self.arrivals(stage)):
            self.links.arrived(None, self.view(place), self.recvs + (1 << stage) - 1 + i)


class GroupScatter:
    def __init__(self, links, view, landed, high):
        self.links, self.view, self.landed = links, view, landed
        bits = list(range(links.bits))
        self.order = bits[::-1] if high else bits
        count = links.groups - 1
        self.sends, self.recvs = links.take(count, count)

    def base(self, stage):
        return sum(self.links.groups >> (s + 1) for s in range(stage))

    def sources(self, stage, flip):
        k = self.links
        b = self.order[stage]
        value = 1 - k.bit(b) if flip else k.bit(b)
        if stage > 0:
            count = k.groups >> (stage + 1)
            return [self.landed(self.base(stage - 1) + value + 2 * i) for i in range(count)]
        places = [value * (1 << b)]
        for b in self.order[1:]:
            places = places + [place + (1 << b) for place in places]
        return [self.view(place) for place in places]

    def start(self, stage):
        k = self.links
        for i, source in enumerate(self.sources(stage, True)):
            at = self.base(stage) + i
            k.send(
                None,
                source,
                self.landed(at),
                self.sends + at,
                self.recvs + at,
                k.partner(self.order[stage]),
            )

    def wait(self, stage, target=None):
        k = self.links
        for i, source in enumerate(self.sources(stage, False)):
            at = self.base(stage) + i
            k.arrived(None, self.landed(at), self.recvs + at)
            add_rows(self.landed(at) if target is None else target, source, self.landed(at))
        return self.landed(self.base(stage))


def row_loop(rows, action, step=16, first=0):
    @pl.loop(0, rows // step)
    def _(i):
        action(pl.ds(pl.multiple_of(first + i * step, step), step))


def spaced(events, blocks):
    count = len(events)
    return [events[b * count // blocks : (b + 1) * count // blocks] for b in range(blocks)]


def attend_kernel(
    groups, ranks, rank_heads, slice_width,
    lengths, tokens, qkv_out, gains, out_w, down_w, gate_up_out, cosine, sine,
    x_all, qkv, gain_rows, normed, queries, keys, values, attended, log_totals,
    attended_all, gate_up, out_all, down_all,
    gains_all, values_t, sends, recvs,
):
    k = Links(groups, ranks, sends, recvs)
    length = lengths[0]
    cols, rows = queries.shape[1], tokens.shape[0]
    depth, half = gate_up_out.shape[1], ranks // 2
    pieces = depth // 16
    blocks = values_t.shape[0]
    split = max(1, HEAD_DIM // out_w.shape[0])
    down_half = down_w.shape[0] // 2

    def unit(group, rank):
        return (
            (lax.div(rank, split) * split + lax.div(group, rank_heads)) * rank_heads
            + lax.rem(group, rank_heads)
        ) * split + lax.rem(rank, split)

    def out_block(group, rank):
        return out_all.at[unit(group, rank)]

    def attended_block(i, rank):
        return attended_all.at[
            pl.ds(i * BLOCK, BLOCK), pl.ds(pl.multiple_of(rank * cols, cols), cols)
        ]

    x_line = LineGather(k, lambda rank: x_all.at[pl.ds(pl.multiple_of(rank * rows, 16), rows)])
    out_line = LineGather(k, lambda rank: out_block(k.d, rank))
    lines = [LineGather(k, lambda rank, i=i: attended_block(i, rank)) for i in range(blocks)]
    gains_ex, qkv_ex = Exchange(k), Exchange(k)
    exchanges = [Exchange(k) for _ in range(pieces)]
    downs = [
        GroupGather(k, lambda group, h=h: down_all.at[group, pl.ds(h * down_half, down_half)], h)
        for h in range(2)
    ]
    late = [
        GroupGather(k, lambda group, h=h, ref=ref: ref.at[group, pl.ds(h * half, half)], h)
        for ref in (qkv, gains_all)
        for h in range(2)
    ]
    out_gathers = [
        GroupGather(k, lambda group, r=r: out_block(group, k.c * half + r), k.c) for r in range(half)
    ]
    gathers = [
        [
            GroupGather(
                k,
                lambda group, h=h, q=q: gate_up.at[group, pl.ds(h * half, half), pl.ds(q * 16, 16)],
                h,
            )
            for h in range(2)
        ]
        for q in range(pieces)
    ]
    over_sends, over_recvs = k.take(half * groups, half * groups)

    def onward(several, stage):
        for gather in several:
            gather.wait(stage)
            if stage + 1 < k.bits:
                gather.start(stage + 1)

    def out_onward(stage):
        for r, gather in enumerate(out_gathers):
            gather.wait(stage)
            if stage + 1 < k.bits:
                gather.start(stage + 1)
            for group in gather.arrivals(stage):
                block = out_block(group, k.c * half + r)
                at = r * groups + group
                k.send(None, block, block, over_sends + at, over_recvs + at, k.sibling)

    def send_out(q):
        part = pl.ds(q * 16, 16)
        exchanges[q].start(
            lambda rank: gate_up_out.at[rank, part], lambda rank: gate_up.at[k.d, rank, part]
        )

    def came_in(q):
        exchanges[q].finish(lambda rank: gate_up.at[k.d, rank, pl.ds(q * 16, 16)])
        for gather in gathers[q]:
            gather.start(0)
        if q + 2 < pieces:
            send_out(q + 2)

    gains_in = lambda rank: gains_all.at[k.d, rank]
    qkv_in = lambda rank: qkv.at[k.d, rank]
    k.barrier()
    gains_ex.start(lambda rank: gains, gains_in)
    qkv_ex.start(lambda rank: qkv_out.at[rank], qkv_in)
    for h, gather in enumerate(downs):
        gather.start(0, down_w.at[pl.ds(h * down_half, down_half)])
    own_down = k.move(down_w, down_all.at[k.d])
    gains_ex.finish(gains_in)
    qkv_ex.finish(qkv_in)
    out_line.start(out_w)
    x_line.start(tokens)
    own = [
        k.move(out_w, out_block(k.d, k.f)),
        k.move(tokens, x_all.at[pl.ds(pl.multiple_of(k.f * rows, 16), rows)]),
    ]
    for gather in late:
        gather.start(0)
    own_down()
    onward(downs, 0)
    for wait in own:
        wait()
    out_line.step(1)
    x_line.step(1)
    onward(late, 0)
    for reach in range(2, k.chips):
        out_line.step(reach)
    out_line.finish()
    for gather in out_gathers:
        gather.start(0)
    for q in range(min(2, pieces)):
        x_line.step(2 + q)
        send_out(q)
    for reach in range(2 + min(2, pieces), k.chips):
        x_line.step(reach)
    for stage in range(1, k.bits):
        onward(late, stage)
    out_onward(0)
    for stage in range(1, k.bits):
        onward(downs, stage)
    x_line.finish()
    members = 128 // slice_width
    for at in range(groups * ranks // members):
        group, first = at * members // ranks, at * members % ranks
        tile = gains_all[group, first].astype(F32)
        for other in range(1, members):
            tile = tile + gains_all[group, first + other].astype(F32)
        gain_rows[:, at * 128 : (at + 1) * 128] = tile[:8]

    events = []
    for q in range(pieces):
        events.append(lambda q=q: came_in(q))
        if q > 0:
            events.append(lambda q=q: onward(gathers[q - 1], 0))
    events.append(lambda: onward(gathers[pieces - 1], 0))
    if k.bits == 2:
        events.append(lambda: out_onward(1))
    plan = spaced(events, 2 * blocks)
    own = []
    for i in range(blocks):
        query = project_block(
            i, x_all, gain_rows, qkv, cosine, sine, normed, queries, keys, values, values_t
        )
        for event in plan[2 * i]:
            event()
        attend_block(i, rank_heads, query, keys, values_t, length, attended, log_totals)
        mine = attended.at[pl.ds(i * BLOCK, BLOCK)]
        lines[i].start(mine)
        own.append(k.move(mine, attended_block(i, k.f)))
        for reach in range(1, k.chips):
            if i - reach >= 0:
                lines[i - reach].step(reach)
        for event in plan[2 * i + 1]:
            event()
    for i in range(blocks, blocks + k.chips - 1):
        for reach in range(1, k.chips):
            if 0 <= i - reach < blocks:
                lines[i - reach].step(reach)
    for stage in range(1, k.bits):
        if k.bits > 2:
            out_onward(stage)
        for several in gathers:
            onward(several, stage)
    for r in range(half):
        for i in range(1, groups):
            group = lax.rem(k.d + i, groups)
            block = out_block(group, (1 - k.c) * half + r)
            k.arrived(None, block, over_recvs + r * groups + group)
    for wait in own:
        wait()
    for line in lines:
        line.finish()
    k.finish()


def far_first(k, t):
    total = 0
    for z in range(k.chips):
        order = sorted(range(k.chips), key=lambda chip: -abs(chip - z))
        total = total + jnp.where(k.z == z, order[t], 0)
    return total


def feed_forward_kernel(
    groups, ranks, attended_all, x_all, out_all, gate_up_all, down_all, grad_out, gain,
    grad_out_all, hidden, output, normed, mixed, grad_gate_up, parts,
    out_w, gate_up, down_w, attended_in, x_in, grad_in, hidden_b, normed_b, gates, mixed_b, grad_b, down_b, parts_b,
    held, landed, local, sends, recvs,
):
    k = Links(groups, ranks, sends, recvs)
    chips, pair = k.chips, hidden_b.shape[0]
    rows = pair // 2
    width, units = out_w.shape[0], down_w.shape[0]
    step = 512
    line = LineGather(k, lambda rank: grad_out_all.at[rank])
    scatter = LineScatter(
        k, None, lambda chip: held.at[chip], lambda slot: landed.at[slot]
    )
    weights = [
        pltpu.make_async_copy(ref, buffer, local.at[n])
        for n, (ref, buffer) in enumerate(((out_all, out_w), (gate_up_all, gate_up), (down_all, down_w)))
    ]
    order = [far_first(k, t) for t in range(chips)]

    def span(t):
        return pl.ds(pl.multiple_of(order[t] * pair, 16), pair)

    def loads(t):
        return [
            pltpu.make_async_copy(ref.at[span(t)], buffer.at[t % 2], local.at[3 + 2 * n + t % 2])
            for n, (ref, buffer) in enumerate(((attended_all, attended_in), (x_all, x_in)))
        ]

    def fetches(t):
        return [
            pltpu.make_async_copy(
                grad_out_all.at[order[t] * 2 + c],
                grad_in.at[t % 2, pl.ds(c * rows, rows)],
                local.at[7 + 2 * (t % 2) + c],
            )
            for c in range(2)
        ]

    def store(n, buffer, ref, t):
        return pltpu.make_async_copy(buffer, ref.at[span(t)], local.at[11 + n])

    for load in loads(0) + weights:
        load.start()
    k.barrier()
    line.start(grad_out)
    own = k.move(grad_out, grad_out_all.at[k.f])
    weights[0].wait()
    gone = None
    for t in range(chips):
        if t + 1 < chips:
            for load in loads(t + 1):
                load.start()
        for load in loads(t):
            load.wait()

        @pl.loop(0, width // step)
        def _(c):
            part = pl.ds(pl.multiple_of(c * step, step), step)
            hidden_b[:, part] = x_in[t % 2, :, part].astype(F32) + dot(
                attended_in[t % 2], out_w[:, part]
            )

        if t > 0:
            store(0, normed_b, normed, t - 1).wait()

        def normalise(part):
            total = hidden_b[part, :]
            normed_b[part, :] = (total * inverse_rms(total) * gain[...]).astype(BF16)

        row_loop(pair, normalise)
        store(0, normed_b, normed, t).start()
        if t == 0:
            weights[1].wait()
        if t == chips - 1:

            @pl.loop(0, rows // 16)
            def _(i):
                source = pl.ds(pl.multiple_of(k.c * rows + i * 16, 16), 16)
                hidden[pl.ds(pl.multiple_of(i * 16, 16), 16), :] = hidden_b[source, :]

        if t > 0:
            store(1, mixed_b, mixed, t - 1).wait()
            line.step(t)
        here = span(t)

        @pl.loop(0, units // BLOCK)
        def _(u):
            part = pl.ds(pl.multiple_of(u * BLOCK, BLOCK), BLOCK)
            far = pl.ds(pl.multiple_of(units + u * BLOCK, BLOCK), BLOCK)
            gate = dot(normed_b[...], gate_up[:, part])
            up = dot(normed_b[...], gate_up[:, far])
            gates[here, part] = gate
            gates[here, far] = up
            mixed_b[:, part] = (gate / (1.0 + jnp.exp(-gate)) * up).astype(BF16)

        store(1, mixed_b, mixed, t).start()
        if t == 0:
            weights[2].wait()
        else:
            gone()

        @pl.loop(0, width // step)
        def _(c):
            part = pl.ds(pl.multiple_of(c * step, step), step)
            down_b[:, part] = dot(mixed_b[...], down_w[:, part]).astype(BF16)

        def core_rows(core):
            return down_b.at[pl.ds(pl.multiple_of(core * rows, 16), rows)]

        gone = scatter.give(order[t], core_rows(1 - k.c), later=False)
        scatter.pair(order[t], core_rows(k.c))
        if t % 2 == 1:
            scatter.step(t // 2)
    store(0, normed_b, normed, chips - 1).wait()
    store(1, mixed_b, mixed, chips - 1).wait()
    gone()
    own()
    for chip in range(chips):
        line.over(chip)
    for fetch in fetches(0):
        fetch.start()
    for t in range(chips):
        if t + 1 < chips:
            for fetch in fetches(t + 1):
                fetch.start()
        for fetch in fetches(t):
            fetch.wait()
        if t > 0:
            store(2, grad_b, grad_gate_up, t - 1).wait()
        here = span(t)

        @pl.loop(0, units // BLOCK)
        def _(u):
            part = pl.ds(pl.multiple_of(u * BLOCK, BLOCK), BLOCK)
            far = pl.ds(pl.multiple_of(units + u * BLOCK, BLOCK), BLOCK)
            gate, up = gates[here, part], gates[here, far]
            grad_mixed = cols_inner(grad_in[t % 2], down_w[part, :])
            sigmoid = 1.0 / (1.0 + jnp.exp(-gate))
            grad_b[:, part] = (
                grad_mixed * up * (sigmoid * (1.0 + gate * (1.0 - sigmoid)))
            ).astype(BF16)
            grad_b[:, far] = (grad_mixed * (gate * sigmoid)).astype(BF16)

        store(2, grad_b, grad_gate_up, t).start()
        if t > 0:
            store(3, parts_b, parts, t - 1).wait()
        if (chips + t) % 2 == 1 and (chips + t) // 2 < chips - 1:
            scatter.step((chips + t) // 2)

        @pl.loop(0, width // step)
        def _(c):
            part = pl.ds(pl.multiple_of(c * step, step), step)
            parts_b[:, part] = cols_inner(grad_b[...], gate_up[part, :]).astype(BF16)

        store(3, parts_b, parts, t).start()
    scatter.last()

    def out_rows(part):
        output[part] = (hidden[part] + held[k.z, part].astype(F32)).astype(BF16)

    row_loop(rows, out_rows)
    store(2, grad_b, grad_gate_up, chips - 1).wait()
    store(3, parts_b, parts, chips - 1).wait()
    k.finish()


def middle_kernel(
    groups, ranks, subs, parts, hidden, grad_out, gain, normed, grad_gate_up_all,
    grad_all, grad_hidden, sums, gate_up_sum,
    grad_gate_up, mine, held, landed, rounded, tile, grad_w, gate_up_landed, local, sends, recvs,
):
    k = Links(groups, ranks, sends, recvs)
    rows = hidden.shape[0] // subs
    depth = grad_w.shape[2]
    step = 512
    scatters, gathers = [], []
    for sub in range(subs):
        piece = pl.ds(sub * rows, rows)
        scatters.append(
            LineScatter(
                k,
                lambda chip, piece=piece: mine.at[chip, piece],
                lambda chip, piece=piece: held.at[chip, piece],
                lambda slot, piece=piece: landed.at[slot, piece],
            )
        )
        gathers.append(LineGather(k, lambda rank, piece=piece: grad_all.at[rank, piece]))
    gate_up_sums = [
        GroupScatter(
            k,
            lambda group, n=n: grad_w.at[group, n],
            lambda i, n=n: gate_up_landed.at[n, i],
            n % 2 == 1,
        )
        for n in range(ranks)
    ]
    per_group = ranks * depth // BLOCK
    per_tile = BLOCK // depth
    tiles = [(q, g) for q in range(per_group) for g in range(groups)]

    def load(i):
        q, g = tiles[i]
        return pltpu.make_async_copy(
            normed.at[:, pl.ds((g * per_group + q) * BLOCK, BLOCK)], tile.at[i % 2], local.at[i % 2]
        )

    whole = pltpu.make_async_copy(grad_gate_up_all, grad_gate_up, local.at[2])

    def work(i):
        q, g = tiles[i]
        if i + 1 < len(tiles):
            load(i + 1).start()
        load(i).wait()
        flipped = tile[i % 2].astype(F32).T.astype(BF16)

        @pl.loop(0, grad_gate_up.shape[1] // step)
        def _(c):
            part = pl.ds(pl.multiple_of(c * step, step), step)
            total = dot(flipped, grad_gate_up[:, part]).astype(BF16)
            for n in range(per_tile):
                grad_w[g, q * per_tile + n, :, part] = total[n * depth : (n + 1) * depth]

        if g == groups - 1:
            for n in range(per_tile):
                gate_up_sums[q * per_tile + n].start(0)

    load(0).start()
    whole.start()
    k.barrier()
    for sub, scatter in enumerate(scatters):
        scatter.start(lambda rank, sub=sub: parts.at[rank, pl.ds(sub * rows, rows)])
    sums[...] = jnp.zeros_like(sums)

    def rows_of(part):
        total = hidden[part]
        scale = inverse_rms(total)
        scaled = total * scale
        grad = held[k.z, part].astype(F32)
        sums[...] += jnp.sum(grad * scaled, 0, keepdims=True)
        grad_total = grad_out[part].astype(F32) + norm_back(grad * gain[...], scaled, scale)
        grad_hidden[part] = grad_total
        rounded[part] = grad_total.astype(BF16)

    own = []
    hops = k.chips - 1
    early = len(tiles) // 4
    plan = spaced(list(range(early, len(tiles))), hops - 1) + [[]] * (subs * hops + 1)
    whole.wait()
    for place in range(early):
        work(place)
    for turn in range(subs + 1):
        if turn < subs:
            scatters[turn].pairs()
        for i in range(hops):
            if turn < subs:
                scatters[turn].step(i)
            if turn > 0:
                gathers[turn - 1].step(i + 1)
            for place in plan[turn * hops + i]:
                work(place)
            if turn == 1 and i == 0:
                for sums_of in gate_up_sums[: ranks // 2]:
                    sums_of.wait(0)
                    sums_of.start(1)
        if turn < subs:
            scatters[turn].last()
            row_loop(rows, rows_of, first=turn * rows)
            piece = pl.ds(turn * rows, rows)
            gathers[turn].start(rounded.at[piece])
            own.append(k.move(rounded.at[piece], grad_all.at[k.f, piece]))
        if turn == 1:
            for sums_of in gate_up_sums[ranks // 2 :]:
                sums_of.wait(0)
                sums_of.start(1)
    for stage in range(1, k.bits):
        for n, sums_of in enumerate(gate_up_sums):
            if stage + 1 < k.bits:
                sums_of.wait(stage)
                sums_of.start(stage + 1)
            else:
                sums_of.wait(stage, gate_up_sum.at[n])
    for gather in gathers:
        gather.finish()
    for wait in own:
        wait()
    k.finish()


def attend_back_kernel(
    groups, ranks, rank_heads, slice_width,
    lengths, out_all, normed, grad_rows, queries, keys, values, attended, log_totals,
    cosine, sine, qkv, gate_up_sum, grad_down, tokens, grad_hidden, gain_rows, sums_two,
    gate_up_grad, down_grad, qkv_grad, out_grad, grad_tokens, gain_grads,
    out_w, grad_qkv, keys_t, grad_keys, grad_values, down_landed, held, landed, parts_b, tile,
    grad_qkv_w, qkv_landed, grad_out_w, out_landed, sums, tiles, tiles_landed, tiles_sum, group_tiles,
    local, sends, recvs,
):
    k = Links(groups, ranks, sends, recvs)
    length = lengths[0]
    cols, width = queries.shape[1], grad_rows.shape[1]
    rows = tokens.shape[0]
    pair = 2 * rows
    blocks = keys_t.shape[0]
    depth = qkv_grad.shape[1]
    step = 512

    def group_sums(ref, landing, count):
        size = ref.shape[1] // count
        return [
            GroupScatter(
                k,
                lambda group, n=n: ref.at[group, pl.ds(n * size, size)],
                lambda i, n=n: landing.at[n, i],
                n % 2 == 1,
            )
            for n in range(count)
        ], size

    down_sums, down_size = group_sums(grad_down, down_landed, down_landed.shape[0])
    out_sums, out_size = group_sums(grad_out_w, out_landed, out_landed.shape[0])
    qkv_sums = [
        GroupScatter(
            k,
            lambda group, n=n: grad_qkv_w.at[group, n],
            lambda i, n=n: qkv_landed.at[n, i],
            n % 2 == 1,
        )
        for n in range(ranks)
    ]
    scatter = LineScatter(
        k, None, lambda chip: held.at[chip], lambda slot: landed.at[slot]
    )
    gate_up_ex, exchange, tile_exchange = Exchange(k), Exchange(k), Exchange(k)
    tile_sends, tile_recvs = k.take(groups, groups)
    gate_up_in = lambda rank: gate_up_grad.at[rank]
    qkv_in = lambda rank: qkv_grad.at[rank]

    def onward(several, stage):
        for sums_of in several:
            sums_of.wait(stage)
            sums_of.start(stage + 1)

    per_group = ranks * depth // BLOCK
    per_tile = BLOCK // depth
    work = [(q, g) for q in range(per_group) for g in range(groups)]

    def load(i):
        q, g = work[i]
        return pltpu.make_async_copy(
            normed.at[:, pl.ds((g * per_group + q) * BLOCK, BLOCK)], tile.at[i % 2], local.at[i % 2]
        )

    def weight_tile(i):
        q, g = work[i]
        if i + 1 < len(work):
            load(i + 1).start()
        load(i).wait()
        flipped = tile[i % 2].astype(F32).T.astype(BF16)
        for c in range(3):
            part = slice(c * cols, (c + 1) * cols)
            total = dot(flipped, grad_qkv[:, part]).astype(BF16)
            for n in range(per_tile):
                grad_qkv_w[g, q * per_tile + n, :, part] = total[n * depth : (n + 1) * depth]
        if g == groups - 1:
            for n in range(per_tile):
                qkv_sums[q * per_tile + n].start(0)

    before = []

    def parts_of(t):
        chip = far_first(k, t)
        here = pl.ds(pl.multiple_of(chip * pair, 16), pair)
        if t > 1:
            before[t - 2]()
            before[t - 2] = lambda: None

        @pl.loop(0, width // step)
        def _(c):
            part = pl.ds(pl.multiple_of(c * step, step), step)
            parts_b[t % 2, :, part] = cols_inner(grad_qkv[here, :], qkv[part, :]).astype(BF16)

        def core_rows(core):
            return parts_b.at[t % 2, pl.ds(pl.multiple_of(core * rows, 16), rows)]

        before.append(scatter.give(chip, core_rows(1 - k.c), later=False))
        return chip, core_rows(k.c)

    def onto(t, chip, mine):
        scatter.pair(chip, mine)
        if t + 1 < k.chips:
            scatter.toward(chip)

    load(0).start()
    fetch = k.move(out_all.at[pl.ds(pl.multiple_of(k.f * cols, cols), cols)], out_w)
    k.barrier()
    for sums_of in down_sums:
        sums_of.start(0)
    gate_up_ex.start(lambda rank: gate_up_sum.at[rank], gate_up_in)
    grad_keys[...] = jnp.zeros_like(grad_keys)
    grad_values[...] = jnp.zeros_like(grad_values)

    @pl.loop(0, blocks)
    def _(i):
        block = pl.ds(pl.multiple_of(i * BLOCK, BLOCK), BLOCK)
        keys_t[i] = keys[block, :].astype(F32).T.astype(BF16)

    fetch()

    def back_rows(i):
        attend_back_rows(
            i, rank_heads, grad_rows, out_w, queries, keys, keys_t, values, attended, length, log_totals,
            cosine, sine, grad_keys, grad_values, grad_qkv,
        )

    pl.loop(0, blocks - 1)(back_rows)
    for stage in range(k.bits - 1):
        onward(down_sums, stage)
    back_rows(blocks - 1)
    pl.loop(0, blocks)(
        lambda i: finish_back_rows(i, cosine, sine, grad_keys, grad_values, grad_qkv)
    )
    shares = spaced(list(range(len(work))), k.chips)
    for t in range(k.chips):
        chip, mine = parts_of(t)
        for i in shares[t]:
            weight_tile(i)
        onto(t, chip, mine)

    out_rows = grad_out_w.shape[1]
    split = groups * out_rows // cols
    out_base = lax.rem(k.f, split) * (cols // out_rows)
    if split > 1:
        grad_out_w[...] = jnp.zeros_like(grad_out_w)

    @pl.loop(0, width // BLOCK)
    def _(t):
        part = pl.ds(pl.multiple_of(t * BLOCK, BLOCK), BLOCK)
        total = rows_inner(attended[...], grad_rows[:, part]).astype(BF16)
        for n in range(cols // out_rows):
            grad_out_w[out_base + n, :, part] = total[n * out_rows : (n + 1) * out_rows]

    for sums_of in out_sums:
        sums_of.start(0)
    for stage in range(k.bits - 1):
        onward(qkv_sums, stage)
        onward(out_sums, stage)
    for n, sums_of in enumerate(qkv_sums):
        exchange.start_piece(n, sums_of.wait(k.bits - 1), qkv_in)
    scatter.last()
    sums[...] = jnp.zeros_like(sums)

    def rows_of(part):
        total = tokens[part].astype(F32)
        scale = inverse_rms(total)
        scaled = total * scale
        grad = held[k.z, part].astype(F32)
        sums[...] += jnp.sum(grad * scaled, 0, keepdims=True)
        grad_tokens[part] = (
            grad_hidden[part] + norm_back(grad * gain_rows[0:1, :], scaled, scale)
        ).astype(BF16)

    row_loop(rows, rows_of)
    tiles[...] = jnp.zeros_like(tiles)
    for rank in range(ranks):
        for group in range(groups):
            at = (group * ranks + rank) * slice_width // 128 * 128
            tiles[rank, group, 0:1] = sums[:, at : at + 128]
            tiles[rank, group, 1:2] = sums_two[:, at : at + 128]
    tile_in = lambda rank: tiles_landed.at[rank]
    tile_exchange.start(lambda rank: tiles.at[rank], tile_in)
    for n, sums_of in enumerate(out_sums):
        sums_of.wait(k.bits - 1, out_grad.at[pl.ds(n * out_size, out_size)])
    for n, sums_of in enumerate(down_sums):
        sums_of.wait(k.bits - 1, down_grad.at[pl.ds(n * down_size, down_size)])
    tile_exchange.finish(tile_in)
    total = tiles_landed[0]
    for rank in range(1, ranks):
        total = total + tiles_landed[rank]
    tiles_sum[...] = total
    for i in range(1, groups):
        other = lax.rem(k.d + i, groups)
        k.send(
            None,
            tiles_sum.at[other],
            group_tiles.at[k.d],
            tile_sends + other,
            tile_recvs + k.d,
            (other, k.f),
        )
    group_tiles[k.d] = tiles_sum[k.d]
    for i in range(1, groups):
        other = lax.rem(k.d + i, groups)
        k.arrived(None, group_tiles.at[other], tile_recvs + other)
    total = group_tiles[0]
    for group in range(1, groups):
        total = total + group_tiles[group]
    gain_grads[...] = total
    for wait in before:
        wait()
    gate_up_ex.finish(gate_up_in)
    exchange.finish(qkv_in, own=False)
    k.finish()


def head_places(ranks, rank_heads, split):
    places = {}
    for rank in range(ranks):
        for b in range(rank_heads):
            head = (rank % split * rank_heads + b) * (ranks // split) + rank // split
            places[head] = (rank, b)
    return [places[head] for head in range(HEADS)]


def finish_kernel(
    groups, places, gate_up_grad, qkv_grad, grad_w_gate, grad_w_up, grad_w_query, grad_w_key, grad_w_value
):
    ranks, cols, units = qkv_grad.shape[0], qkv_grad.shape[2] // 3, gate_up_grad.shape[2] // 2
    part = units // groups
    for rank in range(ranks):
        for group in range(groups):
            at = (group * ranks + rank) * part
            for n, out in enumerate((grad_w_gate, grad_w_up)):
                start = n * units + group * part
                out[:, at : at + part] = gate_up_grad[rank, :, start : start + part].astype(F32)
    for n, out in enumerate((grad_w_query, grad_w_key, grad_w_value)):
        for head in range(0, HEADS, 2):
            halves = []
            for rank, b in places[head : head + 2]:
                start = n * cols + b * HEAD_DIM
                halves.append(qkv_grad[rank, :, start : start + HEAD_DIM].astype(F32))
            at = head * HEAD_DIM
            out[:, at : at + 2 * HEAD_DIM] = jnp.concatenate(halves, 1)


VMEM = pl.BlockSpec(memory_space=pltpu.VMEM)
ANY = pl.BlockSpec(memory_space=pl.ANY)
SMEM = pl.BlockSpec(memory_space=pltpu.SMEM)


def call(kernel, identity, ins, outs, scratch, semaphores, args, local=0):
    return pl.pallas_call(
        kernel,
        out_shape=[jax.ShapeDtypeStruct(shape, kind) for shape, kind, _ in outs],
        in_specs=ins,
        out_specs=[place for _, _, place in outs],
        scratch_shapes=[pltpu.VMEM(shape, kind) for shape, kind in scratch]
        + [pltpu.SemaphoreType.DMA((local,))] * (local > 0)
        + [pltpu.SemaphoreType.DMA((semaphores,))] * 2,
        compiler_params=pltpu.CompilerParams(
            collective_id=identity, has_side_effects=True, vmem_limit_bytes=61 * 1024 * 1024
        ),
    )(*args)


def build(groups, ranks):
    def body(
        tokens, cotangent, lengths, norm_attn, w_query, w_key, w_value, w_output, norm_mlp, w_gate, w_up, w_down
    ):
        rows, width = tokens.shape
        depth = w_query.shape[0]
        count = rows * ranks
        rank_heads = HEADS // ranks
        hidden_part = w_down.shape[0]
        out_rows = w_output.shape[0]
        split = max(1, HEAD_DIM // out_rows)
        rank = lax.axis_index("fsdp")

        def heads_out(weight):
            shaped = weight.reshape(depth, split, rank_heads, ranks // split, HEAD_DIM)
            return shaped.transpose(3, 1, 0, 2, 4).reshape(ranks, depth, rank_heads * HEAD_DIM)

        def heads_in(pieces):
            shaped = pieces.reshape(ranks // split, split, depth, rank_heads, HEAD_DIM)
            return shaped.transpose(2, 1, 3, 0, 4).reshape(depth, HEADS * HEAD_DIM)

        def units_out(weight):
            shaped = weight.reshape(depth, groups, ranks, hidden_part)
            return shaped.transpose(2, 0, 1, 3).reshape(ranks, depth, groups * hidden_part)

        def units_in(pieces):
            shaped = pieces.reshape(ranks, depth, groups, hidden_part)
            return shaped.transpose(1, 2, 0, 3).reshape(depth, groups * ranks * hidden_part)

        span = [[base * split + i for i in range(split)] for base in range(ranks // split)]

        head_cols = rank_heads * HEAD_DIM
        unit_cols = groups * hidden_part
        chips = ranks // 2
        slice_width = norm_attn.shape[0]
        qkv_out = jnp.concatenate([heads_out(w) for w in (w_query, w_key, w_value)], -1)
        gate_up_out = jnp.concatenate([units_out(w) for w in (w_gate, w_up)], -1)
        place = (lax.axis_index("dp") * ranks + rank) * slice_width % 128
        gains = lax.dynamic_update_slice(
            jnp.zeros((16, 128), BF16), jnp.stack([norm_attn, norm_mlp]), (0, place)
        )
        cosine, sine = (jnp.asarray(table) for table in wide_tables(count))
        blocks = count // BLOCK
        heads_shape = ((count, head_cols), BF16, VMEM)
        (
            x_all, qkv, gain_rows, normed_one, queries, keys, values, attended, log_totals,
            attended_all, gate_up, out_all, down_w,
        ) = call(
            functools.partial(attend_kernel, groups, ranks, rank_heads, slice_width),
            5,
            [SMEM] + [VMEM] * 8,
            [
                ((count, width), BF16, VMEM),
                ((groups,) + qkv_out.shape, BF16, VMEM),
                ((8, width), F32, VMEM),
                ((count, width), BF16, VMEM),
            ]
            + [heads_shape] * 4
            + [
                ((blocks, rank_heads, BLOCK), F32, VMEM),
                ((count, width), BF16, ANY),
                ((groups,) + gate_up_out.shape, BF16, ANY),
                ((groups * ranks, out_rows, width), BF16, ANY),
                ((groups,) + w_down.shape, BF16, ANY),
            ],
            [
                ((groups, ranks, 16, 128), BF16),
                ((blocks, head_cols, BLOCK), BF16),
            ],
            448,
            (lengths, tokens, qkv_out, gains, w_output, w_down, gate_up_out, cosine, sine),
        )
        qkv = qkv.reshape(width, -1)
        gain_one, gain_two = gain_rows[0:1], gain_rows[1:2]
        gate_up = gate_up.reshape(width, -1)
        out_all = out_all.reshape(width, width)
        down_w = down_w.reshape(-1, width)
        own_places = rank * rows + jnp.arange(rows, dtype=jnp.int32)
        grad_out = jnp.where(own_places[:, None] < lengths[0], cotangent, jnp.zeros((), BF16))
        pair = 2 * rows
        line_scratch = [
            ((chips, rows, width), BF16),
            ((chips, rows, width), BF16),
            ((chips + 1, rows, width), BF16),
        ]
        grad_out_all, hidden, output, normed_two, mixed, grad_gate_up, parts = call(
            functools.partial(feed_forward_kernel, groups, ranks),
            2,
            [ANY] * 5 + [VMEM] * 2,
            [
                ((ranks, rows, width), BF16, ANY),
                ((rows, width), F32, VMEM),
                ((rows, width), BF16, VMEM),
                ((count, width), BF16, ANY),
                ((count, unit_cols), BF16, ANY),
                ((count, 2 * unit_cols), BF16, ANY),
                ((count, width), BF16, ANY),
            ],
            [
                ((width, width), BF16),
                ((width, 2 * unit_cols), BF16),
                ((unit_cols, width), BF16),
                ((2, pair, width), BF16),
                ((2, pair, width), BF16),
                ((2, pair, width), BF16),
                ((pair, width), F32),
                ((pair, width), BF16),
                ((count, 2 * unit_cols), F32),
                ((pair, unit_cols), BF16),
                ((pair, 2 * unit_cols), BF16),
                ((pair, width), BF16),
                ((pair, width), BF16),
            ]
            + line_scratch[1:],
            128,
            (attended_all, x_all, out_all, gate_up, down_w, grad_out, gain_two),
            local=15,
        )
        grad_down = rows_inner(mixed, grad_out_all.reshape(count, width)).astype(BF16)
        grad_hidden_all, grad_hidden, sums_two, gate_up_sum = call(
            functools.partial(middle_kernel, groups, ranks, 2),
            3,
            [ANY] + [VMEM] * 3 + [ANY] * 2,
            [
                ((ranks, rows, width), BF16, ANY),
                ((rows, width), F32, VMEM),
                ((1, width), F32, VMEM),
                ((ranks, depth, 2 * unit_cols), BF16, VMEM),
            ],
            [((count, 2 * unit_cols), BF16)]
            + line_scratch
            + [
                ((rows, width), BF16),
                ((2, count, BLOCK), BF16),
                ((groups, ranks, depth, 2 * unit_cols), BF16),
                ((ranks, groups - 1, depth, 2 * unit_cols), BF16),
            ],
            160,
            (parts.reshape(ranks, rows, width), hidden, grad_out, gain_two, normed_two, grad_gate_up),
            local=3,
        )
        down_pieces, out_pieces = 4, 2
        out_place = out_rows * split
        tile = (8, 128)
        grad_gate_up_w, grad_w_down, grad_qkv_w, grad_w_output, grad_tokens, sums = call(
            functools.partial(attend_back_kernel, groups, ranks, rank_heads, slice_width),
            6,
            [SMEM, ANY, ANY] + [VMEM] * 15,
            [
                ((ranks, depth, 2 * unit_cols), BF16, ANY),
                ((hidden_part, width), F32, VMEM),
                ((ranks, depth, 3 * head_cols), BF16, ANY),
                ((out_place, width), F32, VMEM),
                ((rows, width), BF16, VMEM),
                (tile, F32, VMEM),
            ],
            [
                ((head_cols, width), BF16),
                ((count, 3 * head_cols), BF16),
                ((blocks, head_cols, BLOCK), BF16),
                ((count, head_cols), F32),
                ((count, head_cols), F32),
                ((down_pieces, groups - 1, hidden_part // down_pieces, width), BF16),
            ]
            + line_scratch[1:]
            + [
                ((2, pair, width), BF16),
                ((2, count, BLOCK), BF16),
                ((groups, ranks, depth, 3 * head_cols), BF16),
                ((ranks, groups - 1, depth, 3 * head_cols), BF16),
                ((groups, out_place, width), BF16),
                ((out_pieces, groups - 1, out_place // out_pieces, width), BF16),
                ((1, width), F32),
                ((ranks, groups) + tile, F32),
                ((ranks, groups) + tile, F32),
                ((groups,) + tile, F32),
                ((groups,) + tile, F32),
            ],
            192,
            (
                lengths,
                out_all,
                normed_one,
                grad_hidden_all.reshape(count, width),
                queries,
                keys,
                values,
                attended,
                log_totals,
                cosine,
                sine,
                qkv,
                gate_up_sum,
                grad_down.reshape(groups, hidden_part, width),
                tokens,
                grad_hidden,
                gain_rows,
                sums_two,
            ),
            local=2,
        )
        if split > 1:
            grad_w_output = lax.psum_scatter(
                grad_w_output, "fsdp", scatter_dimension=0, tiled=True, axis_index_groups=span
            )
        if hidden_part % 128 == 0:
            wide, narrow = (
                jax.ShapeDtypeStruct((depth, size), F32) for size in (w_gate.shape[1], width)
            )
            grad_w_gate, grad_w_up, grad_w_query, grad_w_key, grad_w_value = pl.pallas_call(
                functools.partial(finish_kernel, groups, head_places(ranks, rank_heads, split)),
                out_shape=[wide, wide, narrow, narrow, narrow],
                in_specs=[VMEM] * 2,
                out_specs=[VMEM] * 5,
                compiler_params=pltpu.CompilerParams(vmem_limit_bytes=32 * 1024 * 1024),
            )(grad_gate_up_w, grad_qkv_w)
        else:
            grad_w_gate = units_in(grad_gate_up_w[..., :unit_cols]).astype(F32)
            grad_w_up = units_in(grad_gate_up_w[..., unit_cols:]).astype(F32)
            grad_w_query, grad_w_key, grad_w_value = (
                heads_in(grad_qkv_w[..., i * head_cols : (i + 1) * head_cols]).astype(F32)
                for i in range(3)
            )
        place = (lax.axis_index("dp") * ranks + rank) * slice_width % 128
        sums = lax.dynamic_slice_in_dim(sums, place, slice_width, 1)
        return (
            output,
            grad_tokens,
            sums[0],
            grad_w_query,
            grad_w_key,
            grad_w_value,
            grad_w_output,
            sums[1],
            grad_w_gate,
            grad_w_up,
            grad_w_down,
        )

    return body


def solution(mesh):
    both = P(("dp", "fsdp"))
    rows = P(("dp", "fsdp"), None)
    return jax.shard_map(
        build(mesh.shape["dp"], mesh.shape["fsdp"]),
        mesh=mesh,
        in_specs=(rows, rows, P("dp"), both, rows, rows, rows, rows, both, rows, rows, rows),
        out_specs=(rows, rows, both, rows, rows, rows, rows, both, rows, rows, rows),
        check_vma=False,
    )
```

```python
import functools

import jax
import jax.numpy as jnp
import numpy as np
from jax import lax
from jax.experimental import pallas as pl
from jax.experimental.pallas import tpu as pltpu
from jax.sharding import PartitionSpec as P

HEADS = 32
HEAD_DIM = 64


EPSILON = 1e-05
THETA = 130000.0
BF16 = jnp.bfloat16
F32 = jnp.float32


def dot(left, right):
    return jnp.dot(left, right, preferred_element_type=F32)


def rows_inner(left, right):
    return lax.dot_general(left, right, (((0,), (0,)), ((), ())), preferred_element_type=F32)


def cols_inner(left, right):
    return lax.dot_general(left, right, (((1,), (1,)), ((), ())), preferred_element_type=F32)


def inverse_rms(values):
    return lax.rsqrt(jnp.mean(values * values, -1, keepdims=True) + EPSILON)


def norm_back(grad_scaled, scaled, scale):
    return scale * (grad_scaled - scaled * jnp.mean(grad_scaled * scaled, -1, keepdims=True))


BLOCK = 256
SCALE = 0.125


def turn_halves(values, cosine, sine):
    width = values.shape[1]
    half = HEAD_DIM // 2
    lane = lax.broadcasted_iota(jnp.int32, values.shape, 1)
    ahead = pltpu.roll(values, width - half, 1)
    behind = pltpu.roll(values, half, 1)
    return values * cosine + jnp.where(lane % HEAD_DIM < half, ahead, behind) * sine


def wide_tables(count):
    half = HEAD_DIM // 2
    inverse = np.float32(THETA) ** (-np.arange(half, dtype=np.float32) * np.float32(2.0) / HEAD_DIM)
    angles = np.arange(count, dtype=np.float32)[:, None] * inverse.astype(np.float32)[None, :]
    cosine, sine = np.cos(angles).astype(np.float32), np.sin(angles).astype(np.float32)
    return np.concatenate([cosine] * 4, -1), np.concatenate([-sine, sine] * 2, -1)


def table_rows(table, block, width):
    return jnp.concatenate([table[block, :]] * (width // 128), 1)


def key_bias(j, length):
    place = j * BLOCK + lax.broadcasted_iota(jnp.int32, (BLOCK, 1), 0)
    return jnp.where(place < length, 0.0, -1000000000.0)


def head_rows(values, head):
    row = lax.broadcasted_iota(jnp.int32, values.shape, 0)
    return jnp.where((row >= head * HEAD_DIM) & (row < (head + 1) * HEAD_DIM), values, 0.0)


def future(shape):
    return lax.broadcasted_iota(jnp.int32, shape, 0) > lax.broadcasted_iota(jnp.int32, shape, 1)


def attend_block(i, rank_heads, queries, keys, values_t, length, attended, log_totals):
    queries_t = queries.T
    masked = [(head_rows(queries_t, h) * SCALE).astype(BF16) for h in range(rank_heads)]

    def chunk(j, carry, last):
        part = pl.ds(pl.multiple_of(j * BLOCK, BLOCK), BLOCK)
        key_part, bias_part = keys[part, :], key_bias(j, length)
        after = []
        for h in range(rank_heads):
            top, total, out = carry[h]
            scores = dot(key_part, masked[h]) + bias_part
            if last:
                scores = jnp.where(future(scores.shape), -1000000000.0, scores)
            new_top = jnp.maximum(top, jnp.max(scores, 0, keepdims=True))
            keep = jnp.exp(top - new_top)
            weights = jnp.exp(scores - new_top)
            total = total * keep + jnp.sum(weights, 0, keepdims=True)
            out = out * keep + dot(
                values_t[j, h * HEAD_DIM : (h + 1) * HEAD_DIM, :], weights.astype(BF16)
            )
            after.append((new_top, total, out))
        return tuple(after)

    carry = tuple(
        (
            jnp.full((1, BLOCK), -3.0e38, F32),
            jnp.zeros((1, BLOCK), F32),
            jnp.zeros((HEAD_DIM, BLOCK), F32),
        )
        for _ in range(rank_heads)
    )
    carry = lax.fori_loop(0, i, lambda j, c: chunk(j, c, False), carry)
    carry = chunk(i, carry, True)
    outs = []
    for h, (top, total, out) in enumerate(carry):
        log_totals[i, h : h + 1, :] = top + jnp.log(total)
        outs.append(out * (1.0 / total))
    attended[pl.ds(pl.multiple_of(i * BLOCK, BLOCK), BLOCK), :] = (
        jnp.concatenate(outs, 0).T.astype(BF16)
    )


def project_block(i, x, gain, qkv, cosine, sine, normed, queries, keys, values, values_t):
    cols = queries.shape[1]
    start = i * BLOCK

    def rows_of(part):
        rows = x[part, :].astype(F32)
        normed[part, :] = (rows * inverse_rms(rows) * gain[0:1, :]).astype(BF16)

    pl.loop(0, BLOCK // 16)(
        lambda t: rows_of(pl.ds(pl.multiple_of(start + t * 16, 16), 16))
    )
    block = pl.ds(pl.multiple_of(start, BLOCK), BLOCK)
    rows = normed[block, :]

    def weight(n):
        return qkv[:, :, :, n * cols : (n + 1) * cols].reshape(x.shape[1], cols)

    cos, sin = table_rows(cosine, block, cols), table_rows(sine, block, cols)
    rounded = turn_halves(dot(rows, weight(0)), cos, sin).astype(BF16)
    queries[block, :] = rounded
    keys[block, :] = turn_halves(dot(rows, weight(1)), cos, sin).astype(BF16)
    value = dot(rows, weight(2))
    values[block, :] = value.astype(BF16)
    values_t[i] = value.T.astype(BF16)
    return rounded.astype(F32)


def lanes_of(values, head):
    lane = lax.broadcasted_iota(jnp.int32, values.shape, 1)
    return jnp.where((lane >= head * HEAD_DIM) & (lane < (head + 1) * HEAD_DIM), values, 0.0)


def attend_back_block(
    i, rank_heads, queries, keys, keys_t, values, attended, grad, length, log_totals, grad_keys, grad_values
):
    block = pl.ds(pl.multiple_of(i * BLOCK, BLOCK), BLOCK)
    query = queries[block, :].astype(F32) * SCALE
    query_t, grad_t = query.T, grad.T
    product = attended[block, :].astype(F32).T * grad_t
    masked_q = [head_rows(query_t, h).astype(BF16) for h in range(rank_heads)]
    masked_g = [head_rows(grad_t, h).astype(BF16) for h in range(rank_heads)]
    stacked_q = jnp.concatenate([lanes_of(query, h).astype(BF16) for h in range(rank_heads)], 0)
    stacked_g = jnp.concatenate([lanes_of(grad, h).astype(BF16) for h in range(rank_heads)], 0)
    deltas = [
        jnp.sum(product[h * HEAD_DIM : (h + 1) * HEAD_DIM], 0, keepdims=True)
        for h in range(rank_heads)
    ]
    totals = [log_totals[i, h : h + 1, :] for h in range(rank_heads)]

    def chunk(j, carry, last):
        part = pl.ds(pl.multiple_of(j * BLOCK, BLOCK), BLOCK)
        key_part, value_part, bias_part = keys[part, :], values[part, :], key_bias(j, length)
        after, weights_all, grads_all = [], [], []
        for h in range(rank_heads):
            scores = dot(key_part, masked_q[h]) + bias_part
            if last:
                scores = jnp.where(future(scores.shape), -1000000000.0, scores)
            weights = jnp.exp(scores - totals[h])
            grad_scores = weights * (dot(value_part, masked_g[h]) - deltas[h])
            weights_all.append(weights.astype(BF16))
            grads_all.append(grad_scores.astype(BF16))
            after.append(
                carry[h] + dot(keys_t[j, h * HEAD_DIM : (h + 1) * HEAD_DIM, :], grads_all[-1])
            )
        grad_values[part, :] += dot(jnp.concatenate(weights_all, 1), stacked_g)
        grad_keys[part, :] += dot(jnp.concatenate(grads_all, 1), stacked_q)
        return tuple(after)

    carry = tuple(jnp.zeros((HEAD_DIM, BLOCK), F32) for _ in range(rank_heads))
    carry = lax.fori_loop(0, i, lambda j, c: chunk(j, c, False), carry)
    carry = chunk(i, carry, True)
    return jnp.concatenate(carry, 0).T * SCALE


def attend_back_rows(
    i, rank_heads, grad_hidden, out_w, queries, keys, keys_t, values, attended, length, log_totals,
    cosine, sine, grad_keys, grad_values, grad_qkv,
):
    block = pl.ds(pl.multiple_of(i * BLOCK, BLOCK), BLOCK)
    cols = queries.shape[1]
    grad = cols_inner(grad_hidden[block, :], out_w[...]).astype(BF16).astype(F32)
    grad_q = attend_back_block(
        i, rank_heads, queries, keys, keys_t, values, attended, grad, length, log_totals, grad_keys, grad_values
    )
    grad_qkv[block, :cols] = turn_halves(
        grad_q, table_rows(cosine, block, cols), -table_rows(sine, block, cols)
    ).astype(BF16)


def finish_back_rows(i, cosine, sine, grad_keys, grad_values, grad_qkv):
    block = pl.ds(pl.multiple_of(i * BLOCK, BLOCK), BLOCK)
    cols = grad_keys.shape[1]
    grad_qkv[block, cols : 2 * cols] = turn_halves(
        grad_keys[block, :], table_rows(cosine, block, cols), -table_rows(sine, block, cols)
    ).astype(BF16)
    grad_qkv[block, 2 * cols :] = grad_values[block, :].astype(BF16)


MESH = pl.DeviceIdType.MESH


def when(cond, action):
    if cond is None:
        action()
    else:
        pl.when(cond)(action)


class Links:
    def __init__(self, groups, ranks, sends, recvs):
        self.groups, self.ranks, self.chips = groups, ranks, ranks // 2
        self.bits = groups.bit_length() - 1
        self.sends, self.recvs = sends, recvs
        self.used_sends = self.used_recvs = 0
        self.d, self.f = lax.axis_index("dp"), lax.axis_index("fsdp")
        self.z, self.c = lax.div(self.f, 2), lax.rem(self.f, 2)
        self.sibling = (self.d, self.z * 2 + 1 - self.c)
        self.pending = []

    def bit(self, b):
        return lax.rem(lax.div(self.d, 1 << b), 2)

    def partner(self, b):
        return (self.d + (1 - 2 * self.bit(b)) * (1 << b), self.f)

    def beside(self, way):
        return (self.d, self.f + 2 * way)

    def barrier(self):
        gate = pltpu.get_barrier_semaphore()
        for k in range(1, self.ranks):
            other = lax.rem(self.f + k, self.ranks)
            pl.semaphore_signal(gate, inc=1, device_id=(self.d, other), device_id_type=MESH)
        for k in range(1, self.groups):
            other = lax.rem(self.d + k, self.groups)
            pl.semaphore_signal(gate, inc=1, device_id=(other, self.f), device_id_type=MESH)
        pl.semaphore_wait(gate, self.ranks + self.groups - 2)

    def take(self, sends, recvs):
        first = (self.used_sends, self.used_recvs)
        self.used_sends += sends
        self.used_recvs += recvs
        return first

    def copy(self, source, target, send, recv, device):
        return pltpu.make_async_remote_copy(
            src_ref=source,
            dst_ref=target,
            send_sem=self.sends.at[send],
            recv_sem=self.recvs.at[recv],
            device_id=device,
            device_id_type=MESH,
        )

    def send(self, cond, source, target, send, recv, device, later=True):
        when(cond, lambda: self.copy(source, target, send, recv, device).start())
        gone = lambda: when(
            cond, lambda: self.copy(source, target, send, recv, device).wait_send()
        )
        if later:
            self.pending.append(gone)
        return gone

    def arrived(self, cond, target, recv):
        when(cond, lambda: self.copy(target, target, 0, recv, self.sibling).wait_recv())

    def move(self, source, target):
        send, _ = self.take(1, 0)
        make = lambda: pltpu.make_async_copy(source, target, self.sends.at[send])
        make().start()
        return lambda: make().wait()

    def finish(self):
        for wait in self.pending:
            wait()
        self.pending = []


class LineGather:
    def __init__(self, links, view):
        self.links, self.view = links, view
        chips = links.chips
        self.sends, self.recvs = links.take(3 * chips, 3 * chips)

    def start(self, source):
        k, chips = self.links, self.links.chips
        target = self.view(k.f)
        for side, way in enumerate((1, -1)):
            valid = (k.z + way >= 0) & (k.z + way < chips)
            k.send(
                valid, source, target, self.sends + side * chips, self.recvs + side * chips + 1, k.beside(way)
            )
        k.send(
            None, source, target, self.sends + 2 * chips + k.z, self.recvs + 2 * chips + k.z, k.sibling
        )

    def step(self, reach):
        k, chips = self.links, self.links.chips
        for side, way in enumerate((1, -1)):
            origin = k.z - way * reach
            here = (origin >= 0) & (origin < chips)
            block = self.view(origin * 2 + k.c)
            k.arrived(here, block, self.recvs + side * chips + reach)
            if reach + 1 < chips:
                onward = here & (k.z + way >= 0) & (k.z + way < chips)
                k.send(
                    onward,
                    block,
                    block,
                    self.sends + side * chips + reach,
                    self.recvs + side * chips + reach + 1,
                    k.beside(way),
                )
            k.send(
                here,
                block,
                block,
                self.sends + 2 * chips + origin,
                self.recvs + 2 * chips + origin,
                k.sibling,
            )

    def over(self, chip):
        k = self.links
        k.arrived(None, self.view(chip * 2 + 1 - k.c), self.recvs + 2 * k.chips + chip)

    def finish(self):
        k, chips = self.links, self.links.chips
        for chip in range(chips):
            k.arrived(None, self.view(chip * 2 + 1 - k.c), self.recvs + 2 * chips + chip)


def add_rows(target, *sources, step=16):
    rows = target.shape[0]

    @pl.loop(0, rows // step)
    def _(i):
        part = pl.ds(pl.multiple_of(i * step, step), step)
        total = sources[0][part].astype(F32)
        for source in sources[1:]:
            total = total + source[part].astype(F32)
        target[part] = total.astype(target.dtype)


class LineScatter:
    def __init__(self, links, mine, held, landed):
        self.links, self.mine, self.held, self.landed = links, mine, held, landed
        chips = links.chips
        self.sends, self.recvs = links.take(2 * chips, 3 * chips)
        self.gone = [lambda: None] * 2
        self.own = {}

    def give(self, chip, other, later=True):
        k = self.links
        return k.send(
            None, other, self.held(chip), self.sends + chip, self.recvs + chip, k.sibling, later=later
        )

    def start(self, parts):
        k = self.links
        for chip in range(k.chips):
            self.give(chip, parts(chip * 2 + 1 - k.c))
            self.own[chip] = k.move(parts(chip * 2 + k.c), self.mine(chip))

    def pair(self, chip, mine=None):
        k = self.links
        k.arrived(None, self.held(chip), self.recvs + chip)
        add_rows(self.held(chip), self.held(chip), self.mine(chip) if mine is None else mine)

    def pairs(self):
        for chip in range(self.links.chips):
            self.own[chip]()
            self.pair(chip)

    def place(self, side, chip, at):
        return self.landed(chip if side == 0 else jnp.where(chip == at, self.links.chips, chip))

    def onward(self, side, way, chip, before):
        k, chips = self.links, self.links.chips
        inner = before & (k.z > 0 if way > 0 else k.z < chips - 1)
        arrival = self.recvs + (1 + side) * chips + chip

        def add():
            k.arrived(None, self.place(side, chip, k.z), arrival)
            add_rows(self.held(chip), self.held(chip), self.place(side, chip, k.z))

        pl.when(inner)(add)
        return k.send(
            before,
            self.held(chip),
            self.place(side, chip, k.z + way),
            self.sends + chips + chip,
            arrival,
            k.beside(way),
        )

    def step(self, i):
        k, chips = self.links, self.links.chips
        for side, way in enumerate((1, -1)):
            chip = k.z + way * (chips - 1 - i)
            self.onward(side, way, chip, (chip >= 0) & (chip < chips))

    def toward(self, chip):
        k = self.links
        for side, way in enumerate((1, -1)):
            self.onward(side, way, chip, chip > k.z if way > 0 else chip < k.z)

    def last(self):
        k, chips = self.links, self.links.chips
        for side, inner in enumerate((k.z > 0, k.z < chips - 1)):

            def add():
                block = self.place(side, k.z, k.z)
                k.arrived(None, block, self.recvs + (1 + side) * chips + k.z)
                add_rows(self.held(k.z), self.held(k.z), block)

            pl.when(inner)(add)


class Exchange:
    def __init__(self, links):
        self.links = links
        self.sends, self.recvs = links.take(links.ranks, links.ranks)

    def start(self, source, target):
        k = self.links
        self.own = k.move(source(k.f), target(k.f))
        for i in range(1, k.ranks):
            other = lax.rem(k.f + i, k.ranks)
            k.send(
                None, source(other), target(k.f), self.sends + other, self.recvs + k.f, (k.d, other)
            )

    def finish(self, target, own=True):
        k = self.links
        if own:
            self.own()
        for i in range(1, k.ranks):
            other = lax.rem(k.f + i, k.ranks)
            k.arrived(None, target(other), self.recvs + other)

    def start_piece(self, rank, source, target):
        k = self.links
        k.send(
            k.f != rank, source, target(k.f), self.sends + rank, self.recvs + k.f, (k.d, rank)
        )
        here = lambda: pltpu.make_async_copy(source, target(k.f), k.sends.at[self.sends + rank])
        pl.when(k.f == rank)(lambda: here().start())
        k.pending.append(lambda: pl.when(k.f == rank)(lambda: here().wait()))


class GroupGather:
    def __init__(self, links, view, high):
        self.links, self.view, self.high = links, view, high
        count = links.groups - 1
        self.sends, self.recvs = links.take(count, count)

    def flip(self, stage):
        k = self.links
        low, up = 1 << stage, 1 << (k.bits - 1 - stage)
        size = low + self.high * (up - low)
        return (1 - 2 * lax.rem(lax.div(k.d, size), 2)) * size

    def places(self, stage):
        places = [self.links.d]
        for past in range(stage):
            places = places + [place + self.flip(past) for place in places]
        return places

    def start(self, stage, source=None):
        k = self.links
        for i, place in enumerate(self.places(stage)):
            at = (1 << stage) - 1 + i
            target = self.view(place)
            k.send(
                None,
                target if source is None else source,
                target,
                self.sends + at,
                self.recvs + at,
                (k.d + self.flip(stage), k.f),
            )

    def arrivals(self, stage):
        return [place + self.flip(stage) for place in self.places(stage)]

    def wait(self, stage):
        for i, place in enumerate(self.arrivals(stage)):
            self.links.arrived(None, self.view(place), self.recvs + (1 << stage) - 1 + i)


class GroupScatter:
    def __init__(self, links, view, landed, high):
        self.links, self.view, self.landed = links, view, landed
        bits = list(range(links.bits))
        self.order = bits[::-1] if high else bits
        count = links.groups - 1
        self.sends, self.recvs = links.take(count, count)

    def base(self, stage):
        return sum(self.links.groups >> (s + 1) for s in range(stage))

    def sources(self, stage, flip):
        k = self.links
        b = self.order[stage]
        value = 1 - k.bit(b) if flip else k.bit(b)
        if stage > 0:
            count = k.groups >> (stage + 1)
            return [self.landed(self.base(stage - 1) + value + 2 * i) for i in range(count)]
        places = [value * (1 << b)]
        for b in self.order[1:]:
            places = places + [place + (1 << b) for place in places]
        return [self.view(place) for place in places]

    def start(self, stage):
        k = self.links
        for i, source in enumerate(self.sources(stage, True)):
            at = self.base(stage) + i
            k.send(
                None,
                source,
                self.landed(at),
                self.sends + at,
                self.recvs + at,
                k.partner(self.order[stage]),
            )

    def wait(self, stage, target=None):
        k = self.links
        for i, source in enumerate(self.sources(stage, False)):
            at = self.base(stage) + i
            k.arrived(None, self.landed(at), self.recvs + at)
            add_rows(self.landed(at) if target is None else target, source, self.landed(at))
        return self.landed(self.base(stage))


def row_loop(rows, action, step=16, first=0):
    @pl.loop(0, rows // step)
    def _(i):
        action(pl.ds(pl.multiple_of(first + i * step, step), step))


def spaced(events, blocks):
    count = len(events)
    return [events[b * count // blocks : (b + 1) * count // blocks] for b in range(blocks)]


def head_places(ranks, rank_heads, split):
    places = {}
    for rank in range(ranks):
        for b in range(rank_heads):
            head = (rank % split * rank_heads + b) * (ranks // split) + rank // split
            places[head] = (rank, b)
    return [places[head] for head in range(HEADS)]


def attend_kernel(
    groups, ranks, rank_heads, slice_width, packed, traffic,
    lengths, tokens, w_query, w_key, w_value, gains, out_w, down_w, w_gate, w_up, cosine, sine,
    x_all, qkv, gain_rows, normed, queries, keys, values, attended, log_totals,
    attended_all, gate_up, out_all, down_all,
    gains_all, values_t, qkv_out, gate_up_out, sends, recvs,
):
    k = Links(groups, ranks, sends, recvs)
    places = head_places(ranks, rank_heads, max(1, HEAD_DIM // out_w.shape[0]))
    for rank in range(ranks):
        mine = [[h for h in range(HEADS) if places[h] == (rank, b)][0] for b in range(rank_heads)]
        for n, ref in enumerate((w_query, w_key, w_value)):
            for b in range(0, rank_heads, 2):
                halves = [
                    ref[:, head * HEAD_DIM : (head + 1) * HEAD_DIM].astype(F32)
                    for head in mine[b : b + 2]
                ]
                at = (n * rank_heads + b) * HEAD_DIM
                qkv_out[rank, :, at : at + 2 * HEAD_DIM] = jnp.concatenate(halves, 1).astype(BF16)
    length = lengths[0]
    cols, rows = queries.shape[1], tokens.shape[0]
    depth, half = gate_up_out.shape[1], ranks // 2
    pieces = depth // 16
    blocks = values_t.shape[0]
    split = max(1, HEAD_DIM // out_w.shape[0])
    down_half = down_w.shape[0] // 2

    def unit(group, rank):
        return (
            (lax.div(rank, split) * split + lax.div(group, rank_heads)) * rank_heads
            + lax.rem(group, rank_heads)
        ) * split + lax.rem(rank, split)

    def out_block(group, rank):
        return out_all.at[unit(group, rank)]

    def attended_block(i, rank):
        return attended_all.at[
            pl.ds(i * BLOCK, BLOCK), pl.ds(pl.multiple_of(rank * cols, cols), cols)
        ]

    x_line = LineGather(k, lambda rank: x_all.at[pl.ds(pl.multiple_of(rank * rows, 16), rows)])
    out_line = LineGather(k, lambda rank: out_block(k.d, rank))
    lines = [LineGather(k, lambda rank, i=i: attended_block(i, rank)) for i in range(blocks)]
    gains_ex, qkv_ex = Exchange(k), Exchange(k)
    exchanges = [Exchange(k) for _ in range(pieces)]
    downs = [
        GroupGather(k, lambda group, h=h: down_all.at[group, pl.ds(h * down_half, down_half)], h)
        for h in range(2)
    ]
    late = [
        GroupGather(k, lambda group, h=h, ref=ref: ref.at[group, pl.ds(h * half, half)], h)
        for ref in (qkv, gains_all)
        for h in range(2)
    ]
    out_gathers = [
        GroupGather(k, lambda group, r=r: out_block(group, k.c * half + r), k.c) for r in range(half)
    ]
    gathers = [
        [
            GroupGather(
                k,
                lambda group, h=h, q=q: gate_up.at[group, pl.ds(h * half, half), pl.ds(q * 16, 16)],
                h,
            )
            for h in range(2)
        ]
        for q in range(pieces)
    ]
    over_sends, over_recvs = k.take(half * groups, half * groups)

    def onward(several, stage):
        for gather in several:
            gather.wait(stage)
            if stage + 1 < k.bits:
                gather.start(stage + 1)

    def out_onward(stage):
        for r, gather in enumerate(out_gathers):
            gather.wait(stage)
            if stage + 1 < k.bits:
                gather.start(stage + 1)
            for group in gather.arrivals(stage):
                block = out_block(group, k.c * half + r)
                at = r * groups + group
                k.send(None, block, block, over_sends + at, over_recvs + at, k.sibling)

    units_from = w_gate if packed else gate_up_out

    def send_out(q):
        part = pl.ds(q * 16, 16)
        exchanges[q].start(
            lambda rank: units_from.at[rank, part], lambda rank: gate_up.at[k.d, rank, part]
        )

    def came_in(q):
        exchanges[q].finish(lambda rank: gate_up.at[k.d, rank, pl.ds(q * 16, 16)])
        for gather in gathers[q]:
            gather.start(0)
        if q + 2 < pieces:
            send_out(q + 2)

    gains_in = lambda rank: gains_all.at[k.d, rank]
    qkv_in = lambda rank: qkv.at[k.d, rank]
    k.barrier()
    gains_ex.start(lambda rank: gains, gains_in)
    qkv_ex.start(lambda rank: qkv_out.at[rank], qkv_in)
    for h, gather in enumerate(downs):
        gather.start(0, down_w.at[pl.ds(h * down_half, down_half)])
    own_down = k.move(down_w, down_all.at[k.d])
    if not packed:
        units = gate_up_out.shape[2] // 2
        share = units // groups
        for rank in range(ranks):
            for group in range(groups):
                at = (group * ranks + rank) * share
                for n, ref in enumerate((w_gate, w_up)):
                    start = n * units + group * share
                    gate_up_out[rank, :, start : start + share] = ref[:, at : at + share]
    gains_ex.finish(gains_in)
    qkv_ex.finish(qkv_in)
    out_line.start(out_w)
    x_line.start(tokens)
    own = [
        k.move(out_w, out_block(k.d, k.f)),
        k.move(tokens, x_all.at[pl.ds(pl.multiple_of(k.f * rows, 16), rows)]),
    ]
    for gather in late:
        gather.start(0)
    own_down()
    onward(downs, 0)
    for wait in own:
        wait()
    out_line.step(1)
    x_line.step(1)
    onward(late, 0)
    for reach in range(2, k.chips):
        out_line.step(reach)
    out_line.finish()
    for gather in out_gathers:
        gather.start(0)
    for q in range(min(2, pieces)):
        x_line.step(2 + q)
        send_out(q)
    for reach in range(2 + min(2, pieces), k.chips):
        x_line.step(reach)
    for stage in range(1, k.bits):
        onward(late, stage)
    out_onward(0)
    for stage in range(1, k.bits):
        onward(downs, stage)
    x_line.finish()
    traffic.put(0, 1)
    members = 128 // slice_width
    for at in range(groups * ranks // members):
        group, first = at * members // ranks, at * members % ranks
        tile = gains_all[group, first].astype(F32)
        for other in range(1, members):
            tile = tile + gains_all[group, first + other].astype(F32)
        gain_rows[:, at * 128 : (at + 1) * 128] = tile[:8]

    events = []
    for q in range(pieces):
        events.append(lambda q=q: came_in(q))
        if q > 0:
            events.append(lambda q=q: onward(gathers[q - 1], 0))
    events.append(lambda: onward(gathers[pieces - 1], 0))
    if k.bits == 2:
        events.append(lambda: out_onward(1))
    plan = spaced(events, 2 * blocks)
    own = []
    for i in range(blocks):
        query = project_block(
            i, x_all, gain_rows, qkv, cosine, sine, normed, queries, keys, values, values_t
        )
        for event in plan[2 * i]:
            event()
        attend_block(i, rank_heads, query, keys, values_t, length, attended, log_totals)
        mine = attended.at[pl.ds(i * BLOCK, BLOCK)]
        lines[i].start(mine)
        own.append(k.move(mine, attended_block(i, k.f)))
        for reach in range(1, k.chips):
            if i - reach >= 0:
                lines[i - reach].step(reach)
        for event in plan[2 * i + 1]:
            event()
    for i in range(blocks, blocks + k.chips - 1):
        for reach in range(1, k.chips):
            if 0 <= i - reach < blocks:
                lines[i - reach].step(reach)
    traffic.put()
    for stage in range(1, k.bits):
        if k.bits > 2:
            out_onward(stage)
        for several in gathers:
            onward(several, stage)
    for r in range(half):
        for i in range(1, groups):
            group = lax.rem(k.d + i, groups)
            block = out_block(group, (1 - k.c) * half + r)
            k.arrived(None, block, over_recvs + r * groups + group)
    for wait in own:
        wait()
    for line in lines:
        line.finish()
    k.finish()


def far_first(k, t):
    total = 0
    for z in range(k.chips):
        order = sorted(range(k.chips), key=lambda chip: -abs(chip - z))
        total = total + jnp.where(k.z == z, order[t], 0)
    return total


def feed_forward_kernel(
    groups, ranks, traffic, attended_all, x_all, out_all, gate_up_all, down_all, grad_out, gain_rows,
    grad_out_all, hidden, output, normed, mixed, grad_gate_up, parts,
    out_w, gate_up, down_w, attended_in, x_in, grad_in, hidden_b, normed_b, gates, mixed_b, grad_b, down_b, parts_b,
    held, landed, local, sends, recvs,
):
    k = Links(groups, ranks, sends, recvs)
    chips, pair = k.chips, hidden_b.shape[0]
    rows = pair // 2
    width, units = out_w.shape[0], down_w.shape[0]
    step = 512
    line = LineGather(k, lambda rank: grad_out_all.at[rank])
    scatter = LineScatter(
        k, None, lambda chip: held.at[chip], lambda slot: landed.at[slot]
    )
    weights = [
        pltpu.make_async_copy(ref, buffer, local.at[n])
        for n, (ref, buffer) in enumerate(((out_all, out_w), (gate_up_all, gate_up), (down_all, down_w)))
    ]
    order = [far_first(k, t) for t in range(chips)]

    def span(t):
        return pl.ds(pl.multiple_of(order[t] * pair, 16), pair)

    def loads(t):
        return [
            pltpu.make_async_copy(ref.at[span(t)], buffer.at[t % 2], local.at[3 + 2 * n + t % 2])
            for n, (ref, buffer) in enumerate(((attended_all, attended_in), (x_all, x_in)))
        ]

    def fetches(t):
        return [
            pltpu.make_async_copy(
                grad_out_all.at[order[chips - 1 - t] * 2 + c],
                grad_in.at[t % 2, pl.ds(c * rows, rows)],
                local.at[7 + 2 * (t % 2) + c],
            )
            for c in range(2)
        ]

    def store(n, buffer, ref, t):
        return pltpu.make_async_copy(buffer, ref.at[span(t)], local.at[11 + n])

    for load in loads(0) + weights:
        load.start()
    k.barrier()
    line.start(grad_out)
    own = k.move(grad_out, grad_out_all.at[k.f])
    weights[0].wait()
    gone = []
    for t in range(chips):
        if t + 1 < chips:
            for load in loads(t + 1):
                load.start()
        for load in loads(t):
            load.wait()

        @pl.loop(0, width // step)
        def _(c):
            part = pl.ds(pl.multiple_of(c * step, step), step)
            hidden_b[:, part] = x_in[t % 2, :, part].astype(F32) + dot(
                attended_in[t % 2], out_w[:, part]
            )

        if t > 0:
            store(0, normed_b, normed, t - 1).wait()

        def normalise(part):
            total = hidden_b[part, :]
            normed_b[part, :] = (total * inverse_rms(total) * gain_rows[1:2, :]).astype(BF16)

        row_loop(pair, normalise)
        store(0, normed_b, normed, t).start()
        if t == 0:
            weights[1].wait()
        if t == chips - 1:

            @pl.loop(0, rows // 16)
            def _(i):
                source = pl.ds(pl.multiple_of(k.c * rows + i * 16, 16), 16)
                hidden[pl.ds(pl.multiple_of(i * 16, 16), 16), :] = hidden_b[source, :]

        if t > 0:
            store(1, mixed_b, mixed, t - 1).wait()
        if t > 2:
            line.step(t - 1)
        here = span(t)

        @pl.loop(0, units // BLOCK)
        def _(u):
            part = pl.ds(pl.multiple_of(u * BLOCK, BLOCK), BLOCK)
            far = pl.ds(pl.multiple_of(units + u * BLOCK, BLOCK), BLOCK)
            gate = dot(normed_b[...], gate_up[:, part])
            up = dot(normed_b[...], gate_up[:, far])
            gates[here, part] = gate
            gates[here, far] = up
            mixed_b[:, part] = (gate / (1.0 + jnp.exp(-gate)) * up).astype(BF16)

        store(1, mixed_b, mixed, t).start()
        if t == 0:
            weights[2].wait()
        elif t > 1:
            gone[t - 2]()

        @pl.loop(0, width // step)
        def _(c):
            part = pl.ds(pl.multiple_of(c * step, step), step)
            down_b[t % 2, :, part] = dot(mixed_b[...], down_w[:, part]).astype(BF16)

        def core_rows(t, core):
            return down_b.at[t % 2, pl.ds(pl.multiple_of(core * rows, 16), rows)]

        gone.append(scatter.give(order[t], core_rows(t, 1 - k.c), later=False))
        if t > 0:
            scatter.pair(order[t - 1], core_rows(t - 1, k.c))
        if t == 1:
            line.step(1)
        if t % 2 == 1:
            scatter.step(t // 2)
    store(0, normed_b, normed, chips - 1).wait()
    store(1, mixed_b, mixed, chips - 1).wait()
    for wait in gone[-2:]:
        wait()
    own()
    line.over(order[chips - 1])
    for fetch in fetches(0):
        fetch.start()
    for t in range(chips):
        if t == 1:
            line.step(chips - 1)
        if t + 1 < chips:
            line.over(order[chips - 2 - t])
            for fetch in fetches(t + 1):
                fetch.start()
        for fetch in fetches(t):
            fetch.wait()
        near = chips - 1 - t
        if t > 0:
            store(2, grad_b, grad_gate_up, near + 1).wait()
        here = span(near)

        @pl.loop(0, units // BLOCK)
        def _(u):
            part = pl.ds(pl.multiple_of(u * BLOCK, BLOCK), BLOCK)
            far = pl.ds(pl.multiple_of(units + u * BLOCK, BLOCK), BLOCK)
            gate, up = gates[here, part], gates[here, far]
            grad_mixed = cols_inner(grad_in[t % 2], down_w[part, :])
            sigmoid = 1.0 / (1.0 + jnp.exp(-gate))
            grad_b[:, part] = (
                grad_mixed * up * (sigmoid * (1.0 + gate * (1.0 - sigmoid)))
            ).astype(BF16)
            grad_b[:, far] = (grad_mixed * (gate * sigmoid)).astype(BF16)

        store(2, grad_b, grad_gate_up, near).start()
        if t > 0:
            store(3, parts_b, parts, near + 1).wait()
        if t == 0:
            scatter.pair(order[chips - 1], down_b.at[(chips - 1) % 2, pl.ds(pl.multiple_of(k.c * rows, 16), rows)])
        if (chips + t) % 2 == 1 and (chips + t) // 2 < chips - 1:
            scatter.step((chips + t) // 2)

        @pl.loop(0, width // step)
        def _(c):
            part = pl.ds(pl.multiple_of(c * step, step), step)
            parts_b[:, part] = cols_inner(grad_b[...], gate_up[part, :]).astype(BF16)

        store(3, parts_b, parts, near).start()
    scatter.last()

    def out_rows(part):
        output[part] = (hidden[part] + held[k.z, part].astype(F32)).astype(BF16)

    row_loop(rows, out_rows)
    store(2, grad_b, grad_gate_up, 0).wait()
    store(3, parts_b, parts, 0).wait()
    k.finish()


def middle_kernel(
    groups, ranks, subs, traffic, parts, hidden, grad_out, gain_rows, normed, grad_gate_up, mixed, grad_out_all,
    grad_all, grad_hidden, sums, gate_up_sum, grad_down,
    mine, held, landed, rounded, tile, grad_w, gate_up_landed, local, sends, recvs,
):
    k = Links(groups, ranks, sends, recvs)
    rows = hidden.shape[0] // subs
    depth = grad_w.shape[2]
    step = 512
    scatters, gathers = [], []
    for sub in range(subs):
        piece = pl.ds(sub * rows, rows)
        scatters.append(
            LineScatter(
                k,
                lambda chip, piece=piece: mine.at[chip, piece],
                lambda chip, piece=piece: held.at[chip, piece],
                lambda slot, piece=piece: landed.at[slot, piece],
            )
        )
        gathers.append(LineGather(k, lambda rank, piece=piece: grad_all.at[rank, piece]))
    gate_up_sums = [
        GroupScatter(
            k,
            lambda group, n=n: grad_w.at[group, n],
            lambda i, n=n: gate_up_landed.at[n, i],
            n % 2 == 1,
        )
        for n in range(ranks)
    ]
    per_group = ranks * depth // BLOCK
    per_tile = BLOCK // depth
    tiles = [(q, g) for q in range(per_group) for g in range(groups)]

    downs = mixed.shape[1] // BLOCK

    def load(i):
        ref, at = mixed, i - len(tiles)
        if i < len(tiles):
            ref, at = normed, tiles[i][1] * per_group + tiles[i][0]
        return pltpu.make_async_copy(
            ref.at[:, pl.ds(at * BLOCK, BLOCK)], tile.at[i % 2], local.at[i % 2]
        )

    def work(i):
        if i + 1 < len(tiles) + downs:
            load(i + 1).start()
        load(i).wait()
        if i >= len(tiles):
            flipped = tile[i % 2].astype(F32).T.astype(BF16)
            at = (i - len(tiles)) * BLOCK

            @pl.loop(0, grad_down.shape[1] // step)
            def _(c):
                part = pl.ds(pl.multiple_of(c * step, step), step)
                grad_down[at : at + BLOCK, part] = dot(flipped, grad_out_all[:, part]).astype(BF16)

            return
        q, g = tiles[i]
        flipped = tile[i % 2].astype(F32).T.astype(BF16)

        @pl.loop(0, grad_gate_up.shape[1] // step)
        def _(c):
            part = pl.ds(pl.multiple_of(c * step, step), step)
            total = dot(flipped, grad_gate_up[:, part]).astype(BF16)
            for n in range(per_tile):
                grad_w[g, q * per_tile + n, :, part] = total[n * depth : (n + 1) * depth]

        if g == groups - 1:
            for n in range(per_tile):
                gate_up_sums[q * per_tile + n].start(0)

    load(0).start()
    k.barrier()
    for sub, scatter in enumerate(scatters):
        scatter.start(lambda rank, sub=sub: parts.at[rank, pl.ds(sub * rows, rows)])
    sums[...] = jnp.zeros_like(sums)

    def rows_of(part):
        total = hidden[part]
        scale = inverse_rms(total)
        scaled = total * scale
        grad = held[k.z, part].astype(F32)
        sums[...] += jnp.sum(grad * scaled, 0, keepdims=True)
        grad_total = grad_out[part].astype(F32) + norm_back(grad * gain_rows[1:2, :], scaled, scale)
        grad_hidden[part] = grad_total
        rounded[part] = grad_total.astype(BF16)

    own = []
    hops = k.chips - 1
    early = len(tiles) // 4
    plan = spaced(list(range(early, len(tiles))), hops - 1) + [[]]
    plan = plan + spaced(list(range(len(tiles), len(tiles) + downs)), subs * hops)
    traffic.ready(5)
    for place in range(early):
        work(place)
    for turn in range(subs + 1):
        if turn < subs:
            scatters[turn].pairs()
        for i in range(hops):
            if turn < subs:
                scatters[turn].step(i)
            if turn > 0:
                gathers[turn - 1].step(i + 1)
            for place in plan[turn * hops + i]:
                if place == len(tiles):
                    traffic.ready(7)
                work(place)
            if turn == 1 and i == 0:
                for sums_of in gate_up_sums[: ranks // 2]:
                    sums_of.wait(0)
                    sums_of.start(1)
        if turn < subs:
            scatters[turn].last()
            row_loop(rows, rows_of, first=turn * rows)
            piece = pl.ds(turn * rows, rows)
            gathers[turn].start(rounded.at[piece])
            own.append(k.move(rounded.at[piece], grad_all.at[k.f, piece]))
        if turn == 1:
            for sums_of in gate_up_sums[ranks // 2 :]:
                sums_of.wait(0)
                sums_of.start(1)
    for stage in range(1, k.bits):
        for n, sums_of in enumerate(gate_up_sums):
            if stage + 1 < k.bits:
                sums_of.wait(stage)
                sums_of.start(stage + 1)
            else:
                sums_of.wait(stage, gate_up_sum.at[n])
    for gather in gathers:
        gather.finish()
    for wait in own:
        wait()
    k.finish()


def attend_back_kernel(
    groups, ranks, rank_heads, slice_width, traffic,
    lengths, out_all, normed, grad_rows, queries, keys, values, attended, log_totals,
    cosine, sine, qkv, gate_up_sum, grad_down, tokens, grad_hidden, gain_rows, sums_two,
    gate_up_grad, down_grad, qkv_grad, out_grad, grad_tokens, gain_grads,
    out_w, grad_qkv, keys_t, grad_keys, grad_values, down_landed, held, landed, parts_b, tile,
    grad_qkv_w, qkv_landed, grad_out_w, out_landed, sums, tiles, tiles_landed, tiles_sum, group_tiles,
    local, sends, recvs,
):
    k = Links(groups, ranks, sends, recvs)
    length = lengths[0]
    cols, width = queries.shape[1], grad_rows.shape[1]
    rows = tokens.shape[0]
    pair = 2 * rows
    blocks = keys_t.shape[0]
    depth = qkv_grad.shape[1]
    step = 512

    def group_sums(ref, landing, count):
        size = ref.shape[1] // count
        return [
            GroupScatter(
                k,
                lambda group, n=n: ref.at[group, pl.ds(n * size, size)],
                lambda i, n=n: landing.at[n, i],
                n % 2 == 1,
            )
            for n in range(count)
        ], size

    down_sums, down_size = group_sums(grad_down, down_landed, down_landed.shape[0])
    out_sums, out_size = group_sums(grad_out_w, out_landed, out_landed.shape[0])
    qkv_sums = [
        GroupScatter(
            k,
            lambda group, n=n: grad_qkv_w.at[group, n],
            lambda i, n=n: qkv_landed.at[n, i],
            n % 2 == 1,
        )
        for n in range(ranks)
    ]
    scatter = LineScatter(
        k, None, lambda chip: held.at[chip], lambda slot: landed.at[slot]
    )
    gate_up_ex, exchange, tile_exchange = Exchange(k), Exchange(k), Exchange(k)
    tile_sends, tile_recvs = k.take(groups, groups)
    gate_up_in = lambda rank: gate_up_grad.at[rank]
    qkv_in = lambda rank: qkv_grad.at[rank]

    def onward(several, stage):
        for sums_of in several:
            sums_of.wait(stage)
            sums_of.start(stage + 1)

    per_group = ranks * depth // BLOCK
    per_tile = BLOCK // depth
    work = [(q, g) for q in range(per_group) for g in range(groups)]

    def load(i):
        q, g = work[i]
        return pltpu.make_async_copy(
            normed.at[:, pl.ds((g * per_group + q) * BLOCK, BLOCK)], tile.at[i % 2], local.at[i % 2]
        )

    def weight_tile(i):
        q, g = work[i]
        if i + 1 < len(work):
            load(i + 1).start()
        load(i).wait()
        flipped = tile[i % 2].astype(F32).T.astype(BF16)
        for c in range(3):
            part = slice(c * cols, (c + 1) * cols)
            total = dot(flipped, grad_qkv[:, part]).astype(BF16)
            for n in range(per_tile):
                grad_qkv_w[g, q * per_tile + n, :, part] = total[n * depth : (n + 1) * depth]
        if g == groups - 1:
            for n in range(per_tile):
                qkv_sums[q * per_tile + n].start(0)

    before = []

    def parts_of(t):
        chip = far_first(k, t)
        here = pl.ds(pl.multiple_of(chip * pair, 16), pair)
        if t > 1:
            before[t - 2]()
            before[t - 2] = lambda: None

        @pl.loop(0, width // step)
        def _(c):
            part = pl.ds(pl.multiple_of(c * step, step), step)
            parts_b[t % 2, :, part] = cols_inner(grad_qkv[here, :], qkv[part, :]).astype(BF16)

        def core_rows(core):
            return parts_b.at[t % 2, pl.ds(pl.multiple_of(core * rows, 16), rows)]

        before.append(scatter.give(chip, core_rows(1 - k.c), later=False))
        return chip, core_rows(k.c)

    load(0).start()
    fetch = k.move(out_all.at[pl.ds(pl.multiple_of(k.f * cols, cols), cols)], out_w)
    k.barrier()
    traffic.ready(13)
    for sums_of in down_sums:
        sums_of.start(0)
    gate_up_ex.start(lambda rank: gate_up_sum.at[rank], gate_up_in)
    grad_keys[...] = jnp.zeros_like(grad_keys)
    grad_values[...] = jnp.zeros_like(grad_values)

    traffic.ready(5)

    @pl.loop(0, blocks)
    def _(i):
        block = pl.ds(pl.multiple_of(i * BLOCK, BLOCK), BLOCK)
        keys_t[i] = keys[block, :].astype(F32).T.astype(BF16)

    fetch()
    traffic.ready()

    def back_rows(i):
        attend_back_rows(
            i, rank_heads, grad_rows, out_w, queries, keys, keys_t, values, attended, length, log_totals,
            cosine, sine, grad_keys, grad_values, grad_qkv,
        )

    pl.loop(0, blocks - 1)(back_rows)
    for stage in range(k.bits - 1):
        onward(down_sums, stage)
    back_rows(blocks - 1)
    pl.loop(0, blocks)(
        lambda i: finish_back_rows(i, cosine, sine, grad_keys, grad_values, grad_qkv)
    )
    shares = spaced(list(range(len(work))), 2) + [[]] * k.chips
    given = None
    for t in range(k.chips):
        now = parts_of(t)
        if given is not None:
            scatter.pair(*given)
        given = now
        for i in shares[t]:
            weight_tile(i)
        if t == 1:
            scatter.step(0)
    scatter.pair(*given)

    out_rows = grad_out_w.shape[1]
    split = groups * out_rows // cols
    out_base = lax.rem(k.f, split) * (cols // out_rows)
    if split > 1:
        grad_out_w[...] = jnp.zeros_like(grad_out_w)

    @pl.loop(0, width // BLOCK)
    def _(t):
        part = pl.ds(pl.multiple_of(t * BLOCK, BLOCK), BLOCK)
        total = rows_inner(attended[...], grad_rows[:, part]).astype(BF16)
        for n in range(cols // out_rows):
            grad_out_w[out_base + n, :, part] = total[n * out_rows : (n + 1) * out_rows]

    for sums_of in out_sums:
        sums_of.start(0)
    for stage in range(k.bits - 1):
        onward(qkv_sums, stage)
        if stage == 0:
            scatter.step(1)
    for n, sums_of in enumerate(qkv_sums):
        exchange.start_piece(n, sums_of.wait(k.bits - 1), qkv_in)
        if n == ranks // 2 - 1:
            for i in range(2, k.chips - 1):
                scatter.step(i)
    for stage in range(k.bits - 1):
        onward(out_sums, stage)
    scatter.last()
    sums[...] = jnp.zeros_like(sums)

    def rows_of(part):
        total = tokens[part].astype(F32)
        scale = inverse_rms(total)
        scaled = total * scale
        grad = held[k.z, part].astype(F32)
        sums[...] += jnp.sum(grad * scaled, 0, keepdims=True)
        grad_tokens[part] = (
            grad_hidden[part] + norm_back(grad * gain_rows[0:1, :], scaled, scale)
        ).astype(BF16)

    row_loop(rows, rows_of)
    tiles[...] = jnp.zeros_like(tiles)
    for rank in range(ranks):
        for group in range(groups):
            at = (group * ranks + rank) * slice_width // 128 * 128
            tiles[rank, group, 0:1] = sums[:, at : at + 128]
            tiles[rank, group, 1:2] = sums_two[:, at : at + 128]
    tile_in = lambda rank: tiles_landed.at[rank]
    tile_exchange.start(lambda rank: tiles.at[rank], tile_in)
    for n, sums_of in enumerate(out_sums):
        sums_of.wait(k.bits - 1, out_grad.at[pl.ds(n * out_size, out_size)])
    for n, sums_of in enumerate(down_sums):
        sums_of.wait(k.bits - 1, down_grad.at[pl.ds(n * down_size, down_size)])
    tile_exchange.finish(tile_in)
    total = tiles_landed[0]
    for rank in range(1, ranks):
        total = total + tiles_landed[rank]
    tiles_sum[...] = total
    for i in range(1, groups):
        other = lax.rem(k.d + i, groups)
        k.send(
            None,
            tiles_sum.at[other],
            group_tiles.at[k.d],
            tile_sends + other,
            tile_recvs + k.d,
            (other, k.f),
        )
    group_tiles[k.d] = tiles_sum[k.d]
    for i in range(1, groups):
        other = lax.rem(k.d + i, groups)
        k.arrived(None, group_tiles.at[other], tile_recvs + other)
    total = group_tiles[0]
    for group in range(1, groups):
        total = total + group_tiles[group]
    gain_grads[...] = total
    for wait in before:
        wait()
    gate_up_ex.finish(gate_up_in)
    exchange.finish(qkv_in, own=False)
    k.finish()


def finish_kernel(
    groups, places, gate_up_grad, qkv_grad, grad_w_gate, grad_w_up, grad_w_query, grad_w_key, grad_w_value
):
    ranks, cols, units = qkv_grad.shape[0], qkv_grad.shape[2] // 3, gate_up_grad.shape[2] // 2
    part = units // groups
    for rank in range(ranks):
        for group in range(groups):
            at = (group * ranks + rank) * part
            for n, out in enumerate((grad_w_gate, grad_w_up)):
                start = n * units + group * part
                out[:, at : at + part] = gate_up_grad[rank, :, start : start + part].astype(F32)
    for n, out in enumerate((grad_w_query, grad_w_key, grad_w_value)):
        for head in range(0, HEADS, 2):
            halves = []
            for rank, b in places[head : head + 2]:
                start = n * cols + b * HEAD_DIM
                halves.append(qkv_grad[rank, :, start : start + HEAD_DIM].astype(F32))
            at = head * HEAD_DIM
            out[:, at : at + 2 * HEAD_DIM] = jnp.concatenate(halves, 1)


VMEM = pl.BlockSpec(memory_space=pltpu.VMEM)
ANY = pl.BlockSpec(memory_space=pl.ANY)
SMEM = pl.BlockSpec(memory_space=pltpu.SMEM)
LOAD, STORE = "load", "store"


class Traffic:
    def __init__(self, ins, outs):
        self.ins, self.outs, self.begun = ins, outs, []
        for load in ins.values():
            load.start()

    def ready(self, *places):
        for place in places or tuple(self.ins):
            self.ins.pop(place).wait()

    def put(self, *places):
        for place in places or tuple(self.outs):
            store = self.outs.pop(place)
            store.start()
            self.begun.append(store)

    def close(self):
        self.ready()
        self.put()
        for store in self.begun:
            store.wait()


def call(kernel, identity, ins, outs, scratch, semaphores, args, local=0):
    loads = [i for i, place in enumerate(ins) if place == LOAD]
    stores = [i for i, (_, _, place) in enumerate(outs) if place == STORE]

    def body(*refs):
        inputs, results = list(refs[: len(ins)]), list(refs[len(ins) : len(ins) + len(outs)])
        rest = refs[len(ins) + len(outs) :]
        own = len(scratch) + (local > 0)
        buffers, moves = rest[own : own + len(loads) + len(stores)], rest[-3]
        coming, going = {}, {}
        for n, i in enumerate(loads):
            coming[i] = pltpu.make_async_copy(inputs[i], buffers[n], moves.at[n])
            inputs[i] = buffers[n]
        for n, i in enumerate(stores, len(loads)):
            going[i] = pltpu.make_async_copy(buffers[n], results[i], moves.at[n])
            results[i] = buffers[n]
        traffic = Traffic(coming, going)
        kernel(traffic, *inputs, *results, *rest[:own], *rest[-2:])
        traffic.close()

    return pl.pallas_call(
        body,
        out_shape=[jax.ShapeDtypeStruct(shape, kind) for shape, kind, _ in outs],
        in_specs=[ANY if place == LOAD else place for place in ins],
        out_specs=[ANY if place == STORE else place for _, _, place in outs],
        scratch_shapes=[pltpu.VMEM(shape, kind) for shape, kind in scratch]
        + [pltpu.SemaphoreType.DMA((local,))] * (local > 0)
        + [pltpu.VMEM(args[i].shape, args[i].dtype) for i in loads]
        + [pltpu.VMEM(outs[i][0], outs[i][1]) for i in stores]
        + [pltpu.SemaphoreType.DMA((max(1, len(loads) + len(stores)),))]
        + [pltpu.SemaphoreType.DMA((semaphores,))] * 2,
        compiler_params=pltpu.CompilerParams(
            collective_id=identity, has_side_effects=True, vmem_limit_bytes=61 * 1024 * 1024
        ),
    )(*args)


def build(groups, ranks):
    def body(
        tokens, cotangent, lengths, norm_attn, w_query, w_key, w_value, w_output, norm_mlp, w_gate, w_up, w_down
    ):
        rows, width = tokens.shape
        depth = w_query.shape[0]
        count = rows * ranks
        rank_heads = HEADS // ranks
        hidden_part = w_down.shape[0]
        out_rows = w_output.shape[0]
        split = max(1, HEAD_DIM // out_rows)
        rank = lax.axis_index("fsdp")

        def heads_out(weight):
            shaped = weight.reshape(depth, split, rank_heads, ranks // split, HEAD_DIM)
            return shaped.transpose(3, 1, 0, 2, 4).reshape(ranks, depth, rank_heads * HEAD_DIM)

        def heads_in(pieces):
            shaped = pieces.reshape(ranks // split, split, depth, rank_heads, HEAD_DIM)
            return shaped.transpose(2, 1, 3, 0, 4).reshape(depth, HEADS * HEAD_DIM)

        def units_out(weight):
            shaped = weight.reshape(depth, groups, ranks, hidden_part)
            return shaped.transpose(2, 0, 1, 3).reshape(ranks, depth, groups * hidden_part)

        def units_in(pieces):
            shaped = pieces.reshape(ranks, depth, groups, hidden_part)
            return shaped.transpose(1, 2, 0, 3).reshape(depth, groups * ranks * hidden_part)

        span = [[base * split + i for i in range(split)] for base in range(ranks // split)]

        head_cols = rank_heads * HEAD_DIM
        unit_cols = groups * hidden_part
        chips = ranks // 2
        slice_width = norm_attn.shape[0]
        packed = hidden_part % 128 != 0
        gate_up_shape = (ranks, depth, 2 * unit_cols)
        if packed:
            feeds = (jnp.concatenate([units_out(w) for w in (w_gate, w_up)], -1), w_up)
        else:
            feeds = (w_gate, w_up)
        place = (lax.axis_index("dp") * ranks + rank) * slice_width % 128
        gains = lax.dynamic_update_slice(
            jnp.zeros((16, 128), BF16), jnp.stack([norm_attn, norm_mlp]), (0, place)
        )
        cosine, sine = (jnp.asarray(table) for table in wide_tables(count))
        blocks = count // BLOCK
        heads_shape = ((count, head_cols), BF16, STORE)
        (
            x_all, qkv, gain_rows, normed_one, queries, keys, values, attended, log_totals,
            attended_all, gate_up, out_all, down_w,
        ) = call(
            functools.partial(attend_kernel, groups, ranks, rank_heads, slice_width, packed),
            5,
            [SMEM] + [VMEM] * 11,
            [
                ((count, width), BF16, STORE),
                ((groups, ranks, depth, 3 * head_cols), BF16, STORE),
                ((8, width), F32, VMEM),
                ((count, width), BF16, STORE),
            ]
            + [heads_shape] * 4
            + [
                ((blocks, rank_heads, BLOCK), F32, STORE),
                ((count, width), BF16, ANY),
                ((groups,) + gate_up_shape, BF16, ANY),
                ((groups * ranks, out_rows, width), BF16, ANY),
                ((groups,) + w_down.shape, BF16, ANY),
            ],
            [
                ((groups, ranks, 16, 128), BF16),
                ((blocks, head_cols, BLOCK), BF16),
                ((ranks, depth, 3 * head_cols), BF16),
                (gate_up_shape, BF16),
            ],
            448,
            (lengths, tokens, w_query, w_key, w_value, gains, w_output, w_down) + feeds + (cosine, sine),
        )
        qkv = qkv.reshape(width, -1)
        gate_up = gate_up.reshape(width, -1)
        out_all = out_all.reshape(width, width)
        down_w = down_w.reshape(-1, width)
        own_places = rank * rows + jnp.arange(rows, dtype=jnp.int32)
        grad_out = jnp.where(own_places[:, None] < lengths[0], cotangent, jnp.zeros((), BF16))
        pair = 2 * rows
        line_scratch = [
            ((chips, rows, width), BF16),
            ((chips, rows, width), BF16),
            ((chips + 1, rows, width), BF16),
        ]
        grad_out_all, hidden, output, normed_two, mixed, grad_gate_up, parts = call(
            functools.partial(feed_forward_kernel, groups, ranks),
            2,
            [ANY] * 5 + [VMEM] * 2,
            [
                ((ranks, rows, width), BF16, ANY),
                ((rows, width), F32, VMEM),
                ((rows, width), BF16, VMEM),
                ((count, width), BF16, ANY),
                ((count, unit_cols), BF16, ANY),
                ((count, 2 * unit_cols), BF16, ANY),
                ((count, width), BF16, ANY),
            ],
            [
                ((width, width), BF16),
                ((width, 2 * unit_cols), BF16),
                ((unit_cols, width), BF16),
                ((2, pair, width), BF16),
                ((2, pair, width), BF16),
                ((2, pair, width), BF16),
                ((pair, width), F32),
                ((pair, width), BF16),
                ((count, 2 * unit_cols), F32),
                ((pair, unit_cols), BF16),
                ((pair, 2 * unit_cols), BF16),
                ((2, pair, width), BF16),
                ((pair, width), BF16),
            ]
            + line_scratch[1:],
            128,
            (attended_all, x_all, out_all, gate_up, down_w, grad_out, gain_rows),
            local=15,
        )
        grad_hidden_all, grad_hidden, sums_two, gate_up_sum, grad_down = call(
            functools.partial(middle_kernel, groups, ranks, 2),
            3,
            [ANY] + [VMEM] * 3 + [ANY, LOAD, ANY, LOAD],
            [
                ((ranks, rows, width), BF16, ANY),
                ((rows, width), F32, VMEM),
                ((1, width), F32, VMEM),
                ((ranks, depth, 2 * unit_cols), BF16, VMEM),
                ((unit_cols, width), BF16, STORE),
            ],
            line_scratch
            + [
                ((rows, width), BF16),
                ((2, count, BLOCK), BF16),
                ((groups, ranks, depth, 2 * unit_cols), BF16),
                ((ranks, groups - 1, depth, 2 * unit_cols), BF16),
            ],
            160,
            (
                parts.reshape(ranks, rows, width),
                hidden,
                grad_out,
                gain_rows,
                normed_two,
                grad_gate_up,
                mixed,
                grad_out_all.reshape(count, width),
            ),
            local=2,
        )
        down_pieces, out_pieces = 4, 2
        out_place = out_rows * split
        tile = (8, 128)
        grad_gate_up_w, grad_w_down, grad_qkv_w, grad_w_output, grad_tokens, sums = call(
            functools.partial(attend_back_kernel, groups, ranks, rank_heads, slice_width),
            6,
            [SMEM, ANY, ANY] + [LOAD] * 9 + [ANY, LOAD] + [VMEM] * 4,
            [
                ((ranks, depth, 2 * unit_cols), BF16, ANY),
                ((hidden_part, width), F32, VMEM),
                ((ranks, depth, 3 * head_cols), BF16, ANY),
                ((out_place, width), F32, VMEM),
                ((rows, width), BF16, VMEM),
                (tile, F32, VMEM),
            ],
            [
                ((head_cols, width), BF16),
                ((count, 3 * head_cols), BF16),
                ((blocks, head_cols, BLOCK), BF16),
                ((count, head_cols), F32),
                ((count, head_cols), F32),
                ((down_pieces, groups - 1, hidden_part // down_pieces, width), BF16),
            ]
            + line_scratch[1:]
            + [
                ((2, pair, width), BF16),
                ((2, count, BLOCK), BF16),
                ((groups, ranks, depth, 3 * head_cols), BF16),
                ((ranks, groups - 1, depth, 3 * head_cols), BF16),
                ((groups, out_place, width), BF16),
                ((out_pieces, groups - 1, out_place // out_pieces, width), BF16),
                ((1, width), F32),
                ((ranks, groups) + tile, F32),
                ((ranks, groups) + tile, F32),
                ((groups,) + tile, F32),
                ((groups,) + tile, F32),
            ],
            192,
            (
                lengths,
                out_all,
                normed_one,
                grad_hidden_all.reshape(count, width),
                queries,
                keys,
                values,
                attended,
                log_totals,
                cosine,
                sine,
                qkv,
                gate_up_sum,
                grad_down.reshape(groups, hidden_part, width),
                tokens,
                grad_hidden,
                gain_rows,
                sums_two,
            ),
            local=2,
        )
        if split > 1:
            grad_w_output = lax.psum_scatter(
                grad_w_output, "fsdp", scatter_dimension=0, tiled=True, axis_index_groups=span
            )
        if hidden_part % 128 == 0:
            wide, narrow = (
                jax.ShapeDtypeStruct((depth, size), F32) for size in (w_gate.shape[1], width)
            )
            grad_w_gate, grad_w_up, grad_w_query, grad_w_key, grad_w_value = pl.pallas_call(
                functools.partial(finish_kernel, groups, head_places(ranks, rank_heads, split)),
                out_shape=[wide, wide, narrow, narrow, narrow],
                in_specs=[VMEM] * 2,
                out_specs=[VMEM] * 5,
                compiler_params=pltpu.CompilerParams(vmem_limit_bytes=32 * 1024 * 1024),
            )(grad_gate_up_w, grad_qkv_w)
        else:
            grad_w_gate = units_in(grad_gate_up_w[..., :unit_cols]).astype(F32)
            grad_w_up = units_in(grad_gate_up_w[..., unit_cols:]).astype(F32)
            grad_w_query, grad_w_key, grad_w_value = (
                heads_in(grad_qkv_w[..., i * head_cols : (i + 1) * head_cols]).astype(F32)
                for i in range(3)
            )
        place = (lax.axis_index("dp") * ranks + rank) * slice_width % 128
        sums = lax.dynamic_slice_in_dim(sums, place, slice_width, 1)
        return (
            output,
            grad_tokens,
            sums[0],
            grad_w_query,
            grad_w_key,
            grad_w_value,
            grad_w_output,
            sums[1],
            grad_w_gate,
            grad_w_up,
            grad_w_down,
        )

    return body


def solution(mesh):
    both = P(("dp", "fsdp"))
    rows = P(("dp", "fsdp"), None)
    return jax.shard_map(
        build(mesh.shape["dp"], mesh.shape["fsdp"]),
        mesh=mesh,
        in_specs=(rows, rows, P("dp"), both, rows, rows, rows, rows, both, rows, rows, rows),
        out_specs=(rows, rows, both, rows, rows, rows, rows, both, rows, rows, rows),
        check_vma=False,
    )
```

```python
import functools

import jax
import jax.numpy as jnp
import numpy as np
from jax import lax
from jax.experimental import pallas as pl
from jax.experimental.pallas import tpu as pltpu
from jax.sharding import PartitionSpec as P

HEADS = 32
HEAD_DIM = 64


EPSILON = 1e-05
THETA = 130000.0
BF16 = jnp.bfloat16
F32 = jnp.float32


def dot(left, right):
    return jnp.dot(left, right, preferred_element_type=F32)


def rows_inner(left, right):
    return lax.dot_general(left, right, (((0,), (0,)), ((), ())), preferred_element_type=F32)


def cols_inner(left, right):
    return lax.dot_general(left, right, (((1,), (1,)), ((), ())), preferred_element_type=F32)


def inverse_rms(values):
    return lax.rsqrt(jnp.mean(values * values, -1, keepdims=True) + EPSILON)


def norm_back(grad_scaled, scaled, scale):
    return scale * (grad_scaled - scaled * jnp.mean(grad_scaled * scaled, -1, keepdims=True))


BLOCK = 256
SCALE = 0.125


def turn_halves(values, cosine, sine):
    width = values.shape[1]
    half = HEAD_DIM // 2
    lane = lax.broadcasted_iota(jnp.int32, values.shape, 1)
    ahead = pltpu.roll(values, width - half, 1)
    behind = pltpu.roll(values, half, 1)
    return values * cosine + jnp.where(lane % HEAD_DIM < half, ahead, behind) * sine


def wide_tables(count):
    half = HEAD_DIM // 2
    inverse = np.float32(THETA) ** (-np.arange(half, dtype=np.float32) * np.float32(2.0) / HEAD_DIM)
    angles = np.arange(count, dtype=np.float32)[:, None] * inverse.astype(np.float32)[None, :]
    cosine, sine = np.cos(angles).astype(np.float32), np.sin(angles).astype(np.float32)
    return np.concatenate([cosine] * 4, -1), np.concatenate([-sine, sine] * 2, -1)


def table_rows(table, block, width):
    return jnp.concatenate([table[block, :]] * (width // 128), 1)


def key_bias(j, length):
    place = j * BLOCK + lax.broadcasted_iota(jnp.int32, (BLOCK, 1), 0)
    return jnp.where(place < length, 0.0, -1000000000.0)


def head_rows(values, head):
    row = lax.broadcasted_iota(jnp.int32, values.shape, 0)
    return jnp.where((row >= head * HEAD_DIM) & (row < (head + 1) * HEAD_DIM), values, 0.0)


def future(shape):
    return lax.broadcasted_iota(jnp.int32, shape, 0) > lax.broadcasted_iota(jnp.int32, shape, 1)


def attend_block(i, rank_heads, queries, keys, values_t, length, attended, log_totals):
    queries_t = queries.T
    masked = [(head_rows(queries_t, h) * SCALE).astype(BF16) for h in range(rank_heads)]

    def chunk(j, carry, last):
        part = pl.ds(pl.multiple_of(j * BLOCK, BLOCK), BLOCK)
        key_part, bias_part = keys[part, :], key_bias(j, length)
        after = []
        for h in range(rank_heads):
            top, total, out = carry[h]
            scores = dot(key_part, masked[h]) + bias_part
            if last:
                scores = jnp.where(future(scores.shape), -1000000000.0, scores)
            new_top = jnp.maximum(top, jnp.max(scores, 0, keepdims=True))
            keep = jnp.exp(top - new_top)
            weights = jnp.exp(scores - new_top)
            total = total * keep + jnp.sum(weights, 0, keepdims=True)
            out = out * keep + dot(
                values_t[j, h * HEAD_DIM : (h + 1) * HEAD_DIM, :], weights.astype(BF16)
            )
            after.append((new_top, total, out))
        return tuple(after)

    carry = tuple(
        (
            jnp.full((1, BLOCK), -3.0e38, F32),
            jnp.zeros((1, BLOCK), F32),
            jnp.zeros((HEAD_DIM, BLOCK), F32),
        )
        for _ in range(rank_heads)
    )
    carry = lax.fori_loop(0, i, lambda j, c: chunk(j, c, False), carry)
    carry = chunk(i, carry, True)
    outs = []
    for h, (top, total, out) in enumerate(carry):
        log_totals[i, h : h + 1, :] = top + jnp.log(total)
        outs.append(out * (1.0 / total))
    attended[pl.ds(pl.multiple_of(i * BLOCK, BLOCK), BLOCK), :] = (
        jnp.concatenate(outs, 0).T.astype(BF16)
    )


def project_block(i, x, gain, qkv, cosine, sine, normed, queries, keys, values, values_t):
    cols = queries.shape[1]
    start = i * BLOCK

    def rows_of(part):
        rows = x[part, :].astype(F32)
        normed[part, :] = (rows * inverse_rms(rows) * gain[0:1, :]).astype(BF16)

    pl.loop(0, BLOCK // 16)(
        lambda t: rows_of(pl.ds(pl.multiple_of(start + t * 16, 16), 16))
    )
    block = pl.ds(pl.multiple_of(start, BLOCK), BLOCK)
    rows = normed[block, :]

    def weight(n):
        return qkv[:, :, :, n * cols : (n + 1) * cols].reshape(x.shape[1], cols)

    cos, sin = table_rows(cosine, block, cols), table_rows(sine, block, cols)
    rounded = turn_halves(dot(rows, weight(0)), cos, sin).astype(BF16)
    queries[block, :] = rounded
    keys[block, :] = turn_halves(dot(rows, weight(1)), cos, sin).astype(BF16)
    value = dot(rows, weight(2))
    values[block, :] = value.astype(BF16)
    values_t[i] = value.T.astype(BF16)
    return rounded.astype(F32)


def lanes_of(values, head):
    lane = lax.broadcasted_iota(jnp.int32, values.shape, 1)
    return jnp.where((lane >= head * HEAD_DIM) & (lane < (head + 1) * HEAD_DIM), values, 0.0)


def attend_back_block(
    i, rank_heads, queries, keys, keys_t, values, attended, grad, length, log_totals, grad_keys, grad_values
):
    block = pl.ds(pl.multiple_of(i * BLOCK, BLOCK), BLOCK)
    query = queries[block, :].astype(F32) * SCALE
    query_t, grad_t = query.T, grad.T
    product = attended[block, :].astype(F32).T * grad_t
    masked_q = [head_rows(query_t, h).astype(BF16) for h in range(rank_heads)]
    masked_g = [head_rows(grad_t, h).astype(BF16) for h in range(rank_heads)]
    stacked_q = jnp.concatenate([lanes_of(query, h).astype(BF16) for h in range(rank_heads)], 0)
    stacked_g = jnp.concatenate([lanes_of(grad, h).astype(BF16) for h in range(rank_heads)], 0)
    deltas = [
        jnp.sum(product[h * HEAD_DIM : (h + 1) * HEAD_DIM], 0, keepdims=True)
        for h in range(rank_heads)
    ]
    totals = [log_totals[i, h : h + 1, :] for h in range(rank_heads)]

    def chunk(j, carry, last):
        part = pl.ds(pl.multiple_of(j * BLOCK, BLOCK), BLOCK)
        key_part, value_part, bias_part = keys[part, :], values[part, :], key_bias(j, length)
        after, weights_all, grads_all = [], [], []
        for h in range(rank_heads):
            scores = dot(key_part, masked_q[h]) + bias_part
            if last:
                scores = jnp.where(future(scores.shape), -1000000000.0, scores)
            weights = jnp.exp(scores - totals[h])
            grad_scores = weights * (dot(value_part, masked_g[h]) - deltas[h])
            weights_all.append(weights.astype(BF16))
            grads_all.append(grad_scores.astype(BF16))
            after.append(
                carry[h] + dot(keys_t[j, h * HEAD_DIM : (h + 1) * HEAD_DIM, :], grads_all[-1])
            )
        grad_values[part, :] += dot(jnp.concatenate(weights_all, 1), stacked_g)
        grad_keys[part, :] += dot(jnp.concatenate(grads_all, 1), stacked_q)
        return tuple(after)

    carry = tuple(jnp.zeros((HEAD_DIM, BLOCK), F32) for _ in range(rank_heads))
    carry = lax.fori_loop(0, i, lambda j, c: chunk(j, c, False), carry)
    carry = chunk(i, carry, True)
    return jnp.concatenate(carry, 0).T * SCALE


def attend_back_rows(
    i, rank_heads, grad_hidden, out_w, queries, keys, keys_t, values, attended, length, log_totals,
    cosine, sine, grad_keys, grad_values, grad_qkv,
):
    block = pl.ds(pl.multiple_of(i * BLOCK, BLOCK), BLOCK)
    cols = queries.shape[1]
    grad = cols_inner(grad_hidden[block, :], out_w[...]).astype(BF16).astype(F32)
    grad_q = attend_back_block(
        i, rank_heads, queries, keys, keys_t, values, attended, grad, length, log_totals, grad_keys, grad_values
    )
    grad_qkv[block, :cols] = turn_halves(
        grad_q, table_rows(cosine, block, cols), -table_rows(sine, block, cols)
    ).astype(BF16)


def finish_back_rows(i, cosine, sine, grad_keys, grad_values, grad_qkv):
    block = pl.ds(pl.multiple_of(i * BLOCK, BLOCK), BLOCK)
    cols = grad_keys.shape[1]
    grad_qkv[block, cols : 2 * cols] = turn_halves(
        grad_keys[block, :], table_rows(cosine, block, cols), -table_rows(sine, block, cols)
    ).astype(BF16)
    grad_qkv[block, 2 * cols :] = grad_values[block, :].astype(BF16)


MESH = pl.DeviceIdType.MESH


def when(cond, action):
    if cond is None:
        action()
    else:
        pl.when(cond)(action)


class Links:
    def __init__(self, groups, ranks, sends, recvs):
        self.groups, self.ranks, self.chips = groups, ranks, ranks // 2
        self.bits = groups.bit_length() - 1
        self.sends, self.recvs = sends, recvs
        self.used_sends = self.used_recvs = 0
        self.d, self.f = lax.axis_index("dp"), lax.axis_index("fsdp")
        self.z, self.c = lax.div(self.f, 2), lax.rem(self.f, 2)
        self.sibling = (self.d, self.z * 2 + 1 - self.c)
        self.pending = []

    def bit(self, b):
        return lax.rem(lax.div(self.d, 1 << b), 2)

    def partner(self, b):
        return (self.d + (1 - 2 * self.bit(b)) * (1 << b), self.f)

    def beside(self, way):
        return (self.d, self.f + 2 * way)

    def barrier(self):
        gate = pltpu.get_barrier_semaphore()
        for k in range(1, self.ranks):
            other = lax.rem(self.f + k, self.ranks)
            pl.semaphore_signal(gate, inc=1, device_id=(self.d, other), device_id_type=MESH)
        for k in range(1, self.groups):
            other = lax.rem(self.d + k, self.groups)
            pl.semaphore_signal(gate, inc=1, device_id=(other, self.f), device_id_type=MESH)
        pl.semaphore_wait(gate, self.ranks + self.groups - 2)

    def take(self, sends, recvs):
        first = (self.used_sends, self.used_recvs)
        self.used_sends += sends
        self.used_recvs += recvs
        return first

    def copy(self, source, target, send, recv, device):
        return pltpu.make_async_remote_copy(
            src_ref=source,
            dst_ref=target,
            send_sem=self.sends.at[send],
            recv_sem=self.recvs.at[recv],
            device_id=device,
            device_id_type=MESH,
        )

    def send(self, cond, source, target, send, recv, device, later=True):
        when(cond, lambda: self.copy(source, target, send, recv, device).start())
        gone = lambda: when(
            cond, lambda: self.copy(source, target, send, recv, device).wait_send()
        )
        if later:
            self.pending.append(gone)
        return gone

    def arrived(self, cond, target, recv):
        when(cond, lambda: self.copy(target, target, 0, recv, self.sibling).wait_recv())

    def move(self, source, target):
        send, _ = self.take(1, 0)
        make = lambda: pltpu.make_async_copy(source, target, self.sends.at[send])
        make().start()
        return lambda: make().wait()

    def finish(self):
        for wait in self.pending:
            wait()
        self.pending = []


class LineGather:
    def __init__(self, links, view):
        self.links, self.view = links, view
        chips = links.chips
        self.sends, self.recvs = links.take(3 * chips, 3 * chips)

    def start(self, source):
        k, chips = self.links, self.links.chips
        target = self.view(k.f)
        for side, way in enumerate((1, -1)):
            valid = (k.z + way >= 0) & (k.z + way < chips)
            k.send(
                valid, source, target, self.sends + side * chips, self.recvs + side * chips + 1, k.beside(way)
            )
        k.send(
            None, source, target, self.sends + 2 * chips + k.z, self.recvs + 2 * chips + k.z, k.sibling
        )

    def step(self, reach):
        k, chips = self.links, self.links.chips
        for side, way in enumerate((1, -1)):
            origin = k.z - way * reach
            here = (origin >= 0) & (origin < chips)
            block = self.view(origin * 2 + k.c)
            k.arrived(here, block, self.recvs + side * chips + reach)
            if reach + 1 < chips:
                onward = here & (k.z + way >= 0) & (k.z + way < chips)
                k.send(
                    onward,
                    block,
                    block,
                    self.sends + side * chips + reach,
                    self.recvs + side * chips + reach + 1,
                    k.beside(way),
                )
            k.send(
                here,
                block,
                block,
                self.sends + 2 * chips + origin,
                self.recvs + 2 * chips + origin,
                k.sibling,
            )

    def over(self, chip):
        k = self.links
        k.arrived(None, self.view(chip * 2 + 1 - k.c), self.recvs + 2 * k.chips + chip)

    def finish(self):
        k, chips = self.links, self.links.chips
        for chip in range(chips):
            k.arrived(None, self.view(chip * 2 + 1 - k.c), self.recvs + 2 * chips + chip)


def add_rows(target, *sources, step=16):
    rows = target.shape[0]

    @pl.loop(0, rows // step)
    def _(i):
        part = pl.ds(pl.multiple_of(i * step, step), step)
        total = sources[0][part].astype(F32)
        for source in sources[1:]:
            total = total + source[part].astype(F32)
        target[part] = total.astype(target.dtype)


class LineScatter:
    def __init__(self, links, mine, held, landed):
        self.links, self.mine, self.held, self.landed = links, mine, held, landed
        chips = links.chips
        self.sends, self.recvs = links.take(2 * chips, 3 * chips)
        self.gone = [lambda: None] * 2
        self.own = {}

    def give(self, chip, other, later=True):
        k = self.links
        return k.send(
            None, other, self.held(chip), self.sends + chip, self.recvs + chip, k.sibling, later=later
        )

    def start(self, parts):
        k = self.links
        for chip in range(k.chips):
            self.give(chip, parts(chip * 2 + 1 - k.c))
            self.own[chip] = k.move(parts(chip * 2 + k.c), self.mine(chip))

    def pair(self, chip, mine=None):
        k = self.links
        k.arrived(None, self.held(chip), self.recvs + chip)
        add_rows(self.held(chip), self.held(chip), self.mine(chip) if mine is None else mine)

    def pairs(self):
        for chip in range(self.links.chips):
            self.own[chip]()
            self.pair(chip)

    def place(self, side, chip, at):
        return self.landed(chip if side == 0 else jnp.where(chip == at, self.links.chips, chip))

    def onward(self, side, way, chip, before):
        k, chips = self.links, self.links.chips
        inner = before & (k.z > 0 if way > 0 else k.z < chips - 1)
        arrival = self.recvs + (1 + side) * chips + chip

        def add():
            k.arrived(None, self.place(side, chip, k.z), arrival)
            add_rows(self.held(chip), self.held(chip), self.place(side, chip, k.z))

        pl.when(inner)(add)
        return k.send(
            before,
            self.held(chip),
            self.place(side, chip, k.z + way),
            self.sends + chips + chip,
            arrival,
            k.beside(way),
        )

    def step(self, i):
        k, chips = self.links, self.links.chips
        for side, way in enumerate((1, -1)):
            chip = k.z + way * (chips - 1 - i)
            self.onward(side, way, chip, (chip >= 0) & (chip < chips))

    def toward(self, chip):
        k = self.links
        for side, way in enumerate((1, -1)):
            self.onward(side, way, chip, chip > k.z if way > 0 else chip < k.z)

    def last(self):
        k, chips = self.links, self.links.chips
        for side, inner in enumerate((k.z > 0, k.z < chips - 1)):

            def add():
                block = self.place(side, k.z, k.z)
                k.arrived(None, block, self.recvs + (1 + side) * chips + k.z)
                add_rows(self.held(k.z), self.held(k.z), block)

            pl.when(inner)(add)


class Exchange:
    def __init__(self, links):
        self.links = links
        self.sends, self.recvs = links.take(links.ranks, links.ranks)

    def start(self, source, target):
        k = self.links
        self.own = k.move(source(k.f), target(k.f))
        for i in range(1, k.ranks):
            other = lax.rem(k.f + i, k.ranks)
            k.send(
                None, source(other), target(k.f), self.sends + other, self.recvs + k.f, (k.d, other)
            )

    def finish(self, target, own=True):
        k = self.links
        if own:
            self.own()
        for i in range(1, k.ranks):
            other = lax.rem(k.f + i, k.ranks)
            k.arrived(None, target(other), self.recvs + other)

    def start_piece(self, rank, source, target):
        k = self.links
        k.send(
            k.f != rank, source, target(k.f), self.sends + rank, self.recvs + k.f, (k.d, rank)
        )
        here = lambda: pltpu.make_async_copy(source, target(k.f), k.sends.at[self.sends + rank])
        pl.when(k.f == rank)(lambda: here().start())
        k.pending.append(lambda: pl.when(k.f == rank)(lambda: here().wait()))


class GroupGather:
    def __init__(self, links, view, high):
        self.links, self.view, self.high = links, view, high
        count = links.groups - 1
        self.sends, self.recvs = links.take(count, count)

    def flip(self, stage):
        k = self.links
        low, up = 1 << stage, 1 << (k.bits - 1 - stage)
        size = low + self.high * (up - low)
        return (1 - 2 * lax.rem(lax.div(k.d, size), 2)) * size

    def places(self, stage):
        places = [self.links.d]
        for past in range(stage):
            places = places + [place + self.flip(past) for place in places]
        return places

    def start(self, stage, source=None):
        k = self.links
        for i, place in enumerate(self.places(stage)):
            at = (1 << stage) - 1 + i
            target = self.view(place)
            k.send(
                None,
                target if source is None else source,
                target,
                self.sends + at,
                self.recvs + at,
                (k.d + self.flip(stage), k.f),
            )

    def arrivals(self, stage):
        return [place + self.flip(stage) for place in self.places(stage)]

    def wait(self, stage):
        for i, place in enumerate(self.arrivals(stage)):
            self.links.arrived(None, self.view(place), self.recvs + (1 << stage) - 1 + i)


class GroupScatter:
    def __init__(self, links, view, landed, high):
        self.links, self.view, self.landed = links, view, landed
        bits = list(range(links.bits))
        self.order = bits[::-1] if high else bits
        count = links.groups - 1
        self.sends, self.recvs = links.take(count, count)

    def base(self, stage):
        return sum(self.links.groups >> (s + 1) for s in range(stage))

    def sources(self, stage, flip):
        k = self.links
        b = self.order[stage]
        value = 1 - k.bit(b) if flip else k.bit(b)
        if stage > 0:
            count = k.groups >> (stage + 1)
            return [self.landed(self.base(stage - 1) + value + 2 * i) for i in range(count)]
        places = [value * (1 << b)]
        for b in self.order[1:]:
            places = places + [place + (1 << b) for place in places]
        return [self.view(place) for place in places]

    def start(self, stage):
        k = self.links
        for i, source in enumerate(self.sources(stage, True)):
            at = self.base(stage) + i
            k.send(
                None,
                source,
                self.landed(at),
                self.sends + at,
                self.recvs + at,
                k.partner(self.order[stage]),
            )

    def wait(self, stage, target=None):
        k = self.links
        for i, source in enumerate(self.sources(stage, False)):
            at = self.base(stage) + i
            k.arrived(None, self.landed(at), self.recvs + at)
            add_rows(self.landed(at) if target is None else target, source, self.landed(at))
        return self.landed(self.base(stage))


def row_loop(rows, action, step=16, first=0):
    @pl.loop(0, rows // step)
    def _(i):
        action(pl.ds(pl.multiple_of(first + i * step, step), step))


def spaced(events, blocks):
    count = len(events)
    return [events[b * count // blocks : (b + 1) * count // blocks] for b in range(blocks)]


def head_places(ranks, rank_heads, split):
    places = {}
    for rank in range(ranks):
        for b in range(rank_heads):
            head = (rank % split * rank_heads + b) * (ranks // split) + rank // split
            places[head] = (rank, b)
    return [places[head] for head in range(HEADS)]


def attend_kernel(
    groups, ranks, rank_heads, slice_width, packed, traffic,
    lengths, tokens, w_query, w_key, w_value, gains, out_w, down_w, w_gate, w_up, cosine, sine,
    x_all, qkv, gain_rows, normed, queries, keys, values, attended, log_totals,
    attended_all, gate_up, out_all, down_all,
    gains_all, values_t, qkv_out, gate_up_out, sends, recvs,
):
    k = Links(groups, ranks, sends, recvs)
    places = head_places(ranks, rank_heads, max(1, HEAD_DIM // out_w.shape[0]))
    for rank in range(ranks):
        mine = [[h for h in range(HEADS) if places[h] == (rank, b)][0] for b in range(rank_heads)]
        for n, ref in enumerate((w_query, w_key, w_value)):
            for b in range(0, rank_heads, 2):
                halves = [
                    ref[:, head * HEAD_DIM : (head + 1) * HEAD_DIM].astype(F32)
                    for head in mine[b : b + 2]
                ]
                at = (n * rank_heads + b) * HEAD_DIM
                qkv_out[rank, :, at : at + 2 * HEAD_DIM] = jnp.concatenate(halves, 1).astype(BF16)
    length = lengths[0]
    cols, rows = queries.shape[1], tokens.shape[0]
    depth, half = gate_up_out.shape[1], ranks // 2
    pieces = depth // 16
    blocks = values_t.shape[0]
    split = max(1, HEAD_DIM // out_w.shape[0])
    down_half = down_w.shape[0] // 2

    def unit(group, rank):
        return (
            (lax.div(rank, split) * split + lax.div(group, rank_heads)) * rank_heads
            + lax.rem(group, rank_heads)
        ) * split + lax.rem(rank, split)

    def out_block(group, rank):
        return out_all.at[unit(group, rank)]

    def attended_block(i, rank):
        return attended_all.at[
            pl.ds(i * BLOCK, BLOCK), pl.ds(pl.multiple_of(rank * cols, cols), cols)
        ]

    x_line = LineGather(k, lambda rank: x_all.at[pl.ds(pl.multiple_of(rank * rows, 16), rows)])
    out_line = LineGather(k, lambda rank: out_block(k.d, rank))
    lines = [LineGather(k, lambda rank, i=i: attended_block(i, rank)) for i in range(blocks)]
    gains_ex, qkv_ex = Exchange(k), Exchange(k)
    exchanges = [Exchange(k) for _ in range(pieces)]
    downs = [
        GroupGather(k, lambda group, h=h: down_all.at[group, pl.ds(h * down_half, down_half)], h)
        for h in range(2)
    ]
    late = [
        GroupGather(k, lambda group, h=h, ref=ref: ref.at[group, pl.ds(h * half, half)], h)
        for ref in (qkv, gains_all)
        for h in range(2)
    ]
    out_gathers = [
        GroupGather(k, lambda group, r=r: out_block(group, k.c * half + r), k.c) for r in range(half)
    ]
    gathers = [
        [
            GroupGather(
                k,
                lambda group, h=h, q=q: gate_up.at[group, pl.ds(h * half, half), pl.ds(q * 16, 16)],
                h,
            )
            for h in range(2)
        ]
        for q in range(pieces)
    ]
    over_sends, over_recvs = k.take(half * groups, half * groups)

    def onward(several, stage):
        for gather in several:
            gather.wait(stage)
            if stage + 1 < k.bits:
                gather.start(stage + 1)

    def out_onward(stage):
        for r, gather in enumerate(out_gathers):
            gather.wait(stage)
            if stage + 1 < k.bits:
                gather.start(stage + 1)
            for group in gather.arrivals(stage):
                block = out_block(group, k.c * half + r)
                at = r * groups + group
                k.send(None, block, block, over_sends + at, over_recvs + at, k.sibling)

    units_from = w_gate if packed else gate_up_out

    def send_out(q):
        part = pl.ds(q * 16, 16)
        exchanges[q].start(
            lambda rank: units_from.at[rank, part], lambda rank: gate_up.at[k.d, rank, part]
        )

    def came_in(q):
        exchanges[q].finish(lambda rank: gate_up.at[k.d, rank, pl.ds(q * 16, 16)])
        for gather in gathers[q]:
            gather.start(0)
        if q + 2 < pieces:
            send_out(q + 2)

    gains_in = lambda rank: gains_all.at[k.d, rank]
    qkv_in = lambda rank: qkv.at[k.d, rank]
    k.barrier()
    gains_ex.start(lambda rank: gains, gains_in)
    qkv_ex.start(lambda rank: qkv_out.at[rank], qkv_in)
    for h, gather in enumerate(downs):
        gather.start(0, down_w.at[pl.ds(h * down_half, down_half)])
    own_down = k.move(down_w, down_all.at[k.d])
    if not packed:
        units = gate_up_out.shape[2] // 2
        share = units // groups
        for rank in range(ranks):
            for group in range(groups):
                at = (group * ranks + rank) * share
                for n, ref in enumerate((w_gate, w_up)):
                    start = n * units + group * share
                    gate_up_out[rank, :, start : start + share] = ref[:, at : at + share]
    gains_ex.finish(gains_in)
    qkv_ex.finish(qkv_in)
    out_line.start(out_w)
    x_line.start(tokens)
    own = [
        k.move(out_w, out_block(k.d, k.f)),
        k.move(tokens, x_all.at[pl.ds(pl.multiple_of(k.f * rows, 16), rows)]),
    ]
    for gather in late:
        gather.start(0)
    own_down()
    onward(downs, 0)
    for wait in own:
        wait()
    out_line.step(1)
    x_line.step(1)
    onward(late, 0)
    for reach in range(2, k.chips):
        out_line.step(reach)
    out_line.finish()
    for gather in out_gathers:
        gather.start(0)
    for q in range(min(2, pieces)):
        x_line.step(2 + q)
        send_out(q)
    for reach in range(2 + min(2, pieces), k.chips):
        x_line.step(reach)
    for stage in range(1, k.bits):
        onward(late, stage)
    out_onward(0)
    for stage in range(1, k.bits):
        onward(downs, stage)
    x_line.finish()
    traffic.put(0, 1)
    members = 128 // slice_width
    for at in range(groups * ranks // members):
        group, first = at * members // ranks, at * members % ranks
        tile = gains_all[group, first].astype(F32)
        for other in range(1, members):
            tile = tile + gains_all[group, first + other].astype(F32)
        gain_rows[:, at * 128 : (at + 1) * 128] = tile[:8]

    events = []
    for q in range(pieces):
        events.append(lambda q=q: came_in(q))
        if q > 0:
            events.append(lambda q=q: onward(gathers[q - 1], 0))
    events.append(lambda: onward(gathers[pieces - 1], 0))
    if k.bits == 2:
        events.append(lambda: out_onward(1))
    plan = spaced(events, 2 * blocks)
    own = []
    for i in range(blocks):
        query = project_block(
            i, x_all, gain_rows, qkv, cosine, sine, normed, queries, keys, values, values_t
        )
        for event in plan[2 * i]:
            event()
        attend_block(i, rank_heads, query, keys, values_t, length, attended, log_totals)
        mine = attended.at[pl.ds(i * BLOCK, BLOCK)]
        lines[i].start(mine)
        own.append(k.move(mine, attended_block(i, k.f)))
        for reach in range(1, k.chips):
            if i - reach >= 0:
                lines[i - reach].step(reach)
        for event in plan[2 * i + 1]:
            event()
    for i in range(blocks, blocks + k.chips - 1):
        for reach in range(1, k.chips):
            if 0 <= i - reach < blocks:
                lines[i - reach].step(reach)
    traffic.put()
    for stage in range(1, k.bits):
        if k.bits > 2:
            out_onward(stage)
        for several in gathers:
            onward(several, stage)
    for r in range(half):
        for i in range(1, groups):
            group = lax.rem(k.d + i, groups)
            block = out_block(group, (1 - k.c) * half + r)
            k.arrived(None, block, over_recvs + r * groups + group)
    for wait in own:
        wait()
    for line in lines:
        line.finish()
    k.finish()


def far_first(k, t):
    total = 0
    for z in range(k.chips):
        order = sorted(range(k.chips), key=lambda chip: -abs(chip - z))
        total = total + jnp.where(k.z == z, order[t], 0)
    return total


def feed_forward_kernel(
    groups, ranks, traffic, attended_all, x_all, out_all, gate_up_all, down_all, grad_out, gain_rows,
    grad_out_all, hidden, output, normed, mixed, grad_gate_up, parts,
    out_w, gate_up, down_w, attended_in, x_in, grad_in, hidden_b, normed_b, gates, mixed_b, grad_b, down_b, parts_b,
    held, landed, local, sends, recvs,
):
    k = Links(groups, ranks, sends, recvs)
    chips, pair = k.chips, hidden_b.shape[0]
    rows = pair // 2
    width, units = out_w.shape[0], down_w.shape[0]
    step = 1024
    chunk = 512
    line = LineGather(k, lambda rank: grad_out_all.at[rank])
    scatter = LineScatter(
        k, None, lambda chip: held.at[chip], lambda slot: landed.at[slot]
    )
    weights = [
        pltpu.make_async_copy(ref, buffer, local.at[n])
        for n, (ref, buffer) in enumerate(((out_all, out_w), (gate_up_all, gate_up), (down_all, down_w)))
    ]
    order = [far_first(k, t) for t in range(chips)]

    def span(t):
        return pl.ds(pl.multiple_of(order[t] * pair, 16), pair)

    def loads(t):
        return [
            pltpu.make_async_copy(ref.at[span(t)], buffer.at[t % 2], local.at[3 + 2 * n + t % 2])
            for n, (ref, buffer) in enumerate(((attended_all, attended_in), (x_all, x_in)))
        ]

    def fetches(t):
        return [
            pltpu.make_async_copy(
                grad_out_all.at[order[chips - 1 - t] * 2 + c],
                grad_in.at[t % 2, pl.ds(c * rows, rows)],
                local.at[7 + 2 * (t % 2) + c],
            )
            for c in range(2)
        ]

    def store(n, buffer, ref, t):
        return pltpu.make_async_copy(buffer, ref.at[span(t)], local.at[11 + n])

    for load in loads(0) + weights:
        load.start()
    k.barrier()
    line.start(grad_out)
    own = k.move(grad_out, grad_out_all.at[k.f])
    weights[0].wait()
    gone = []
    for t in range(chips):
        if t + 1 < chips:
            for load in loads(t + 1):
                load.start()
        for load in loads(t):
            load.wait()

        @pl.loop(0, width // step)
        def _(c):
            part = pl.ds(pl.multiple_of(c * step, step), step)
            hidden_b[:, part] = x_in[t % 2, :, part].astype(F32) + dot(
                attended_in[t % 2], out_w[:, part]
            )

        if t > 0:
            store(0, normed_b, normed, t - 1).wait()

        def normalise(part):
            total = hidden_b[part, :]
            normed_b[part, :] = (total * inverse_rms(total) * gain_rows[1:2, :]).astype(BF16)

        row_loop(pair, normalise)
        store(0, normed_b, normed, t).start()
        if t == 0:
            weights[1].wait()
        if t == chips - 1:

            @pl.loop(0, rows // 16)
            def _(i):
                source = pl.ds(pl.multiple_of(k.c * rows + i * 16, 16), 16)
                hidden[pl.ds(pl.multiple_of(i * 16, 16), 16), :] = hidden_b[source, :]

        if t > 0:
            store(1, mixed_b, mixed, t - 1).wait()
        if t > 2:
            line.step(t - 1)
        here = span(t)

        @pl.loop(0, units // chunk)
        def _(u):
            part = pl.ds(pl.multiple_of(u * chunk, chunk), chunk)
            far = pl.ds(pl.multiple_of(units + u * chunk, chunk), chunk)
            gate = dot(normed_b[...], gate_up[:, part])
            up = dot(normed_b[...], gate_up[:, far])
            gates[here, part] = gate
            gates[here, far] = up
            mixed_b[:, part] = (gate / (1.0 + jnp.exp(-gate)) * up).astype(BF16)

        store(1, mixed_b, mixed, t).start()
        if t == 0:
            weights[2].wait()
        elif t > 1:
            gone[t - 2]()

        @pl.loop(0, width // step)
        def _(c):
            part = pl.ds(pl.multiple_of(c * step, step), step)
            down_b[t % 2, :, part] = dot(mixed_b[...], down_w[:, part]).astype(BF16)

        def core_rows(t, core):
            return down_b.at[t % 2, pl.ds(pl.multiple_of(core * rows, 16), rows)]

        gone.append(scatter.give(order[t], core_rows(t, 1 - k.c), later=False))
        if t > 0:
            scatter.pair(order[t - 1], core_rows(t - 1, k.c))
        if t == 1:
            line.step(1)
        if t % 2 == 1:
            scatter.step(t // 2)
    store(0, normed_b, normed, chips - 1).wait()
    store(1, mixed_b, mixed, chips - 1).wait()
    for wait in gone[-2:]:
        wait()
    own()
    line.over(order[chips - 1])
    for fetch in fetches(0):
        fetch.start()
    for t in range(chips):
        if t == 1:
            line.step(chips - 1)
        if t + 1 < chips:
            line.over(order[chips - 2 - t])
            for fetch in fetches(t + 1):
                fetch.start()
        for fetch in fetches(t):
            fetch.wait()
        near = chips - 1 - t
        if t > 0:
            store(2, grad_b, grad_gate_up, near + 1).wait()
        here = span(near)

        @pl.loop(0, units // chunk)
        def _(u):
            part = pl.ds(pl.multiple_of(u * chunk, chunk), chunk)
            far = pl.ds(pl.multiple_of(units + u * chunk, chunk), chunk)
            gate, up = gates[here, part], gates[here, far]
            grad_mixed = cols_inner(grad_in[t % 2], down_w[part, :])
            sigmoid = 1.0 / (1.0 + jnp.exp(-gate))
            grad_b[:, part] = (
                grad_mixed * up * (sigmoid * (1.0 + gate * (1.0 - sigmoid)))
            ).astype(BF16)
            grad_b[:, far] = (grad_mixed * (gate * sigmoid)).astype(BF16)

        store(2, grad_b, grad_gate_up, near).start()
        if t > 0:
            store(3, parts_b, parts, near + 1).wait()
        if t == 0:
            scatter.pair(order[chips - 1], down_b.at[(chips - 1) % 2, pl.ds(pl.multiple_of(k.c * rows, 16), rows)])
        if (chips + t) % 2 == 1 and (chips + t) // 2 < chips - 1:
            scatter.step((chips + t) // 2)

        @pl.loop(0, width // step)
        def _(c):
            part = pl.ds(pl.multiple_of(c * step, step), step)
            parts_b[:, part] = cols_inner(grad_b[...], gate_up[part, :]).astype(BF16)

        store(3, parts_b, parts, near).start()
    scatter.last()

    def out_rows(part):
        output[part] = (hidden[part] + held[k.z, part].astype(F32)).astype(BF16)

    row_loop(rows, out_rows)
    store(2, grad_b, grad_gate_up, 0).wait()
    store(3, parts_b, parts, 0).wait()
    k.finish()


def middle_kernel(
    groups, ranks, subs, traffic, parts, hidden, grad_out, gain_rows, normed, grad_gate_up, mixed, grad_out_all,
    grad_all, grad_hidden, sums, gate_up_sum, grad_down,
    mine, held, landed, rounded, tile, grad_w, gate_up_landed, local, sends, recvs,
):
    k = Links(groups, ranks, sends, recvs)
    rows = hidden.shape[0] // subs
    depth = grad_w.shape[2]
    step = 1024
    scatters, gathers = [], []
    for sub in range(subs):
        piece = pl.ds(sub * rows, rows)
        scatters.append(
            LineScatter(
                k,
                lambda chip, piece=piece: mine.at[chip, piece],
                lambda chip, piece=piece: held.at[chip, piece],
                lambda slot, piece=piece: landed.at[slot, piece],
            )
        )
        gathers.append(LineGather(k, lambda rank, piece=piece: grad_all.at[rank, piece]))
    gate_up_sums = [
        GroupScatter(
            k,
            lambda group, n=n: grad_w.at[group, n],
            lambda i, n=n: gate_up_landed.at[n, i],
            n % 2 == 1,
        )
        for n in range(ranks)
    ]
    per_group = ranks * depth // BLOCK
    per_tile = BLOCK // depth
    tiles = [(q, g) for q in range(per_group) for g in range(groups)]

    downs = mixed.shape[1] // BLOCK

    def load(i):
        ref, at = mixed, i - len(tiles)
        if i < len(tiles):
            ref, at = normed, tiles[i][1] * per_group + tiles[i][0]
        return pltpu.make_async_copy(
            ref.at[:, pl.ds(at * BLOCK, BLOCK)], tile.at[i % 2], local.at[i % 2]
        )

    def work(i):
        if i + 1 < len(tiles) + downs:
            load(i + 1).start()
        load(i).wait()
        if i >= len(tiles):
            flipped = tile[i % 2].astype(F32).T.astype(BF16)
            at = (i - len(tiles)) * BLOCK

            @pl.loop(0, grad_down.shape[1] // step)
            def _(c):
                part = pl.ds(pl.multiple_of(c * step, step), step)
                grad_down[at : at + BLOCK, part] = dot(flipped, grad_out_all[:, part]).astype(BF16)

            return
        q, g = tiles[i]
        flipped = tile[i % 2].astype(F32).T.astype(BF16)

        @pl.loop(0, grad_gate_up.shape[1] // step)
        def _(c):
            part = pl.ds(pl.multiple_of(c * step, step), step)
            total = dot(flipped, grad_gate_up[:, part]).astype(BF16)
            for n in range(per_tile):
                grad_w[g, q * per_tile + n, :, part] = total[n * depth : (n + 1) * depth]

        if g == groups - 1:
            for n in range(per_tile):
                gate_up_sums[q * per_tile + n].start(0)

    load(0).start()
    k.barrier()
    for sub, scatter in enumerate(scatters):
        scatter.start(lambda rank, sub=sub: parts.at[rank, pl.ds(sub * rows, rows)])
    sums[...] = jnp.zeros_like(sums)

    def rows_of(part):
        total = hidden[part]
        scale = inverse_rms(total)
        scaled = total * scale
        grad = held[k.z, part].astype(F32)
        sums[...] += jnp.sum(grad * scaled, 0, keepdims=True)
        grad_total = grad_out[part].astype(F32) + norm_back(grad * gain_rows[1:2, :], scaled, scale)
        grad_hidden[part] = grad_total
        rounded[part] = grad_total.astype(BF16)

    own = []
    hops = k.chips - 1
    early = len(tiles) // 4
    plan = spaced(list(range(early, len(tiles))), hops - 1) + [[]]
    plan = plan + spaced(list(range(len(tiles), len(tiles) + downs)), subs * hops)
    traffic.ready(5)
    for place in range(early):
        work(place)
    for turn in range(subs + 1):
        if turn < subs:
            scatters[turn].pairs()
        for i in range(hops):
            if turn < subs:
                scatters[turn].step(i)
            if turn > 0:
                gathers[turn - 1].step(i + 1)
            for place in plan[turn * hops + i]:
                if place == len(tiles):
                    traffic.ready(7)
                work(place)
            if turn == 1 and i == 0:
                for sums_of in gate_up_sums[: ranks // 2]:
                    sums_of.wait(0)
                    sums_of.start(1)
        if turn < subs:
            scatters[turn].last()
            row_loop(rows, rows_of, first=turn * rows)
            piece = pl.ds(turn * rows, rows)
            gathers[turn].start(rounded.at[piece])
            own.append(k.move(rounded.at[piece], grad_all.at[k.f, piece]))
        if turn == 1:
            for sums_of in gate_up_sums[ranks // 2 :]:
                sums_of.wait(0)
                sums_of.start(1)
    for stage in range(1, k.bits):
        for n, sums_of in enumerate(gate_up_sums):
            if stage + 1 < k.bits:
                sums_of.wait(stage)
                sums_of.start(stage + 1)
            else:
                sums_of.wait(stage, gate_up_sum.at[n])
    for gather in gathers:
        gather.finish()
    for wait in own:
        wait()
    k.finish()


def attend_back_kernel(
    groups, ranks, rank_heads, slice_width, traffic,
    lengths, out_all, normed, grad_rows, queries, keys, values, attended, log_totals,
    cosine, sine, qkv, gate_up_sum, grad_down, tokens, grad_hidden, gain_rows, sums_two,
    gate_up_grad, down_grad, qkv_grad, out_grad, grad_tokens, gain_grads,
    out_w, grad_qkv, keys_t, grad_keys, grad_values, down_landed, held, landed, parts_b, tile,
    grad_qkv_w, qkv_landed, grad_out_w, out_landed, sums, tiles, tiles_landed, tiles_sum, group_tiles,
    local, sends, recvs,
):
    k = Links(groups, ranks, sends, recvs)
    length = lengths[0]
    cols, width = queries.shape[1], grad_rows.shape[1]
    rows = tokens.shape[0]
    pair = 2 * rows
    blocks = keys_t.shape[0]
    depth = qkv_grad.shape[1]
    step = 512

    def group_sums(ref, landing, count):
        size = ref.shape[1] // count
        return [
            GroupScatter(
                k,
                lambda group, n=n: ref.at[group, pl.ds(n * size, size)],
                lambda i, n=n: landing.at[n, i],
                n % 2 == 1,
            )
            for n in range(count)
        ], size

    down_sums, down_size = group_sums(grad_down, down_landed, down_landed.shape[0])
    out_sums, out_size = group_sums(grad_out_w, out_landed, out_landed.shape[0])
    qkv_sums = [
        GroupScatter(
            k,
            lambda group, n=n: grad_qkv_w.at[group, n],
            lambda i, n=n: qkv_landed.at[n, i],
            n % 2 == 1,
        )
        for n in range(ranks)
    ]
    scatter = LineScatter(
        k, None, lambda chip: held.at[chip], lambda slot: landed.at[slot]
    )
    gate_up_ex, exchange, tile_exchange = Exchange(k), Exchange(k), Exchange(k)
    tile_sends, tile_recvs = k.take(groups, groups)
    gate_up_in = lambda rank: gate_up_grad.at[rank]
    qkv_in = lambda rank: qkv_grad.at[rank]

    def onward(several, stage):
        for sums_of in several:
            sums_of.wait(stage)
            sums_of.start(stage + 1)

    per_group = ranks * depth // BLOCK
    per_tile = BLOCK // depth
    work = [(q, g) for q in range(per_group) for g in range(groups)]

    def load(i):
        q, g = work[i]
        return pltpu.make_async_copy(
            normed.at[:, pl.ds((g * per_group + q) * BLOCK, BLOCK)], tile.at[i % 2], local.at[i % 2]
        )

    def weight_tile(i):
        q, g = work[i]
        if i + 1 < len(work):
            load(i + 1).start()
        load(i).wait()
        flipped = tile[i % 2].astype(F32).T.astype(BF16)
        for c in range(3):
            part = slice(c * cols, (c + 1) * cols)
            total = dot(flipped, grad_qkv[:, part]).astype(BF16)
            for n in range(per_tile):
                grad_qkv_w[g, q * per_tile + n, :, part] = total[n * depth : (n + 1) * depth]
        if g == groups - 1:
            for n in range(per_tile):
                qkv_sums[q * per_tile + n].start(0)

    before = []

    def parts_of(t):
        chip = far_first(k, t)
        here = pl.ds(pl.multiple_of(chip * pair, 16), pair)
        if t > 1:
            before[t - 2]()
            before[t - 2] = lambda: None

        @pl.loop(0, width // step)
        def _(c):
            part = pl.ds(pl.multiple_of(c * step, step), step)
            parts_b[t % 2, :, part] = cols_inner(grad_qkv[here, :], qkv[part, :]).astype(BF16)

        def core_rows(core):
            return parts_b.at[t % 2, pl.ds(pl.multiple_of(core * rows, 16), rows)]

        before.append(scatter.give(chip, core_rows(1 - k.c), later=False))
        return chip, core_rows(k.c)

    load(0).start()
    fetch = k.move(out_all.at[pl.ds(pl.multiple_of(k.f * cols, cols), cols)], out_w)
    k.barrier()
    traffic.ready(13)
    for sums_of in down_sums:
        sums_of.start(0)
    gate_up_ex.start(lambda rank: gate_up_sum.at[rank], gate_up_in)
    grad_keys[...] = jnp.zeros_like(grad_keys)
    grad_values[...] = jnp.zeros_like(grad_values)

    traffic.ready(5)

    @pl.loop(0, blocks)
    def _(i):
        block = pl.ds(pl.multiple_of(i * BLOCK, BLOCK), BLOCK)
        keys_t[i] = keys[block, :].astype(F32).T.astype(BF16)

    fetch()
    traffic.ready()

    def back_rows(i):
        attend_back_rows(
            i, rank_heads, grad_rows, out_w, queries, keys, keys_t, values, attended, length, log_totals,
            cosine, sine, grad_keys, grad_values, grad_qkv,
        )

    pl.loop(0, blocks - 1)(back_rows)
    for stage in range(k.bits - 1):
        onward(down_sums, stage)
    back_rows(blocks - 1)
    pl.loop(0, blocks)(
        lambda i: finish_back_rows(i, cosine, sine, grad_keys, grad_values, grad_qkv)
    )
    shares = spaced(list(range(len(work))), 2) + [[]] * k.chips
    given = None
    for t in range(k.chips):
        now = parts_of(t)
        if given is not None:
            scatter.pair(*given)
        given = now
        for i in shares[t]:
            weight_tile(i)
        if t == 1:
            scatter.step(0)
    scatter.pair(*given)

    out_rows = grad_out_w.shape[1]
    split = groups * out_rows // cols
    out_base = lax.rem(k.f, split) * (cols // out_rows)
    if split > 1:
        grad_out_w[...] = jnp.zeros_like(grad_out_w)

    @pl.loop(0, width // BLOCK)
    def _(t):
        part = pl.ds(pl.multiple_of(t * BLOCK, BLOCK), BLOCK)
        total = rows_inner(attended[...], grad_rows[:, part]).astype(BF16)
        for n in range(cols // out_rows):
            grad_out_w[out_base + n, :, part] = total[n * out_rows : (n + 1) * out_rows]

    for sums_of in out_sums:
        sums_of.start(0)
    for stage in range(k.bits - 1):
        onward(qkv_sums, stage)
        if stage == 0:
            scatter.step(1)
    for n, sums_of in enumerate(qkv_sums):
        exchange.start_piece(n, sums_of.wait(k.bits - 1), qkv_in)
        if n == ranks // 2 - 1:
            for i in range(2, k.chips - 1):
                scatter.step(i)
    for stage in range(k.bits - 1):
        onward(out_sums, stage)
    scatter.last()
    sums[...] = jnp.zeros_like(sums)

    def rows_of(part):
        total = tokens[part].astype(F32)
        scale = inverse_rms(total)
        scaled = total * scale
        grad = held[k.z, part].astype(F32)
        sums[...] += jnp.sum(grad * scaled, 0, keepdims=True)
        grad_tokens[part] = (
            grad_hidden[part] + norm_back(grad * gain_rows[0:1, :], scaled, scale)
        ).astype(BF16)

    row_loop(rows, rows_of)
    tiles[...] = jnp.zeros_like(tiles)
    for rank in range(ranks):
        for group in range(groups):
            at = (group * ranks + rank) * slice_width // 128 * 128
            tiles[rank, group, 0:1] = sums[:, at : at + 128]
            tiles[rank, group, 1:2] = sums_two[:, at : at + 128]
    tile_in = lambda rank: tiles_landed.at[rank]
    tile_exchange.start(lambda rank: tiles.at[rank], tile_in)
    for n, sums_of in enumerate(out_sums):
        sums_of.wait(k.bits - 1, out_grad.at[pl.ds(n * out_size, out_size)])
    for n, sums_of in enumerate(down_sums):
        sums_of.wait(k.bits - 1, down_grad.at[pl.ds(n * down_size, down_size)])
    tile_exchange.finish(tile_in)
    total = tiles_landed[0]
    for rank in range(1, ranks):
        total = total + tiles_landed[rank]
    tiles_sum[...] = total
    for i in range(1, groups):
        other = lax.rem(k.d + i, groups)
        k.send(
            None,
            tiles_sum.at[other],
            group_tiles.at[k.d],
            tile_sends + other,
            tile_recvs + k.d,
            (other, k.f),
        )
    group_tiles[k.d] = tiles_sum[k.d]
    for i in range(1, groups):
        other = lax.rem(k.d + i, groups)
        k.arrived(None, group_tiles.at[other], tile_recvs + other)
    total = group_tiles[0]
    for group in range(1, groups):
        total = total + group_tiles[group]
    gain_grads[...] = total
    for wait in before:
        wait()
    gate_up_ex.finish(gate_up_in)
    exchange.finish(qkv_in, own=False)
    k.finish()


def finish_kernel(
    groups, places, gate_up_grad, qkv_grad, grad_w_gate, grad_w_up, grad_w_query, grad_w_key, grad_w_value
):
    ranks, cols, units = qkv_grad.shape[0], qkv_grad.shape[2] // 3, gate_up_grad.shape[2] // 2
    part = units // groups
    for rank in range(ranks):
        for group in range(groups):
            at = (group * ranks + rank) * part
            for n, out in enumerate((grad_w_gate, grad_w_up)):
                start = n * units + group * part
                out[:, at : at + part] = gate_up_grad[rank, :, start : start + part].astype(F32)
    for n, out in enumerate((grad_w_query, grad_w_key, grad_w_value)):
        for head in range(0, HEADS, 2):
            halves = []
            for rank, b in places[head : head + 2]:
                start = n * cols + b * HEAD_DIM
                halves.append(qkv_grad[rank, :, start : start + HEAD_DIM].astype(F32))
            at = head * HEAD_DIM
            out[:, at : at + 2 * HEAD_DIM] = jnp.concatenate(halves, 1)


VMEM = pl.BlockSpec(memory_space=pltpu.VMEM)
ANY = pl.BlockSpec(memory_space=pl.ANY)
SMEM = pl.BlockSpec(memory_space=pltpu.SMEM)
LOAD, STORE = "load", "store"


class Traffic:
    def __init__(self, ins, outs):
        self.ins, self.outs, self.begun = ins, outs, []
        for load in ins.values():
            load.start()

    def ready(self, *places):
        for place in places or tuple(self.ins):
            self.ins.pop(place).wait()

    def put(self, *places):
        for place in places or tuple(self.outs):
            store = self.outs.pop(place)
            store.start()
            self.begun.append(store)

    def close(self):
        self.ready()
        self.put()
        for store in self.begun:
            store.wait()


def call(kernel, identity, ins, outs, scratch, semaphores, args, local=0):
    loads = [i for i, place in enumerate(ins) if place == LOAD]
    stores = [i for i, (_, _, place) in enumerate(outs) if place == STORE]

    def body(*refs):
        inputs, results = list(refs[: len(ins)]), list(refs[len(ins) : len(ins) + len(outs)])
        rest = refs[len(ins) + len(outs) :]
        own = len(scratch) + (local > 0)
        buffers, moves = rest[own : own + len(loads) + len(stores)], rest[-3]
        coming, going = {}, {}
        for n, i in enumerate(loads):
            coming[i] = pltpu.make_async_copy(inputs[i], buffers[n], moves.at[n])
            inputs[i] = buffers[n]
        for n, i in enumerate(stores, len(loads)):
            going[i] = pltpu.make_async_copy(buffers[n], results[i], moves.at[n])
            results[i] = buffers[n]
        traffic = Traffic(coming, going)
        kernel(traffic, *inputs, *results, *rest[:own], *rest[-2:])
        traffic.close()

    return pl.pallas_call(
        body,
        out_shape=[jax.ShapeDtypeStruct(shape, kind) for shape, kind, _ in outs],
        in_specs=[ANY if place == LOAD else place for place in ins],
        out_specs=[ANY if place == STORE else place for _, _, place in outs],
        scratch_shapes=[pltpu.VMEM(shape, kind) for shape, kind in scratch]
        + [pltpu.SemaphoreType.DMA((local,))] * (local > 0)
        + [pltpu.VMEM(args[i].shape, args[i].dtype) for i in loads]
        + [pltpu.VMEM(outs[i][0], outs[i][1]) for i in stores]
        + [pltpu.SemaphoreType.DMA((max(1, len(loads) + len(stores)),))]
        + [pltpu.SemaphoreType.DMA((semaphores,))] * 2,
        compiler_params=pltpu.CompilerParams(
            collective_id=identity, has_side_effects=True, vmem_limit_bytes=61 * 1024 * 1024
        ),
    )(*args)


def build(groups, ranks):
    def body(
        tokens, cotangent, lengths, norm_attn, w_query, w_key, w_value, w_output, norm_mlp, w_gate, w_up, w_down
    ):
        rows, width = tokens.shape
        depth = w_query.shape[0]
        count = rows * ranks
        rank_heads = HEADS // ranks
        hidden_part = w_down.shape[0]
        out_rows = w_output.shape[0]
        split = max(1, HEAD_DIM // out_rows)
        rank = lax.axis_index("fsdp")

        def heads_out(weight):
            shaped = weight.reshape(depth, split, rank_heads, ranks // split, HEAD_DIM)
            return shaped.transpose(3, 1, 0, 2, 4).reshape(ranks, depth, rank_heads * HEAD_DIM)

        def heads_in(pieces):
            shaped = pieces.reshape(ranks // split, split, depth, rank_heads, HEAD_DIM)
            return shaped.transpose(2, 1, 3, 0, 4).reshape(depth, HEADS * HEAD_DIM)

        def units_out(weight):
            shaped = weight.reshape(depth, groups, ranks, hidden_part)
            return shaped.transpose(2, 0, 1, 3).reshape(ranks, depth, groups * hidden_part)

        def units_in(pieces):
            shaped = pieces.reshape(ranks, depth, groups, hidden_part)
            return shaped.transpose(1, 2, 0, 3).reshape(depth, groups * ranks * hidden_part)

        span = [[base * split + i for i in range(split)] for base in range(ranks // split)]

        head_cols = rank_heads * HEAD_DIM
        unit_cols = groups * hidden_part
        chips = ranks // 2
        slice_width = norm_attn.shape[0]
        packed = hidden_part % 128 != 0
        gate_up_shape = (ranks, depth, 2 * unit_cols)
        if packed:
            feeds = (jnp.concatenate([units_out(w) for w in (w_gate, w_up)], -1), w_up)
        else:
            feeds = (w_gate, w_up)
        place = (lax.axis_index("dp") * ranks + rank) * slice_width % 128
        gains = lax.dynamic_update_slice(
            jnp.zeros((16, 128), BF16), jnp.stack([norm_attn, norm_mlp]), (0, place)
        )
        cosine, sine = (jnp.asarray(table) for table in wide_tables(count))
        blocks = count // BLOCK
        heads_shape = ((count, head_cols), BF16, STORE)
        (
            x_all, qkv, gain_rows, normed_one, queries, keys, values, attended, log_totals,
            attended_all, gate_up, out_all, down_w,
        ) = call(
            functools.partial(attend_kernel, groups, ranks, rank_heads, slice_width, packed),
            5,
            [SMEM] + [VMEM] * 11,
            [
                ((count, width), BF16, STORE),
                ((groups, ranks, depth, 3 * head_cols), BF16, STORE),
                ((8, width), F32, VMEM),
                ((count, width), BF16, STORE),
            ]
            + [heads_shape] * 4
            + [
                ((blocks, rank_heads, BLOCK), F32, STORE),
                ((count, width), BF16, ANY),
                ((groups,) + gate_up_shape, BF16, ANY),
                ((groups * ranks, out_rows, width), BF16, ANY),
                ((groups,) + w_down.shape, BF16, ANY),
            ],
            [
                ((groups, ranks, 16, 128), BF16),
                ((blocks, head_cols, BLOCK), BF16),
                ((ranks, depth, 3 * head_cols), BF16),
                (gate_up_shape, BF16),
            ],
            448,
            (lengths, tokens, w_query, w_key, w_value, gains, w_output, w_down) + feeds + (cosine, sine),
        )
        qkv = qkv.reshape(width, -1)
        gate_up = gate_up.reshape(width, -1)
        out_all = out_all.reshape(width, width)
        down_w = down_w.reshape(-1, width)
        own_places = rank * rows + jnp.arange(rows, dtype=jnp.int32)
        grad_out = jnp.where(own_places[:, None] < lengths[0], cotangent, jnp.zeros((), BF16))
        pair = 2 * rows
        line_scratch = [
            ((chips, rows, width), BF16),
            ((chips, rows, width), BF16),
            ((chips + 1, rows, width), BF16),
        ]
        grad_out_all, hidden, output, normed_two, mixed, grad_gate_up, parts = call(
            functools.partial(feed_forward_kernel, groups, ranks),
            2,
            [ANY] * 5 + [VMEM] * 2,
            [
                ((ranks, rows, width), BF16, ANY),
                ((rows, width), F32, VMEM),
                ((rows, width), BF16, VMEM),
                ((count, width), BF16, ANY),
                ((count, unit_cols), BF16, ANY),
                ((count, 2 * unit_cols), BF16, ANY),
                ((count, width), BF16, ANY),
            ],
            [
                ((width, width), BF16),
                ((width, 2 * unit_cols), BF16),
                ((unit_cols, width), BF16),
                ((2, pair, width), BF16),
                ((2, pair, width), BF16),
                ((2, pair, width), BF16),
                ((pair, width), F32),
                ((pair, width), BF16),
                ((count, 2 * unit_cols), F32),
                ((pair, unit_cols), BF16),
                ((pair, 2 * unit_cols), BF16),
                ((2, pair, width), BF16),
                ((pair, width), BF16),
            ]
            + line_scratch[1:],
            128,
            (attended_all, x_all, out_all, gate_up, down_w, grad_out, gain_rows),
            local=15,
        )
        grad_hidden_all, grad_hidden, sums_two, gate_up_sum, grad_down = call(
            functools.partial(middle_kernel, groups, ranks, 2),
            3,
            [ANY] + [VMEM] * 3 + [ANY, LOAD, ANY, LOAD],
            [
                ((ranks, rows, width), BF16, ANY),
                ((rows, width), F32, VMEM),
                ((1, width), F32, VMEM),
                ((ranks, depth, 2 * unit_cols), BF16, VMEM),
                ((unit_cols, width), BF16, STORE),
            ],
            line_scratch
            + [
                ((rows, width), BF16),
                ((2, count, BLOCK), BF16),
                ((groups, ranks, depth, 2 * unit_cols), BF16),
                ((ranks, groups - 1, depth, 2 * unit_cols), BF16),
            ],
            160,
            (
                parts.reshape(ranks, rows, width),
                hidden,
                grad_out,
                gain_rows,
                normed_two,
                grad_gate_up,
                mixed,
                grad_out_all.reshape(count, width),
            ),
            local=2,
        )
        down_pieces, out_pieces = 4, 2
        out_place = out_rows * split
        tile = (8, 128)
        grad_gate_up_w, grad_w_down, grad_qkv_w, grad_w_output, grad_tokens, sums = call(
            functools.partial(attend_back_kernel, groups, ranks, rank_heads, slice_width),
            6,
            [SMEM, ANY, ANY] + [LOAD] * 9 + [ANY, LOAD] + [VMEM] * 4,
            [
                ((ranks, depth, 2 * unit_cols), BF16, ANY),
                ((hidden_part, width), F32, VMEM),
                ((ranks, depth, 3 * head_cols), BF16, ANY),
                ((out_place, width), F32, VMEM),
                ((rows, width), BF16, VMEM),
                (tile, F32, VMEM),
            ],
            [
                ((head_cols, width), BF16),
                ((count, 3 * head_cols), BF16),
                ((blocks, head_cols, BLOCK), BF16),
                ((count, head_cols), F32),
                ((count, head_cols), F32),
                ((down_pieces, groups - 1, hidden_part // down_pieces, width), BF16),
            ]
            + line_scratch[1:]
            + [
                ((2, pair, width), BF16),
                ((2, count, BLOCK), BF16),
                ((groups, ranks, depth, 3 * head_cols), BF16),
                ((ranks, groups - 1, depth, 3 * head_cols), BF16),
                ((groups, out_place, width), BF16),
                ((out_pieces, groups - 1, out_place // out_pieces, width), BF16),
                ((1, width), F32),
                ((ranks, groups) + tile, F32),
                ((ranks, groups) + tile, F32),
                ((groups,) + tile, F32),
                ((groups,) + tile, F32),
            ],
            192,
            (
                lengths,
                out_all,
                normed_one,
                grad_hidden_all.reshape(count, width),
                queries,
                keys,
                values,
                attended,
                log_totals,
                cosine,
                sine,
                qkv,
                gate_up_sum,
                grad_down.reshape(groups, hidden_part, width),
                tokens,
                grad_hidden,
                gain_rows,
                sums_two,
            ),
            local=2,
        )
        if split > 1:
            grad_w_output = lax.psum_scatter(
                grad_w_output, "fsdp", scatter_dimension=0, tiled=True, axis_index_groups=span
            )
        if hidden_part % 128 == 0:
            wide, narrow = (
                jax.ShapeDtypeStruct((depth, size), F32) for size in (w_gate.shape[1], width)
            )
            grad_w_gate, grad_w_up, grad_w_query, grad_w_key, grad_w_value = pl.pallas_call(
                functools.partial(finish_kernel, groups, head_places(ranks, rank_heads, split)),
                out_shape=[wide, wide, narrow, narrow, narrow],
                in_specs=[VMEM] * 2,
                out_specs=[VMEM] * 5,
                compiler_params=pltpu.CompilerParams(vmem_limit_bytes=32 * 1024 * 1024),
            )(grad_gate_up_w, grad_qkv_w)
        else:
            grad_w_gate = units_in(grad_gate_up_w[..., :unit_cols]).astype(F32)
            grad_w_up = units_in(grad_gate_up_w[..., unit_cols:]).astype(F32)
            grad_w_query, grad_w_key, grad_w_value = (
                heads_in(grad_qkv_w[..., i * head_cols : (i + 1) * head_cols]).astype(F32)
                for i in range(3)
            )
        place = (lax.axis_index("dp") * ranks + rank) * slice_width % 128
        sums = lax.dynamic_slice_in_dim(sums, place, slice_width, 1)
        return (
            output,
            grad_tokens,
            sums[0],
            grad_w_query,
            grad_w_key,
            grad_w_value,
            grad_w_output,
            sums[1],
            grad_w_gate,
            grad_w_up,
            grad_w_down,
        )

    return body


def solution(mesh):
    both = P(("dp", "fsdp"))
    rows = P(("dp", "fsdp"), None)
    return jax.shard_map(
        build(mesh.shape["dp"], mesh.shape["fsdp"]),
        mesh=mesh,
        in_specs=(rows, rows, P("dp"), both, rows, rows, rows, rows, both, rows, rows, rows),
        out_specs=(rows, rows, both, rows, rows, rows, rows, both, rows, rows, rows),
        check_vma=False,
    )
```

```python
import functools

import jax
import jax.numpy as jnp
import numpy as np
from jax import lax
from jax.experimental import pallas as pl
from jax.experimental.pallas import tpu as pltpu
from jax.sharding import PartitionSpec as P

HEADS = 32
HEAD_DIM = 64


EPSILON = 1e-05
THETA = 130000.0
BF16 = jnp.bfloat16
F32 = jnp.float32


def dot(left, right):
    return jnp.dot(left, right, preferred_element_type=F32)


def rows_inner(left, right):
    return lax.dot_general(left, right, (((0,), (0,)), ((), ())), preferred_element_type=F32)


def cols_inner(left, right):
    return lax.dot_general(left, right, (((1,), (1,)), ((), ())), preferred_element_type=F32)


def inverse_rms(values):
    return lax.rsqrt(jnp.mean(values * values, -1, keepdims=True) + EPSILON)


def norm_back(grad_scaled, scaled, scale):
    return scale * (grad_scaled - scaled * jnp.mean(grad_scaled * scaled, -1, keepdims=True))


BLOCK = 256
SCALE = 0.125


def turn_halves(values, cosine, sine):
    width = values.shape[1]
    half = HEAD_DIM // 2
    lane = lax.broadcasted_iota(jnp.int32, values.shape, 1)
    ahead = pltpu.roll(values, width - half, 1)
    behind = pltpu.roll(values, half, 1)
    return values * cosine + jnp.where(lane % HEAD_DIM < half, ahead, behind) * sine


def wide_tables(count):
    half = HEAD_DIM // 2
    inverse = np.float32(THETA) ** (-np.arange(half, dtype=np.float32) * np.float32(2.0) / HEAD_DIM)
    angles = np.arange(count, dtype=np.float32)[:, None] * inverse.astype(np.float32)[None, :]
    cosine, sine = np.cos(angles).astype(np.float32), np.sin(angles).astype(np.float32)
    return np.concatenate([cosine] * 4, -1), np.concatenate([-sine, sine] * 2, -1)


def table_rows(table, block, width):
    return jnp.concatenate([table[block, :]] * (width // 128), 1)


def key_bias(j, length):
    place = j * BLOCK + lax.broadcasted_iota(jnp.int32, (BLOCK, 1), 0)
    return jnp.where(place < length, 0.0, -1000000000.0)


def head_rows(values, head):
    row = lax.broadcasted_iota(jnp.int32, values.shape, 0)
    return jnp.where((row >= head * HEAD_DIM) & (row < (head + 1) * HEAD_DIM), values, 0.0)


def future(shape):
    return lax.broadcasted_iota(jnp.int32, shape, 0) > lax.broadcasted_iota(jnp.int32, shape, 1)


def attend_block(i, rank_heads, queries, keys, values_t, length, attended, log_totals):
    queries_t = queries.T
    masked = [(head_rows(queries_t, h) * SCALE).astype(BF16) for h in range(rank_heads)]

    def chunk(j, carry, last):
        part = pl.ds(pl.multiple_of(j * BLOCK, BLOCK), BLOCK)
        key_part, bias_part = keys[part, :], key_bias(j, length)
        after = []
        for h in range(rank_heads):
            top, total, out = carry[h]
            scores = dot(key_part, masked[h]) + bias_part
            if last:
                scores = jnp.where(future(scores.shape), -1000000000.0, scores)
            new_top = jnp.maximum(top, jnp.max(scores, 0, keepdims=True))
            keep = jnp.exp(top - new_top)
            weights = jnp.exp(scores - new_top)
            total = total * keep + jnp.sum(weights, 0, keepdims=True)
            out = out * keep + dot(
                values_t[j, h * HEAD_DIM : (h + 1) * HEAD_DIM, :], weights.astype(BF16)
            )
            after.append((new_top, total, out))
        return tuple(after)

    carry = tuple(
        (
            jnp.full((1, BLOCK), -3.0e38, F32),
            jnp.zeros((1, BLOCK), F32),
            jnp.zeros((HEAD_DIM, BLOCK), F32),
        )
        for _ in range(rank_heads)
    )
    carry = lax.fori_loop(0, i, lambda j, c: chunk(j, c, False), carry)
    carry = chunk(i, carry, True)
    outs = []
    for h, (top, total, out) in enumerate(carry):
        log_totals[i, h : h + 1, :] = top + jnp.log(total)
        outs.append(out * (1.0 / total))
    attended[pl.ds(pl.multiple_of(i * BLOCK, BLOCK), BLOCK), :] = (
        jnp.concatenate(outs, 0).T.astype(BF16)
    )


def project_block(i, x, gain, qkv, cosine, sine, normed, queries, keys, values, values_t):
    cols = queries.shape[1]
    start = i * BLOCK

    def rows_of(part):
        rows = x[part, :].astype(F32)
        normed[part, :] = (rows * inverse_rms(rows) * gain[0:1, :]).astype(BF16)

    pl.loop(0, BLOCK // 16)(
        lambda t: rows_of(pl.ds(pl.multiple_of(start + t * 16, 16), 16))
    )
    block = pl.ds(pl.multiple_of(start, BLOCK), BLOCK)
    rows = normed[block, :]

    def weight(n):
        return qkv[:, :, :, n * cols : (n + 1) * cols].reshape(x.shape[1], cols)

    cos, sin = table_rows(cosine, block, cols), table_rows(sine, block, cols)
    rounded = turn_halves(dot(rows, weight(0)), cos, sin).astype(BF16)
    queries[block, :] = rounded
    keys[block, :] = turn_halves(dot(rows, weight(1)), cos, sin).astype(BF16)
    value = dot(rows, weight(2))
    values[block, :] = value.astype(BF16)
    values_t[i] = value.T.astype(BF16)
    return rounded.astype(F32)


def lanes_of(values, head):
    lane = lax.broadcasted_iota(jnp.int32, values.shape, 1)
    return jnp.where((lane >= head * HEAD_DIM) & (lane < (head + 1) * HEAD_DIM), values, 0.0)


def attend_back_block(
    i, rank_heads, queries, keys, keys_t, values, attended, grad, length, log_totals, grad_keys, grad_values
):
    block = pl.ds(pl.multiple_of(i * BLOCK, BLOCK), BLOCK)
    query = queries[block, :].astype(F32) * SCALE
    query_t, grad_t = query.T, grad.T
    product = attended[block, :].astype(F32).T * grad_t
    masked_q = [head_rows(query_t, h).astype(BF16) for h in range(rank_heads)]
    masked_g = [head_rows(grad_t, h).astype(BF16) for h in range(rank_heads)]
    stacked_q = jnp.concatenate([lanes_of(query, h).astype(BF16) for h in range(rank_heads)], 0)
    stacked_g = jnp.concatenate([lanes_of(grad, h).astype(BF16) for h in range(rank_heads)], 0)
    deltas = [
        jnp.sum(product[h * HEAD_DIM : (h + 1) * HEAD_DIM], 0, keepdims=True)
        for h in range(rank_heads)
    ]
    totals = [log_totals[i, h : h + 1, :] for h in range(rank_heads)]

    def chunk(j, carry, last):
        part = pl.ds(pl.multiple_of(j * BLOCK, BLOCK), BLOCK)
        key_part, value_part, bias_part = keys[part, :], values[part, :], key_bias(j, length)
        after, weights_all, grads_all = [], [], []
        for h in range(rank_heads):
            scores = dot(key_part, masked_q[h]) + bias_part
            if last:
                scores = jnp.where(future(scores.shape), -1000000000.0, scores)
            weights = jnp.exp(scores - totals[h])
            grad_scores = weights * (dot(value_part, masked_g[h]) - deltas[h])
            weights_all.append(weights.astype(BF16))
            grads_all.append(grad_scores.astype(BF16))
            after.append(
                carry[h] + dot(keys_t[j, h * HEAD_DIM : (h + 1) * HEAD_DIM, :], grads_all[-1])
            )
        grad_values[part, :] += dot(jnp.concatenate(weights_all, 1), stacked_g)
        grad_keys[part, :] += dot(jnp.concatenate(grads_all, 1), stacked_q)
        return tuple(after)

    carry = tuple(jnp.zeros((HEAD_DIM, BLOCK), F32) for _ in range(rank_heads))
    carry = lax.fori_loop(0, i, lambda j, c: chunk(j, c, False), carry)
    carry = chunk(i, carry, True)
    return jnp.concatenate(carry, 0).T * SCALE


def attend_back_rows(
    i, rank_heads, grad_hidden, out_w, queries, keys, keys_t, values, attended, length, log_totals,
    cosine, sine, grad_keys, grad_values, grad_qkv,
):
    block = pl.ds(pl.multiple_of(i * BLOCK, BLOCK), BLOCK)
    cols = queries.shape[1]
    grad = cols_inner(grad_hidden[block, :], out_w[...]).astype(BF16).astype(F32)
    grad_q = attend_back_block(
        i, rank_heads, queries, keys, keys_t, values, attended, grad, length, log_totals, grad_keys, grad_values
    )
    grad_qkv[block, :cols] = turn_halves(
        grad_q, table_rows(cosine, block, cols), -table_rows(sine, block, cols)
    ).astype(BF16)


def finish_back_rows(i, cosine, sine, grad_keys, grad_values, grad_qkv):
    block = pl.ds(pl.multiple_of(i * BLOCK, BLOCK), BLOCK)
    cols = grad_keys.shape[1]
    grad_qkv[block, cols : 2 * cols] = turn_halves(
        grad_keys[block, :], table_rows(cosine, block, cols), -table_rows(sine, block, cols)
    ).astype(BF16)
    grad_qkv[block, 2 * cols :] = grad_values[block, :].astype(BF16)


MESH = pl.DeviceIdType.MESH


def when(cond, action):
    if cond is None:
        action()
    else:
        pl.when(cond)(action)


class Links:
    def __init__(self, groups, ranks, sends, recvs):
        self.groups, self.ranks, self.chips = groups, ranks, ranks // 2
        self.bits = groups.bit_length() - 1
        self.sends, self.recvs = sends, recvs
        self.used_sends = self.used_recvs = 0
        self.d, self.f = lax.axis_index("dp"), lax.axis_index("fsdp")
        self.z, self.c = lax.div(self.f, 2), lax.rem(self.f, 2)
        self.sibling = (self.d, self.z * 2 + 1 - self.c)
        self.pending = []

    def bit(self, b):
        return lax.rem(lax.div(self.d, 1 << b), 2)

    def partner(self, b):
        return (self.d + (1 - 2 * self.bit(b)) * (1 << b), self.f)

    def beside(self, way):
        return (self.d, self.f + 2 * way)

    def barrier(self):
        gate = pltpu.get_barrier_semaphore()
        for k in range(1, self.ranks):
            other = lax.rem(self.f + k, self.ranks)
            pl.semaphore_signal(gate, inc=1, device_id=(self.d, other), device_id_type=MESH)
        for k in range(1, self.groups):
            other = lax.rem(self.d + k, self.groups)
            pl.semaphore_signal(gate, inc=1, device_id=(other, self.f), device_id_type=MESH)
        pl.semaphore_wait(gate, self.ranks + self.groups - 2)

    def take(self, sends, recvs):
        first = (self.used_sends, self.used_recvs)
        self.used_sends += sends
        self.used_recvs += recvs
        return first

    def copy(self, source, target, send, recv, device):
        return pltpu.make_async_remote_copy(
            src_ref=source,
            dst_ref=target,
            send_sem=self.sends.at[send],
            recv_sem=self.recvs.at[recv],
            device_id=device,
            device_id_type=MESH,
        )

    def send(self, cond, source, target, send, recv, device, later=True):
        when(cond, lambda: self.copy(source, target, send, recv, device).start())
        gone = lambda: when(
            cond, lambda: self.copy(source, target, send, recv, device).wait_send()
        )
        if later:
            self.pending.append(gone)
        return gone

    def arrived(self, cond, target, recv):
        when(cond, lambda: self.copy(target, target, 0, recv, self.sibling).wait_recv())

    def move(self, source, target):
        send, _ = self.take(1, 0)
        make = lambda: pltpu.make_async_copy(source, target, self.sends.at[send])
        make().start()
        return lambda: make().wait()

    def finish(self):
        for wait in self.pending:
            wait()
        self.pending = []


class LineGather:
    def __init__(self, links, view):
        self.links, self.view = links, view
        chips = links.chips
        self.sends, self.recvs = links.take(3 * chips, 3 * chips)

    def start(self, source):
        k, chips = self.links, self.links.chips
        target = self.view(k.f)
        for side, way in enumerate((1, -1)):
            valid = (k.z + way >= 0) & (k.z + way < chips)
            k.send(
                valid, source, target, self.sends + side * chips, self.recvs + side * chips + 1, k.beside(way)
            )
        k.send(
            None, source, target, self.sends + 2 * chips + k.z, self.recvs + 2 * chips + k.z, k.sibling
        )

    def step(self, reach):
        k, chips = self.links, self.links.chips
        for side, way in enumerate((1, -1)):
            origin = k.z - way * reach
            here = (origin >= 0) & (origin < chips)
            block = self.view(origin * 2 + k.c)
            k.arrived(here, block, self.recvs + side * chips + reach)
            if reach + 1 < chips:
                onward = here & (k.z + way >= 0) & (k.z + way < chips)
                k.send(
                    onward,
                    block,
                    block,
                    self.sends + side * chips + reach,
                    self.recvs + side * chips + reach + 1,
                    k.beside(way),
                )
            k.send(
                here,
                block,
                block,
                self.sends + 2 * chips + origin,
                self.recvs + 2 * chips + origin,
                k.sibling,
            )

    def over(self, chip):
        k = self.links
        k.arrived(None, self.view(chip * 2 + 1 - k.c), self.recvs + 2 * k.chips + chip)

    def finish(self):
        k, chips = self.links, self.links.chips
        for chip in range(chips):
            k.arrived(None, self.view(chip * 2 + 1 - k.c), self.recvs + 2 * chips + chip)


def add_rows(target, *sources, step=16):
    rows = target.shape[0]

    @pl.loop(0, rows // step)
    def _(i):
        part = pl.ds(pl.multiple_of(i * step, step), step)
        total = sources[0][part].astype(F32)
        for source in sources[1:]:
            total = total + source[part].astype(F32)
        target[part] = total.astype(target.dtype)


class LineScatter:
    def __init__(self, links, mine, held, landed):
        self.links, self.mine, self.held, self.landed = links, mine, held, landed
        chips = links.chips
        self.sends, self.recvs = links.take(2 * chips, 3 * chips)
        self.gone = [lambda: None] * 2
        self.own = {}

    def give(self, chip, other, later=True):
        k = self.links
        return k.send(
            None, other, self.held(chip), self.sends + chip, self.recvs + chip, k.sibling, later=later
        )

    def start(self, parts):
        k = self.links
        for chip in range(k.chips):
            self.give(chip, parts(chip * 2 + 1 - k.c))
            self.own[chip] = k.move(parts(chip * 2 + k.c), self.mine(chip))

    def pair(self, chip, mine=None):
        k = self.links
        k.arrived(None, self.held(chip), self.recvs + chip)
        add_rows(self.held(chip), self.held(chip), self.mine(chip) if mine is None else mine)

    def pairs(self):
        for chip in range(self.links.chips):
            self.own[chip]()
            self.pair(chip)

    def place(self, side, chip, at):
        return self.landed(chip if side == 0 else jnp.where(chip == at, self.links.chips, chip))

    def onward(self, side, way, chip, before):
        k, chips = self.links, self.links.chips
        inner = before & (k.z > 0 if way > 0 else k.z < chips - 1)
        arrival = self.recvs + (1 + side) * chips + chip

        def add():
            k.arrived(None, self.place(side, chip, k.z), arrival)
            add_rows(self.held(chip), self.held(chip), self.place(side, chip, k.z))

        pl.when(inner)(add)
        return k.send(
            before,
            self.held(chip),
            self.place(side, chip, k.z + way),
            self.sends + chips + chip,
            arrival,
            k.beside(way),
        )

    def step(self, i):
        k, chips = self.links, self.links.chips
        for side, way in enumerate((1, -1)):
            chip = k.z + way * (chips - 1 - i)
            self.onward(side, way, chip, (chip >= 0) & (chip < chips))

    def toward(self, chip):
        k = self.links
        for side, way in enumerate((1, -1)):
            self.onward(side, way, chip, chip > k.z if way > 0 else chip < k.z)

    def last(self):
        k, chips = self.links, self.links.chips
        for side, inner in enumerate((k.z > 0, k.z < chips - 1)):

            def add():
                block = self.place(side, k.z, k.z)
                k.arrived(None, block, self.recvs + (1 + side) * chips + k.z)
                add_rows(self.held(k.z), self.held(k.z), block)

            pl.when(inner)(add)


class Exchange:
    def __init__(self, links):
        self.links = links
        self.sends, self.recvs = links.take(links.ranks, links.ranks)

    def start(self, source, target):
        k = self.links
        self.own = k.move(source(k.f), target(k.f))
        for i in range(1, k.ranks):
            other = lax.rem(k.f + i, k.ranks)
            k.send(
                None, source(other), target(k.f), self.sends + other, self.recvs + k.f, (k.d, other)
            )

    def finish(self, target, own=True):
        k = self.links
        if own:
            self.own()
        for i in range(1, k.ranks):
            other = lax.rem(k.f + i, k.ranks)
            k.arrived(None, target(other), self.recvs + other)

    def start_piece(self, rank, source, target):
        k = self.links
        k.send(
            k.f != rank, source, target(k.f), self.sends + rank, self.recvs + k.f, (k.d, rank)
        )
        here = lambda: pltpu.make_async_copy(source, target(k.f), k.sends.at[self.sends + rank])
        pl.when(k.f == rank)(lambda: here().start())
        k.pending.append(lambda: pl.when(k.f == rank)(lambda: here().wait()))


class GroupGather:
    def __init__(self, links, view, high):
        self.links, self.view, self.high = links, view, high
        count = links.groups - 1
        self.sends, self.recvs = links.take(count, count)

    def flip(self, stage):
        k = self.links
        low, up = 1 << stage, 1 << (k.bits - 1 - stage)
        size = low + self.high * (up - low)
        return (1 - 2 * lax.rem(lax.div(k.d, size), 2)) * size

    def places(self, stage):
        places = [self.links.d]
        for past in range(stage):
            places = places + [place + self.flip(past) for place in places]
        return places

    def start(self, stage, source=None):
        k = self.links
        for i, place in enumerate(self.places(stage)):
            at = (1 << stage) - 1 + i
            target = self.view(place)
            k.send(
                None,
                target if source is None else source,
                target,
                self.sends + at,
                self.recvs + at,
                (k.d + self.flip(stage), k.f),
            )

    def arrivals(self, stage):
        return [place + self.flip(stage) for place in self.places(stage)]

    def wait(self, stage):
        for i, place in enumerate(self.arrivals(stage)):
            self.links.arrived(None, self.view(place), self.recvs + (1 << stage) - 1 + i)


class GroupScatter:
    def __init__(self, links, view, landed, high):
        self.links, self.view, self.landed = links, view, landed
        bits = list(range(links.bits))
        self.order = bits[::-1] if high else bits
        count = links.groups - 1
        self.sends, self.recvs = links.take(count, count)

    def base(self, stage):
        return sum(self.links.groups >> (s + 1) for s in range(stage))

    def sources(self, stage, flip):
        k = self.links
        b = self.order[stage]
        value = 1 - k.bit(b) if flip else k.bit(b)
        if stage > 0:
            count = k.groups >> (stage + 1)
            return [self.landed(self.base(stage - 1) + value + 2 * i) for i in range(count)]
        places = [value * (1 << b)]
        for b in self.order[1:]:
            places = places + [place + (1 << b) for place in places]
        return [self.view(place) for place in places]

    def start(self, stage):
        k = self.links
        for i, source in enumerate(self.sources(stage, True)):
            at = self.base(stage) + i
            k.send(
                None,
                source,
                self.landed(at),
                self.sends + at,
                self.recvs + at,
                k.partner(self.order[stage]),
            )

    def wait(self, stage, target=None):
        k = self.links
        for i, source in enumerate(self.sources(stage, False)):
            at = self.base(stage) + i
            k.arrived(None, self.landed(at), self.recvs + at)
            add_rows(self.landed(at) if target is None else target, source, self.landed(at))
        return self.landed(self.base(stage))


def row_loop(rows, action, step=16, first=0):
    @pl.loop(0, rows // step)
    def _(i):
        action(pl.ds(pl.multiple_of(first + i * step, step), step))


def spaced(events, blocks):
    count = len(events)
    return [events[b * count // blocks : (b + 1) * count // blocks] for b in range(blocks)]


def head_places(ranks, rank_heads, split):
    places = {}
    for rank in range(ranks):
        for b in range(rank_heads):
            head = (rank % split * rank_heads + b) * (ranks // split) + rank // split
            places[head] = (rank, b)
    return [places[head] for head in range(HEADS)]


def attend_kernel(
    groups, ranks, rank_heads, slice_width, packed, traffic,
    lengths, tokens, w_query, w_key, w_value, gains, out_w, down_w, w_gate, w_up, cosine, sine,
    x_all, qkv, gain_rows, normed, queries, keys, values, attended, log_totals,
    attended_all, gate_up, out_all, down_all,
    gains_all, values_t, qkv_out, gate_up_out, sends, recvs,
):
    k = Links(groups, ranks, sends, recvs)
    places = head_places(ranks, rank_heads, max(1, HEAD_DIM // out_w.shape[0]))
    for rank in range(ranks):
        mine = [[h for h in range(HEADS) if places[h] == (rank, b)][0] for b in range(rank_heads)]
        for n, ref in enumerate((w_query, w_key, w_value)):
            for b in range(0, rank_heads, 2):
                halves = [
                    ref[:, head * HEAD_DIM : (head + 1) * HEAD_DIM].astype(F32)
                    for head in mine[b : b + 2]
                ]
                at = (n * rank_heads + b) * HEAD_DIM
                qkv_out[rank, :, at : at + 2 * HEAD_DIM] = jnp.concatenate(halves, 1).astype(BF16)
    length = lengths[0]
    cols, rows = queries.shape[1], tokens.shape[0]
    depth, half = gate_up_out.shape[1], ranks // 2
    pieces = depth // 16
    blocks = values_t.shape[0]
    split = max(1, HEAD_DIM // out_w.shape[0])
    down_half = down_w.shape[0] // 2

    def unit(group, rank):
        return (
            (lax.div(rank, split) * split + lax.div(group, rank_heads)) * rank_heads
            + lax.rem(group, rank_heads)
        ) * split + lax.rem(rank, split)

    def out_block(group, rank):
        return out_all.at[unit(group, rank)]

    def attended_block(i, rank):
        return attended_all.at[
            pl.ds(i * BLOCK, BLOCK), pl.ds(pl.multiple_of(rank * cols, cols), cols)
        ]

    x_line = LineGather(k, lambda rank: x_all.at[pl.ds(pl.multiple_of(rank * rows, 16), rows)])
    out_line = LineGather(k, lambda rank: out_block(k.d, rank))
    lines = [LineGather(k, lambda rank, i=i: attended_block(i, rank)) for i in range(blocks)]
    gains_ex, qkv_ex = Exchange(k), Exchange(k)
    exchanges = [Exchange(k) for _ in range(pieces)]
    downs = [
        GroupGather(k, lambda group, h=h: down_all.at[group, pl.ds(h * down_half, down_half)], h)
        for h in range(2)
    ]
    late = [
        GroupGather(k, lambda group, h=h, ref=ref: ref.at[group, pl.ds(h * half, half)], h)
        for ref in (qkv, gains_all)
        for h in range(2)
    ]
    out_gathers = [
        GroupGather(k, lambda group, r=r: out_block(group, k.c * half + r), k.c) for r in range(half)
    ]
    gathers = [
        [
            GroupGather(
                k,
                lambda group, h=h, q=q: gate_up.at[group, pl.ds(h * half, half), pl.ds(q * 16, 16)],
                h,
            )
            for h in range(2)
        ]
        for q in range(pieces)
    ]
    over_sends, over_recvs = k.take(half * groups, half * groups)

    def onward(several, stage):
        for gather in several:
            gather.wait(stage)
            if stage + 1 < k.bits:
                gather.start(stage + 1)

    def out_onward(stage):
        for r, gather in enumerate(out_gathers):
            gather.wait(stage)
            if stage + 1 < k.bits:
                gather.start(stage + 1)
            for group in gather.arrivals(stage):
                block = out_block(group, k.c * half + r)
                at = r * groups + group
                k.send(None, block, block, over_sends + at, over_recvs + at, k.sibling)

    units_from = w_gate if packed else gate_up_out

    def send_out(q):
        part = pl.ds(q * 16, 16)
        exchanges[q].start(
            lambda rank: units_from.at[rank, part], lambda rank: gate_up.at[k.d, rank, part]
        )

    def came_in(q):
        exchanges[q].finish(lambda rank: gate_up.at[k.d, rank, pl.ds(q * 16, 16)])
        for gather in gathers[q]:
            gather.start(0)
        if q + 2 < pieces:
            send_out(q + 2)

    gains_in = lambda rank: gains_all.at[k.d, rank]
    qkv_in = lambda rank: qkv.at[k.d, rank]
    k.barrier()
    gains_ex.start(lambda rank: gains, gains_in)
    qkv_ex.start(lambda rank: qkv_out.at[rank], qkv_in)
    for h, gather in enumerate(downs):
        gather.start(0, down_w.at[pl.ds(h * down_half, down_half)])
    own_down = k.move(down_w, down_all.at[k.d])
    if not packed:
        units = gate_up_out.shape[2] // 2
        share = units // groups
        for rank in range(ranks):
            for group in range(groups):
                at = (group * ranks + rank) * share
                for n, ref in enumerate((w_gate, w_up)):
                    start = n * units + group * share
                    gate_up_out[rank, :, start : start + share] = ref[:, at : at + share]
    out_line.start(out_w)
    gains_ex.finish(gains_in)
    qkv_ex.finish(qkv_in)
    x_line.start(tokens)
    own = [
        k.move(out_w, out_block(k.d, k.f)),
        k.move(tokens, x_all.at[pl.ds(pl.multiple_of(k.f * rows, 16), rows)]),
    ]
    for gather in late:
        gather.start(0)
    own_down()
    onward(downs, 0)
    for wait in own:
        wait()
    out_line.step(1)
    x_line.step(1)
    onward(late, 0)
    for reach in range(2, k.chips):
        out_line.step(reach)
    out_line.finish()
    for gather in out_gathers:
        gather.start(0)
    x_line.step(2)
    for q in range(min(2, pieces)):
        send_out(q)
    for reach in range(3, k.chips):
        x_line.step(reach)
    for stage in range(1, k.bits):
        onward(late, stage)
    out_onward(0)
    for stage in range(1, k.bits):
        onward(downs, stage)
    x_line.finish()
    traffic.put(0, 1)
    members = 128 // slice_width
    for at in range(groups * ranks // members):
        group, first = at * members // ranks, at * members % ranks
        tile = gains_all[group, first].astype(F32)
        for other in range(1, members):
            tile = tile + gains_all[group, first + other].astype(F32)
        gain_rows[:, at * 128 : (at + 1) * 128] = tile[:8]

    events = []
    for q in range(pieces):
        events.append(lambda q=q: came_in(q))
        if q > 0:
            events.append(lambda q=q: onward(gathers[q - 1], 0))
    events.append(lambda: onward(gathers[pieces - 1], 0))
    if k.bits == 2:
        events.append(lambda: out_onward(1))
    plan = spaced(events, 2 * blocks)
    own = []
    for i in range(blocks):
        query = project_block(
            i, x_all, gain_rows, qkv, cosine, sine, normed, queries, keys, values, values_t
        )
        for event in plan[2 * i]:
            event()
        attend_block(i, rank_heads, query, keys, values_t, length, attended, log_totals)
        mine = attended.at[pl.ds(i * BLOCK, BLOCK)]
        lines[i].start(mine)
        own.append(k.move(mine, attended_block(i, k.f)))
        for reach in range(1, k.chips):
            if i - reach >= 0:
                lines[i - reach].step(reach)
        for event in plan[2 * i + 1]:
            event()
    for i in range(blocks, blocks + k.chips - 1):
        for reach in range(1, k.chips):
            if 0 <= i - reach < blocks:
                lines[i - reach].step(reach)
    traffic.put()
    for stage in range(1, k.bits):
        if k.bits > 2:
            out_onward(stage)
        for several in gathers:
            onward(several, stage)
    for r in range(half):
        for i in range(1, groups):
            group = lax.rem(k.d + i, groups)
            block = out_block(group, (1 - k.c) * half + r)
            k.arrived(None, block, over_recvs + r * groups + group)
    for wait in own:
        wait()
    for line in lines:
        line.finish()
    k.finish()


def far_first(k, t):
    total = 0
    for z in range(k.chips):
        order = sorted(range(k.chips), key=lambda chip: -abs(chip - z))
        total = total + jnp.where(k.z == z, order[t], 0)
    return total


def feed_forward_kernel(
    groups, ranks, traffic, attended_all, x_all, out_all, gate_up_all, down_all, grad_out, gain_rows,
    grad_out_all, hidden, output, normed, mixed, grad_gate_up, parts,
    out_w, gate_up, down_w, attended_in, x_in, grad_in, hidden_b, normed_b, gates, mixed_b, grad_b, down_b, parts_b,
    held, landed, local, sends, recvs,
):
    k = Links(groups, ranks, sends, recvs)
    chips, pair = k.chips, hidden_b.shape[0]
    rows = pair // 2
    width, units = out_w.shape[0], down_w.shape[0]
    step = 1024
    chunk = 512
    line = LineGather(k, lambda rank: grad_out_all.at[rank])
    scatter = LineScatter(
        k, None, lambda chip: held.at[chip], lambda slot: landed.at[slot]
    )
    weights = [
        pltpu.make_async_copy(ref, buffer, local.at[n])
        for n, (ref, buffer) in enumerate(((out_all, out_w), (gate_up_all, gate_up), (down_all, down_w)))
    ]
    order = [far_first(k, t) for t in range(chips)]

    def span(t):
        return pl.ds(pl.multiple_of(order[t] * pair, 16), pair)

    def loads(t):
        return [
            pltpu.make_async_copy(ref.at[span(t)], buffer.at[t % 2], local.at[3 + 2 * n + t % 2])
            for n, (ref, buffer) in enumerate(((attended_all, attended_in), (x_all, x_in)))
        ]

    def fetches(t):
        return [
            pltpu.make_async_copy(
                grad_out_all.at[order[chips - 1 - t] * 2 + c],
                grad_in.at[t % 2, pl.ds(c * rows, rows)],
                local.at[7 + 2 * (t % 2) + c],
            )
            for c in range(2)
        ]

    def store(n, buffer, ref, t):
        return pltpu.make_async_copy(buffer, ref.at[span(t)], local.at[11 + n])

    for load in loads(0) + weights:
        load.start()
    k.barrier()
    line.start(grad_out)
    own = k.move(grad_out, grad_out_all.at[k.f])
    weights[0].wait()
    gone = []
    for t in range(chips):
        if t + 1 < chips:
            for load in loads(t + 1):
                load.start()
        for load in loads(t):
            load.wait()

        @pl.loop(0, width // step)
        def _(c):
            part = pl.ds(pl.multiple_of(c * step, step), step)
            hidden_b[:, part] = x_in[t % 2, :, part].astype(F32) + dot(
                attended_in[t % 2], out_w[:, part]
            )

        if t > 0:
            store(0, normed_b, normed, t - 1).wait()

        def normalise(part):
            total = hidden_b[part, :]
            normed_b[part, :] = (total * inverse_rms(total) * gain_rows[1:2, :]).astype(BF16)

        row_loop(pair, normalise)
        store(0, normed_b, normed, t).start()
        if t == 0:
            weights[1].wait()
        if t == chips - 1:

            @pl.loop(0, rows // 16)
            def _(i):
                source = pl.ds(pl.multiple_of(k.c * rows + i * 16, 16), 16)
                hidden[pl.ds(pl.multiple_of(i * 16, 16), 16), :] = hidden_b[source, :]

        if t > 0:
            store(1, mixed_b, mixed, t - 1).wait()
        if t > 2:
            line.step(t - 1)
        here = span(t)

        @pl.loop(0, units // chunk)
        def _(u):
            part = pl.ds(pl.multiple_of(u * chunk, chunk), chunk)
            far = pl.ds(pl.multiple_of(units + u * chunk, chunk), chunk)
            gate = dot(normed_b[...], gate_up[:, part])
            up = dot(normed_b[...], gate_up[:, far])
            gates[here, part] = gate
            gates[here, far] = up
            mixed_b[:, part] = (gate / (1.0 + jnp.exp(-gate)) * up).astype(BF16)

        store(1, mixed_b, mixed, t).start()
        if t == 0:
            weights[2].wait()
        elif t > 1:
            gone[t - 2]()

        @pl.loop(0, width // step)
        def _(c):
            part = pl.ds(pl.multiple_of(c * step, step), step)
            down_b[t % 2, :, part] = dot(mixed_b[...], down_w[:, part]).astype(BF16)

        def core_rows(t, core):
            return down_b.at[t % 2, pl.ds(pl.multiple_of(core * rows, 16), rows)]

        gone.append(scatter.give(order[t], core_rows(t, 1 - k.c), later=False))
        if t > 0:
            scatter.pair(order[t - 1], core_rows(t - 1, k.c))
        if t == 1:
            line.step(1)
        if t % 2 == 1:
            scatter.step(t // 2)
    store(0, normed_b, normed, chips - 1).wait()
    store(1, mixed_b, mixed, chips - 1).wait()
    for wait in gone[-2:]:
        wait()
    own()
    line.over(order[chips - 1])
    for fetch in fetches(0):
        fetch.start()
    for t in range(chips):
        if t == 1:
            line.step(chips - 1)
        if t + 1 < chips:
            line.over(order[chips - 2 - t])
            for fetch in fetches(t + 1):
                fetch.start()
        for fetch in fetches(t):
            fetch.wait()
        near = chips - 1 - t
        if t > 0:
            store(2, grad_b, grad_gate_up, near + 1).wait()
        here = span(near)

        @pl.loop(0, units // chunk)
        def _(u):
            part = pl.ds(pl.multiple_of(u * chunk, chunk), chunk)
            far = pl.ds(pl.multiple_of(units + u * chunk, chunk), chunk)
            gate, up = gates[here, part], gates[here, far]
            grad_mixed = cols_inner(grad_in[t % 2], down_w[part, :])
            sigmoid = 1.0 / (1.0 + jnp.exp(-gate))
            grad_b[:, part] = (
                grad_mixed * up * (sigmoid * (1.0 + gate * (1.0 - sigmoid)))
            ).astype(BF16)
            grad_b[:, far] = (grad_mixed * (gate * sigmoid)).astype(BF16)

        store(2, grad_b, grad_gate_up, near).start()
        if t > 0:
            store(3, parts_b, parts, near + 1).wait()
        if t == 0:
            scatter.pair(order[chips - 1], down_b.at[(chips - 1) % 2, pl.ds(pl.multiple_of(k.c * rows, 16), rows)])
        if (chips + t) % 2 == 1 and (chips + t) // 2 < chips - 1:
            scatter.step((chips + t) // 2)

        @pl.loop(0, width // step)
        def _(c):
            part = pl.ds(pl.multiple_of(c * step, step), step)
            parts_b[:, part] = cols_inner(grad_b[...], gate_up[part, :]).astype(BF16)

        store(3, parts_b, parts, near).start()
    scatter.last()

    def out_rows(part):
        output[part] = (hidden[part] + held[k.z, part].astype(F32)).astype(BF16)

    row_loop(rows, out_rows)
    store(2, grad_b, grad_gate_up, 0).wait()
    store(3, parts_b, parts, 0).wait()
    k.finish()


def middle_kernel(
    groups, ranks, subs, traffic, parts, hidden, grad_out, gain_rows, normed, grad_gate_up, mixed, grad_out_all,
    grad_all, grad_hidden, sums, gate_up_sum, grad_down,
    mine, held, landed, rounded, tile, grad_w, gate_up_landed, local, sends, recvs,
):
    k = Links(groups, ranks, sends, recvs)
    rows = hidden.shape[0] // subs
    depth = grad_w.shape[2]
    step = 1024
    scatters, gathers = [], []
    for sub in range(subs):
        piece = pl.ds(sub * rows, rows)
        scatters.append(
            LineScatter(
                k,
                lambda chip, piece=piece: mine.at[chip, piece],
                lambda chip, piece=piece: held.at[chip, piece],
                lambda slot, piece=piece: landed.at[slot, piece],
            )
        )
        gathers.append(LineGather(k, lambda rank, piece=piece: grad_all.at[rank, piece]))
    gate_up_sums = [
        GroupScatter(
            k,
            lambda group, n=n: grad_w.at[group, n],
            lambda i, n=n: gate_up_landed.at[n, i],
            n % 2 == 1,
        )
        for n in range(ranks)
    ]
    per_group = ranks * depth // BLOCK
    per_tile = BLOCK // depth
    tiles = [(q, g) for q in range(per_group) for g in range(groups)]

    downs = mixed.shape[1] // BLOCK

    def load(i):
        ref, at = mixed, i - len(tiles)
        if i < len(tiles):
            ref, at = normed, tiles[i][1] * per_group + tiles[i][0]
        return pltpu.make_async_copy(
            ref.at[:, pl.ds(at * BLOCK, BLOCK)], tile.at[i % 2], local.at[i % 2]
        )

    def work(i):
        if i + 1 < len(tiles) + downs:
            load(i + 1).start()
        load(i).wait()
        if i >= len(tiles):
            flipped = tile[i % 2].astype(F32).T.astype(BF16)
            at = (i - len(tiles)) * BLOCK

            @pl.loop(0, grad_down.shape[1] // step)
            def _(c):
                part = pl.ds(pl.multiple_of(c * step, step), step)
                grad_down[at : at + BLOCK, part] = dot(flipped, grad_out_all[:, part]).astype(BF16)

            return
        q, g = tiles[i]
        flipped = tile[i % 2].astype(F32).T.astype(BF16)

        @pl.loop(0, grad_gate_up.shape[1] // step)
        def _(c):
            part = pl.ds(pl.multiple_of(c * step, step), step)
            total = dot(flipped, grad_gate_up[:, part]).astype(BF16)
            for n in range(per_tile):
                grad_w[g, q * per_tile + n, :, part] = total[n * depth : (n + 1) * depth]

        if g == groups - 1:
            for n in range(per_tile):
                gate_up_sums[q * per_tile + n].start(0)

    load(0).start()
    k.barrier()
    for sub, scatter in enumerate(scatters):
        scatter.start(lambda rank, sub=sub: parts.at[rank, pl.ds(sub * rows, rows)])
    sums[...] = jnp.zeros_like(sums)

    def rows_of(part):
        total = hidden[part]
        scale = inverse_rms(total)
        scaled = total * scale
        grad = held[k.z, part].astype(F32)
        sums[...] += jnp.sum(grad * scaled, 0, keepdims=True)
        grad_total = grad_out[part].astype(F32) + norm_back(grad * gain_rows[1:2, :], scaled, scale)
        grad_hidden[part] = grad_total
        rounded[part] = grad_total.astype(BF16)

    own = []
    hops = k.chips - 1
    early = len(tiles) // 4
    plan = spaced(list(range(early, len(tiles))), hops - 1) + [[]]
    plan = plan + spaced(list(range(len(tiles), len(tiles) + downs)), subs * hops)
    traffic.ready(5)
    for place in range(early):
        work(place)
    for turn in range(subs + 1):
        if turn < subs:
            scatters[turn].pairs()
        for i in range(hops):
            if turn < subs:
                scatters[turn].step(i)
            if turn > 0:
                gathers[turn - 1].step(i + 1)
            for place in plan[turn * hops + i]:
                if place == len(tiles):
                    traffic.ready(7)
                work(place)
            if turn == 1 and i == 0:
                for sums_of in gate_up_sums[: ranks // 2]:
                    sums_of.wait(0)
                    sums_of.start(1)
        if turn < subs:
            scatters[turn].last()
            row_loop(rows, rows_of, first=turn * rows)
            piece = pl.ds(turn * rows, rows)
            gathers[turn].start(rounded.at[piece])
            own.append(k.move(rounded.at[piece], grad_all.at[k.f, piece]))
        if turn == 1:
            for sums_of in gate_up_sums[ranks // 2 :]:
                sums_of.wait(0)
                sums_of.start(1)
    for stage in range(1, k.bits):
        for n, sums_of in enumerate(gate_up_sums):
            if stage + 1 < k.bits:
                sums_of.wait(stage)
                sums_of.start(stage + 1)
            else:
                sums_of.wait(stage, gate_up_sum.at[n])
    for gather in gathers:
        gather.finish()
    for wait in own:
        wait()
    k.finish()


def attend_back_kernel(
    groups, ranks, rank_heads, slice_width, traffic,
    lengths, out_all, normed, grad_rows, queries, keys, values, attended, log_totals,
    cosine, sine, qkv, gate_up_sum, grad_down, tokens, grad_hidden, gain_rows, sums_two,
    gate_up_grad, down_grad, qkv_grad, out_grad, grad_tokens, gain_grads,
    out_w, grad_qkv, keys_t, grad_keys, grad_values, down_landed, held, landed, parts_b, tile,
    grad_qkv_w, qkv_landed, grad_out_w, out_landed, sums, tiles, tiles_landed, tiles_sum, group_tiles,
    local, sends, recvs,
):
    k = Links(groups, ranks, sends, recvs)
    length = lengths[0]
    cols, width = queries.shape[1], grad_rows.shape[1]
    rows = tokens.shape[0]
    pair = 2 * rows
    blocks = keys_t.shape[0]
    depth = qkv_grad.shape[1]
    step = 512

    def group_sums(ref, landing, count):
        size = ref.shape[1] // count
        return [
            GroupScatter(
                k,
                lambda group, n=n: ref.at[group, pl.ds(n * size, size)],
                lambda i, n=n: landing.at[n, i],
                n % 2 == 1,
            )
            for n in range(count)
        ], size

    down_sums, down_size = group_sums(grad_down, down_landed, down_landed.shape[0])
    out_sums, out_size = group_sums(grad_out_w, out_landed, out_landed.shape[0])
    qkv_sums = [
        GroupScatter(
            k,
            lambda group, n=n: grad_qkv_w.at[group, n],
            lambda i, n=n: qkv_landed.at[n, i],
            n % 2 == 1,
        )
        for n in range(ranks)
    ]
    scatter = LineScatter(
        k, None, lambda chip: held.at[chip], lambda slot: landed.at[slot]
    )
    gate_up_ex, exchange, tile_exchange = Exchange(k), Exchange(k), Exchange(k)
    tile_sends, tile_recvs = k.take(groups, groups)
    gate_up_in = lambda rank: gate_up_grad.at[rank]
    qkv_in = lambda rank: qkv_grad.at[rank]

    def onward(several, stage):
        for sums_of in several:
            sums_of.wait(stage)
            sums_of.start(stage + 1)

    per_group = ranks * depth // BLOCK
    per_tile = BLOCK // depth
    work = [(q, g) for q in range(per_group) for g in range(groups)]

    def load(i):
        q, g = work[i]
        return pltpu.make_async_copy(
            normed.at[:, pl.ds((g * per_group + q) * BLOCK, BLOCK)], tile.at[i % 2], local.at[i % 2]
        )

    def weight_tile(i):
        q, g = work[i]
        if i + 1 < len(work):
            load(i + 1).start()
        load(i).wait()
        flipped = tile[i % 2].astype(F32).T.astype(BF16)
        for c in range(3):
            part = slice(c * cols, (c + 1) * cols)
            total = dot(flipped, grad_qkv[:, part]).astype(BF16)
            for n in range(per_tile):
                grad_qkv_w[g, q * per_tile + n, :, part] = total[n * depth : (n + 1) * depth]
        if g == groups - 1:
            for n in range(per_tile):
                qkv_sums[q * per_tile + n].start(0)

    before = []

    def parts_of(t):
        chip = far_first(k, t)
        here = pl.ds(pl.multiple_of(chip * pair, 16), pair)
        if t > 1:
            before[t - 2]()
            before[t - 2] = lambda: None

        @pl.loop(0, width // step)
        def _(c):
            part = pl.ds(pl.multiple_of(c * step, step), step)
            parts_b[t % 2, :, part] = cols_inner(grad_qkv[here, :], qkv[part, :]).astype(BF16)

        def core_rows(core):
            return parts_b.at[t % 2, pl.ds(pl.multiple_of(core * rows, 16), rows)]

        before.append(scatter.give(chip, core_rows(1 - k.c), later=False))
        return chip, core_rows(k.c)

    load(0).start()
    fetch = k.move(out_all.at[pl.ds(pl.multiple_of(k.f * cols, cols), cols)], out_w)
    k.barrier()
    traffic.ready(13)
    for sums_of in down_sums:
        sums_of.start(0)
    gate_up_ex.start(lambda rank: gate_up_sum.at[rank], gate_up_in)
    grad_keys[...] = jnp.zeros_like(grad_keys)
    grad_values[...] = jnp.zeros_like(grad_values)

    traffic.ready(5)

    @pl.loop(0, blocks)
    def _(i):
        block = pl.ds(pl.multiple_of(i * BLOCK, BLOCK), BLOCK)
        keys_t[i] = keys[block, :].astype(F32).T.astype(BF16)

    fetch()
    traffic.ready()

    def back_rows(i):
        attend_back_rows(
            i, rank_heads, grad_rows, out_w, queries, keys, keys_t, values, attended, length, log_totals,
            cosine, sine, grad_keys, grad_values, grad_qkv,
        )

    pl.loop(0, blocks - 1)(back_rows)
    for stage in range(k.bits - 1):
        onward(down_sums, stage)
    back_rows(blocks - 1)
    pl.loop(0, blocks)(
        lambda i: finish_back_rows(i, cosine, sine, grad_keys, grad_values, grad_qkv)
    )
    shares = spaced(list(range(len(work))), 2) + [[]] * k.chips
    given = None
    for t in range(k.chips):
        now = parts_of(t)
        if given is not None:
            scatter.pair(*given)
        given = now
        for i in shares[t]:
            weight_tile(i)
        if t == 1:
            scatter.step(0)
    scatter.pair(*given)

    out_rows = grad_out_w.shape[1]
    split = groups * out_rows // cols
    out_base = lax.rem(k.f, split) * (cols // out_rows)
    if split > 1:
        grad_out_w[...] = jnp.zeros_like(grad_out_w)

    @pl.loop(0, width // BLOCK)
    def _(t):
        part = pl.ds(pl.multiple_of(t * BLOCK, BLOCK), BLOCK)
        total = rows_inner(attended[...], grad_rows[:, part]).astype(BF16)
        for n in range(cols // out_rows):
            grad_out_w[out_base + n, :, part] = total[n * out_rows : (n + 1) * out_rows]

    for sums_of in out_sums:
        sums_of.start(0)
    for stage in range(k.bits - 1):
        onward(qkv_sums, stage)
        if stage == 0:
            scatter.step(1)
    for n, sums_of in enumerate(qkv_sums):
        exchange.start_piece(n, sums_of.wait(k.bits - 1), qkv_in)
        if n == ranks // 2 - 1:
            for i in range(2, k.chips - 1):
                scatter.step(i)
    for stage in range(k.bits - 1):
        onward(out_sums, stage)
    scatter.last()
    sums[...] = jnp.zeros_like(sums)

    def rows_of(part):
        total = tokens[part].astype(F32)
        scale = inverse_rms(total)
        scaled = total * scale
        grad = held[k.z, part].astype(F32)
        sums[...] += jnp.sum(grad * scaled, 0, keepdims=True)
        grad_tokens[part] = (
            grad_hidden[part] + norm_back(grad * gain_rows[0:1, :], scaled, scale)
        ).astype(BF16)

    row_loop(rows, rows_of)
    tiles[...] = jnp.zeros_like(tiles)
    for rank in range(ranks):
        for group in range(groups):
            at = (group * ranks + rank) * slice_width // 128 * 128
            tiles[rank, group, 0:1] = sums[:, at : at + 128]
            tiles[rank, group, 1:2] = sums_two[:, at : at + 128]
    tile_in = lambda rank: tiles_landed.at[rank]
    tile_exchange.start(lambda rank: tiles.at[rank], tile_in)
    for n, sums_of in enumerate(out_sums):
        sums_of.wait(k.bits - 1, out_grad.at[pl.ds(n * out_size, out_size)])
    for n, sums_of in enumerate(down_sums):
        sums_of.wait(k.bits - 1, down_grad.at[pl.ds(n * down_size, down_size)])
    tile_exchange.finish(tile_in)
    total = tiles_landed[0]
    for rank in range(1, ranks):
        total = total + tiles_landed[rank]
    tiles_sum[...] = total
    for i in range(1, groups):
        other = lax.rem(k.d + i, groups)
        k.send(
            None,
            tiles_sum.at[other],
            group_tiles.at[k.d],
            tile_sends + other,
            tile_recvs + k.d,
            (other, k.f),
        )
    group_tiles[k.d] = tiles_sum[k.d]
    for i in range(1, groups):
        other = lax.rem(k.d + i, groups)
        k.arrived(None, group_tiles.at[other], tile_recvs + other)
    total = group_tiles[0]
    for group in range(1, groups):
        total = total + group_tiles[group]
    gain_grads[...] = total
    for wait in before:
        wait()
    gate_up_ex.finish(gate_up_in)
    exchange.finish(qkv_in, own=False)
    k.finish()


def finish_kernel(
    groups, places, gate_up_grad, qkv_grad, grad_w_gate, grad_w_up, grad_w_query, grad_w_key, grad_w_value
):
    ranks, cols, units = qkv_grad.shape[0], qkv_grad.shape[2] // 3, gate_up_grad.shape[2] // 2
    part = units // groups
    for rank in range(ranks):
        for group in range(groups):
            at = (group * ranks + rank) * part
            for n, out in enumerate((grad_w_gate, grad_w_up)):
                start = n * units + group * part
                out[:, at : at + part] = gate_up_grad[rank, :, start : start + part].astype(F32)
    for n, out in enumerate((grad_w_query, grad_w_key, grad_w_value)):
        for head in range(0, HEADS, 2):
            halves = []
            for rank, b in places[head : head + 2]:
                start = n * cols + b * HEAD_DIM
                halves.append(qkv_grad[rank, :, start : start + HEAD_DIM].astype(F32))
            at = head * HEAD_DIM
            out[:, at : at + 2 * HEAD_DIM] = jnp.concatenate(halves, 1)


VMEM = pl.BlockSpec(memory_space=pltpu.VMEM)
ANY = pl.BlockSpec(memory_space=pl.ANY)
SMEM = pl.BlockSpec(memory_space=pltpu.SMEM)
LOAD, STORE = "load", "store"


class Traffic:
    def __init__(self, ins, outs):
        self.ins, self.outs, self.begun = ins, outs, []
        for load in ins.values():
            load.start()

    def ready(self, *places):
        for place in places or tuple(self.ins):
            self.ins.pop(place).wait()

    def put(self, *places):
        for place in places or tuple(self.outs):
            store = self.outs.pop(place)
            store.start()
            self.begun.append(store)

    def close(self):
        self.ready()
        self.put()
        for store in self.begun:
            store.wait()


def call(kernel, identity, ins, outs, scratch, semaphores, args, local=0):
    loads = [i for i, place in enumerate(ins) if place == LOAD]
    stores = [i for i, (_, _, place) in enumerate(outs) if place == STORE]

    def body(*refs):
        inputs, results = list(refs[: len(ins)]), list(refs[len(ins) : len(ins) + len(outs)])
        rest = refs[len(ins) + len(outs) :]
        own = len(scratch) + (local > 0)
        buffers, moves = rest[own : own + len(loads) + len(stores)], rest[-3]
        coming, going = {}, {}
        for n, i in enumerate(loads):
            coming[i] = pltpu.make_async_copy(inputs[i], buffers[n], moves.at[n])
            inputs[i] = buffers[n]
        for n, i in enumerate(stores, len(loads)):
            going[i] = pltpu.make_async_copy(buffers[n], results[i], moves.at[n])
            results[i] = buffers[n]
        traffic = Traffic(coming, going)
        kernel(traffic, *inputs, *results, *rest[:own], *rest[-2:])
        traffic.close()

    return pl.pallas_call(
        body,
        out_shape=[jax.ShapeDtypeStruct(shape, kind) for shape, kind, _ in outs],
        in_specs=[ANY if place == LOAD else place for place in ins],
        out_specs=[ANY if place == STORE else place for _, _, place in outs],
        scratch_shapes=[pltpu.VMEM(shape, kind) for shape, kind in scratch]
        + [pltpu.SemaphoreType.DMA((local,))] * (local > 0)
        + [pltpu.VMEM(args[i].shape, args[i].dtype) for i in loads]
        + [pltpu.VMEM(outs[i][0], outs[i][1]) for i in stores]
        + [pltpu.SemaphoreType.DMA((max(1, len(loads) + len(stores)),))]
        + [pltpu.SemaphoreType.DMA((semaphores,))] * 2,
        compiler_params=pltpu.CompilerParams(
            collective_id=identity, has_side_effects=True, vmem_limit_bytes=61 * 1024 * 1024
        ),
    )(*args)


def build(groups, ranks):
    def body(
        tokens, cotangent, lengths, norm_attn, w_query, w_key, w_value, w_output, norm_mlp, w_gate, w_up, w_down
    ):
        rows, width = tokens.shape
        depth = w_query.shape[0]
        count = rows * ranks
        rank_heads = HEADS // ranks
        hidden_part = w_down.shape[0]
        out_rows = w_output.shape[0]
        split = max(1, HEAD_DIM // out_rows)
        rank = lax.axis_index("fsdp")

        def heads_out(weight):
            shaped = weight.reshape(depth, split, rank_heads, ranks // split, HEAD_DIM)
            return shaped.transpose(3, 1, 0, 2, 4).reshape(ranks, depth, rank_heads * HEAD_DIM)

        def heads_in(pieces):
            shaped = pieces.reshape(ranks // split, split, depth, rank_heads, HEAD_DIM)
            return shaped.transpose(2, 1, 3, 0, 4).reshape(depth, HEADS * HEAD_DIM)

        def units_out(weight):
            shaped = weight.reshape(depth, groups, ranks, hidden_part)
            return shaped.transpose(2, 0, 1, 3).reshape(ranks, depth, groups * hidden_part)

        def units_in(pieces):
            shaped = pieces.reshape(ranks, depth, groups, hidden_part)
            return shaped.transpose(1, 2, 0, 3).reshape(depth, groups * ranks * hidden_part)

        span = [[base * split + i for i in range(split)] for base in range(ranks // split)]

        head_cols = rank_heads * HEAD_DIM
        unit_cols = groups * hidden_part
        chips = ranks // 2
        slice_width = norm_attn.shape[0]
        packed = hidden_part % 128 != 0
        gate_up_shape = (ranks, depth, 2 * unit_cols)
        if packed:
            feeds = (jnp.concatenate([units_out(w) for w in (w_gate, w_up)], -1), w_up)
        else:
            feeds = (w_gate, w_up)
        place = (lax.axis_index("dp") * ranks + rank) * slice_width % 128
        gains = lax.dynamic_update_slice(
            jnp.zeros((16, 128), BF16), jnp.stack([norm_attn, norm_mlp]), (0, place)
        )
        cosine, sine = (jnp.asarray(table) for table in wide_tables(count))
        blocks = count // BLOCK
        heads_shape = ((count, head_cols), BF16, STORE)
        (
            x_all, qkv, gain_rows, normed_one, queries, keys, values, attended, log_totals,
            attended_all, gate_up, out_all, down_w,
        ) = call(
            functools.partial(attend_kernel, groups, ranks, rank_heads, slice_width, packed),
            5,
            [SMEM] + [VMEM] * 11,
            [
                ((count, width), BF16, STORE),
                ((groups, ranks, depth, 3 * head_cols), BF16, STORE),
                ((8, width), F32, VMEM),
                ((count, width), BF16, STORE),
            ]
            + [heads_shape] * 4
            + [
                ((blocks, rank_heads, BLOCK), F32, STORE),
                ((count, width), BF16, ANY),
                ((groups,) + gate_up_shape, BF16, ANY),
                ((groups * ranks, out_rows, width), BF16, ANY),
                ((groups,) + w_down.shape, BF16, ANY),
            ],
            [
                ((groups, ranks, 16, 128), BF16),
                ((blocks, head_cols, BLOCK), BF16),
                ((ranks, depth, 3 * head_cols), BF16),
                (gate_up_shape, BF16),
            ],
            448,
            (lengths, tokens, w_query, w_key, w_value, gains, w_output, w_down) + feeds + (cosine, sine),
        )
        qkv = qkv.reshape(width, -1)
        gate_up = gate_up.reshape(width, -1)
        out_all = out_all.reshape(width, width)
        down_w = down_w.reshape(-1, width)
        own_places = rank * rows + jnp.arange(rows, dtype=jnp.int32)
        grad_out = jnp.where(own_places[:, None] < lengths[0], cotangent, jnp.zeros((), BF16))
        pair = 2 * rows
        line_scratch = [
            ((chips, rows, width), BF16),
            ((chips, rows, width), BF16),
            ((chips + 1, rows, width), BF16),
        ]
        grad_out_all, hidden, output, normed_two, mixed, grad_gate_up, parts = call(
            functools.partial(feed_forward_kernel, groups, ranks),
            2,
            [ANY] * 5 + [VMEM] * 2,
            [
                ((ranks, rows, width), BF16, ANY),
                ((rows, width), F32, VMEM),
                ((rows, width), BF16, VMEM),
                ((count, width), BF16, ANY),
                ((count, unit_cols), BF16, ANY),
                ((count, 2 * unit_cols), BF16, ANY),
                ((count, width), BF16, ANY),
            ],
            [
                ((width, width), BF16),
                ((width, 2 * unit_cols), BF16),
                ((unit_cols, width), BF16),
                ((2, pair, width), BF16),
                ((2, pair, width), BF16),
                ((2, pair, width), BF16),
                ((pair, width), F32),
                ((pair, width), BF16),
                ((count, 2 * unit_cols), F32),
                ((pair, unit_cols), BF16),
                ((pair, 2 * unit_cols), BF16),
                ((2, pair, width), BF16),
                ((pair, width), BF16),
            ]
            + line_scratch[1:],
            128,
            (attended_all, x_all, out_all, gate_up, down_w, grad_out, gain_rows),
            local=15,
        )
        grad_hidden_all, grad_hidden, sums_two, gate_up_sum, grad_down = call(
            functools.partial(middle_kernel, groups, ranks, 2),
            3,
            [ANY] + [VMEM] * 3 + [ANY, LOAD, ANY, LOAD],
            [
                ((ranks, rows, width), BF16, ANY),
                ((rows, width), F32, VMEM),
                ((1, width), F32, VMEM),
                ((ranks, depth, 2 * unit_cols), BF16, VMEM),
                ((unit_cols, width), BF16, STORE),
            ],
            line_scratch
            + [
                ((rows, width), BF16),
                ((2, count, BLOCK), BF16),
                ((groups, ranks, depth, 2 * unit_cols), BF16),
                ((ranks, groups - 1, depth, 2 * unit_cols), BF16),
            ],
            160,
            (
                parts.reshape(ranks, rows, width),
                hidden,
                grad_out,
                gain_rows,
                normed_two,
                grad_gate_up,
                mixed,
                grad_out_all.reshape(count, width),
            ),
            local=2,
        )
        down_pieces, out_pieces = 4, 2
        out_place = out_rows * split
        tile = (8, 128)
        grad_gate_up_w, grad_w_down, grad_qkv_w, grad_w_output, grad_tokens, sums = call(
            functools.partial(attend_back_kernel, groups, ranks, rank_heads, slice_width),
            6,
            [SMEM, ANY, ANY] + [LOAD] * 9 + [ANY, LOAD] + [VMEM] * 4,
            [
                ((ranks, depth, 2 * unit_cols), BF16, ANY),
                ((hidden_part, width), F32, VMEM),
                ((ranks, depth, 3 * head_cols), BF16, ANY),
                ((out_place, width), F32, VMEM),
                ((rows, width), BF16, VMEM),
                (tile, F32, VMEM),
            ],
            [
                ((head_cols, width), BF16),
                ((count, 3 * head_cols), BF16),
                ((blocks, head_cols, BLOCK), BF16),
                ((count, head_cols), F32),
                ((count, head_cols), F32),
                ((down_pieces, groups - 1, hidden_part // down_pieces, width), BF16),
            ]
            + line_scratch[1:]
            + [
                ((2, pair, width), BF16),
                ((2, count, BLOCK), BF16),
                ((groups, ranks, depth, 3 * head_cols), BF16),
                ((ranks, groups - 1, depth, 3 * head_cols), BF16),
                ((groups, out_place, width), BF16),
                ((out_pieces, groups - 1, out_place // out_pieces, width), BF16),
                ((1, width), F32),
                ((ranks, groups) + tile, F32),
                ((ranks, groups) + tile, F32),
                ((groups,) + tile, F32),
                ((groups,) + tile, F32),
            ],
            192,
            (
                lengths,
                out_all,
                normed_one,
                grad_hidden_all.reshape(count, width),
                queries,
                keys,
                values,
                attended,
                log_totals,
                cosine,
                sine,
                qkv,
                gate_up_sum,
                grad_down.reshape(groups, hidden_part, width),
                tokens,
                grad_hidden,
                gain_rows,
                sums_two,
            ),
            local=2,
        )
        if split > 1:
            grad_w_output = lax.psum_scatter(
                grad_w_output, "fsdp", scatter_dimension=0, tiled=True, axis_index_groups=span
            )
        if hidden_part % 128 == 0:
            wide, narrow = (
                jax.ShapeDtypeStruct((depth, size), F32) for size in (w_gate.shape[1], width)
            )
            grad_w_gate, grad_w_up, grad_w_query, grad_w_key, grad_w_value = pl.pallas_call(
                functools.partial(finish_kernel, groups, head_places(ranks, rank_heads, split)),
                out_shape=[wide, wide, narrow, narrow, narrow],
                in_specs=[VMEM] * 2,
                out_specs=[VMEM] * 5,
                compiler_params=pltpu.CompilerParams(vmem_limit_bytes=32 * 1024 * 1024),
            )(grad_gate_up_w, grad_qkv_w)
        else:
            grad_w_gate = units_in(grad_gate_up_w[..., :unit_cols]).astype(F32)
            grad_w_up = units_in(grad_gate_up_w[..., unit_cols:]).astype(F32)
            grad_w_query, grad_w_key, grad_w_value = (
                heads_in(grad_qkv_w[..., i * head_cols : (i + 1) * head_cols]).astype(F32)
                for i in range(3)
            )
        place = (lax.axis_index("dp") * ranks + rank) * slice_width % 128
        sums = lax.dynamic_slice_in_dim(sums, place, slice_width, 1)
        return (
            output,
            grad_tokens,
            sums[0],
            grad_w_query,
            grad_w_key,
            grad_w_value,
            grad_w_output,
            sums[1],
            grad_w_gate,
            grad_w_up,
            grad_w_down,
        )

    return body


def solution(mesh):
    both = P(("dp", "fsdp"))
    rows = P(("dp", "fsdp"), None)
    return jax.shard_map(
        build(mesh.shape["dp"], mesh.shape["fsdp"]),
        mesh=mesh,
        in_specs=(rows, rows, P("dp"), both, rows, rows, rows, rows, both, rows, rows, rows),
        out_specs=(rows, rows, both, rows, rows, rows, rows, both, rows, rows, rows),
        check_vma=False,
    )
```
